128 devices in a mesh: grp: 4 (over z), seq: 32 (over x, y, core).
Axes of the slice: x: 4, y: 4, z: 4, core: 2. Of those that a mesh axis runs over, the one named last changes fastest.
Arguments:
- tokens: bfloat16 [65536, 1024], P(('grp', 'seq')), may hold values from -6 to 6
- fine_query: bfloat16 [1024, 1024], replicated, may hold values from -4 to 4, as said below
- fine_key: bfloat16 [1024, 1024], replicated, may hold values from -4 to 4, as said below
- fine_value: bfloat16 [1024, 1024], replicated, may hold values from -0.1875 to 0.1875
- fine_out: bfloat16 [1024, 1024], replicated, may hold values from -0.1875 to 0.1875
- short_weight: bfloat16 [8192, 1024], P('seq'), may hold values from -0.0625 to 0.0625
- coarse_query: bfloat16 [1024, 1024], replicated, may hold values from -4 to 4, as said below
- coarse_key: bfloat16 [1024, 1024], replicated, may hold values from -4 to 4, as said below
- coarse_value: bfloat16 [1024, 1024], replicated, may hold values from -0.1875 to 0.1875
- coarse_out: bfloat16 [1024, 1024], replicated, may hold values from -0.375 to 0.375
Outputs:
- upsampled: bfloat16 [65536, 1024], P(('grp', 'seq'))
The draws below stay inside these ranges and needn't reach their ends.
Inputs may be any that keep to these rules, and one draw needn't show every extreme that they name: `fine_query`: entries of order 1024 ** -0.5 or a few times that. `fine_key`: entries of order 1024 ** -0.5 or a few times that. `coarse_query`: entries of order 1024 ** -0.5 or a few times that. `coarse_key`: entries of order 1024 ** -0.5 or a few times that.
All inputs are finite; a program needn't handle non-finite values.
Results may differ from the reference program's by a relative error of at most 0.02.
Values may be sent and summed in bfloat16 or wider, within the bound.
No kernel may reach another device: no remote copies, remote signals or barrier semaphores. Data moves between devices by JAX's collectives and lax.ppermute only.
A program may use at most 256 MiB of HBM per device.

```python
import math
import jax
import jax.numpy as jnp
from jax import lax

HEADS = 16
HEAD_DIM = 64
D = 1024
SHORT = 8
WIN = 1024
TOK_DEV = 512
TOKENS = 65536


def fresh_part(key):
    return jax.random.truncated_normal(key, -6.0, 6.0, (D, D), jnp.float32) * (1.6 * D ** (-0.5))


def draw_fine_query(key, part):
    key = jax.random.fold_in(key, 11)
    return fresh_part(key).astype(jnp.bfloat16)


def draw_fine_key(key, part):
    key = jax.random.fold_in(key, 12)
    return fresh_part(key).astype(jnp.bfloat16)


def draw_coarse_query(key, part):
    key = jax.random.fold_in(key, 13)
    return fresh_part(key).astype(jnp.bfloat16)


def draw_coarse_key(key, part):
    key = jax.random.fold_in(key, 14)
    return fresh_part(key).astype(jnp.bfloat16)


def levels(rng, dims, split, low, largest):
    loudness = 1.0
    for position, parts in split:
        steps = jax.random.uniform(jax.random.fold_in(jax.random.fold_in(rng, 6), position), (parts,), jnp.float32, low / len(split), largest / len(split))
        loudness = loudness * jnp.repeat(jnp.exp(steps), dims[position] // parts).reshape((-1,) + (1,) * (len(dims) - 1 - position))
    return loudness


def scatter_about(own_key, shape, scale, limit, shards=(), kind=jnp.bfloat16):
    result = jax.random.normal(own_key, shape, jnp.float32) * scale
    if len(shards) > 0:
        result = levels(own_key, shape, shards, -0.22, 0.18) * result
    return jnp.clip(result, min=-limit, max=limit).astype(kind)


def setup_inputs(seed: int = 0) -> dict:
    splits = jax.random.split(jax.random.key(seed), 11)
    return {
        "tokens": scatter_about(splits[0], (TOKENS, D), 1.0, 6.0, ((0, 128),)),
        "fine_query": draw_fine_query(jax.random.fold_in(splits[10], 71), 0),
        "fine_key": draw_fine_key(jax.random.fold_in(splits[10], 71), 0),
        "fine_value": scatter_about(splits[3], (D, D), D ** -0.5, 0.1875),
        "fine_out": scatter_about(splits[4], (D, D), D ** -0.5, 0.1875),
        "short_weight": scatter_about(splits[5], (SHORT * D, D), (SHORT * D) ** -0.5, 0.0625, ((0, 32),)),
        "coarse_query": draw_coarse_query(jax.random.fold_in(splits[10], 71), 0),
        "coarse_key": draw_coarse_key(jax.random.fold_in(splits[10], 71), 0),
        "coarse_value": scatter_about(splits[8], (D, D), D ** -0.5, 0.1875),
        "coarse_out": scatter_about(splits[9], (D, D), (D // 4) ** -0.5, 0.375),
    }


def normed(rows):
    values = rows.astype(jnp.float32)
    scale = lax.rsqrt(lax.optimization_barrier(jnp.mean(values * values, axis=-1, keepdims=True)) + 1e-06)
    return (values * scale).astype(jnp.bfloat16)

def project(rows, weight):
    return jnp.dot(rows, weight, preferred_element_type=jnp.float32).astype(jnp.bfloat16)

def attend(query, keys, values, keep):
    count = query.shape[0]
    width = keys.shape[0]
    query_heads = query.astype(jnp.float32).reshape(count, HEADS, HEAD_DIM)
    key_heads = keys.astype(jnp.float32).reshape(width, HEADS, HEAD_DIM)
    value_heads = values.astype(jnp.float32).reshape(width, HEADS, HEAD_DIM)
    scores = jnp.einsum('qhd,khd->hqk', query_heads, key_heads) * (1.0 / math.sqrt(HEAD_DIM))
    scores = jnp.where(keep[None], scores, -1e+30)
    top = lax.optimization_barrier(jnp.max(scores, axis=-1, keepdims=True))
    weights = jnp.where(keep[None], jnp.exp(scores - top), 0.0)
    total = lax.optimization_barrier(jnp.sum(weights, axis=-1))
    rounded = lax.optimization_barrier(weights.astype(jnp.bfloat16))
    mixed = jnp.einsum('hqk,khd->hqd', rounded.astype(jnp.float32), value_heads)
    mixed = mixed / total[..., None]
    return jnp.transpose(mixed, (1, 0, 2)).reshape(count, HEADS * HEAD_DIM).astype(jnp.bfloat16)

def reference(tokens, fine_query, fine_key, fine_value, fine_out, short_weight, coarse_query, coarse_key, coarse_value, coarse_out):
    total_rows, width = tokens.shape
    fine_normed = normed(tokens)
    query = project(fine_normed, fine_query)
    keys = project(fine_normed, fine_key)
    values = project(fine_normed, fine_value)
    padded_keys = jnp.concatenate([jnp.zeros((WIN, width), jnp.bfloat16), keys], axis=0)
    padded_values = jnp.concatenate([jnp.zeros((WIN, width), jnp.bfloat16), values], axis=0)

    def fine_block(block):
        start = (block * TOK_DEV).astype(jnp.int32)
        query_rows = lax.dynamic_slice_in_dim(query, start, TOK_DEV, 0)
        key_rows = lax.dynamic_slice_in_dim(padded_keys, start, WIN + TOK_DEV, 0)
        value_rows = lax.dynamic_slice_in_dim(padded_values, start, WIN + TOK_DEV, 0)
        query_pos = start + jnp.arange(TOK_DEV, dtype=jnp.int32)
        key_pos = start - WIN + jnp.arange(WIN + TOK_DEV, dtype=jnp.int32)
        keep = (key_pos[None, :] <= query_pos[:, None]) & (key_pos[None, :] > query_pos[:, None] - WIN) & (key_pos[None, :] >= 0)
        return attend(query_rows, key_rows, value_rows, keep)
    fine_mixed = lax.map(fine_block, jnp.arange(total_rows // TOK_DEV, dtype=jnp.int32)).reshape(total_rows, width)
    hidden = (tokens.astype(jnp.float32) + jnp.dot(fine_mixed, fine_out, preferred_element_type=jnp.float32)).astype(jnp.bfloat16)
    delayed = jnp.concatenate([jnp.zeros((SHORT - 1, width), jnp.bfloat16), hidden[:total_rows - (SHORT - 1)]], axis=0)
    grouped = delayed.reshape(total_rows // SHORT, SHORT * width)
    shortened = jnp.dot(grouped, short_weight, preferred_element_type=jnp.float32).astype(jnp.bfloat16)
    coarse_normed = normed(shortened)
    coarse_q = project(coarse_normed, coarse_query)
    coarse_k = project(coarse_normed, coarse_key)
    coarse_v = project(coarse_normed, coarse_value)
    coarse_rows = total_rows // SHORT
    block_rows = math.gcd(512, coarse_rows)
    key_pos = jnp.arange(coarse_rows, dtype=jnp.int32)

    def coarse_block(block):
        start = (block * block_rows).astype(jnp.int32)
        query_rows = lax.dynamic_slice_in_dim(coarse_q, start, block_rows, 0)
        query_pos = start + jnp.arange(block_rows, dtype=jnp.int32)
        keep = key_pos[None, :] <= query_pos[:, None]
        return attend(query_rows, coarse_k, coarse_v, keep)
    coarse_mixed = lax.map(coarse_block, jnp.arange(coarse_rows // block_rows, dtype=jnp.int32)).reshape(coarse_rows, width)
    refined = shortened.astype(jnp.float32) + jnp.dot(coarse_mixed, coarse_out, preferred_element_type=jnp.float32)
    return (hidden.astype(jnp.float32) + jnp.repeat(refined, SHORT, axis=0)).astype(jnp.bfloat16)
```

```python
import functools
import math

import jax
import jax.numpy as jnp
from jax import lax
from jax.experimental import pallas as pl
from jax.experimental.pallas import tpu as pltpu
from jax.sharding import Mesh, PartitionSpec as P

HEAD_DIM = 64
HEADS = 16
SHORT = 8
WIN = 1024
SCALE = math.log2(math.e) / math.sqrt(HEAD_DIM)
ALL = ("z", "x", "y", "c")
QB = 128
PAIR = 2 * HEAD_DIM
NEG = -1e30


def from_behind(block, distance):
    devices = range(128)
    route = [(i - distance, i) for i in devices if i - distance in devices]
    return lax.ppermute(block, ALL, route)


def normed(rows):
    values = rows.astype(jnp.float32)
    scale = lax.rsqrt(jnp.mean(values * values, axis=-1, keepdims=True) + 1e-06)
    return (values * scale).astype(jnp.bfloat16)


def dot(a, b, contract):
    return lax.dot_general(a, b, (contract, ((), ())), preferred_element_type=jnp.float32)


def fine_kernel(place_ref, q_ref, k_ref, v_ref, out_ref, s_ref, p_ref):
    count = q_ref.shape[0]
    span = WIN + QB
    lane = lax.broadcasted_iota(jnp.int32, (QB, PAIR), 1)
    row = lax.broadcasted_iota(jnp.int32, (QB, 2 * QB), 0)
    col = lax.broadcasted_iota(jnp.int32, (QB, 2 * QB), 1) % QB
    last = row <= col
    ones = jnp.ones((16, span), jnp.bfloat16)

    def units(masked):
        for b in range(count // QB):
            q = q_ref[b * QB : (b + 1) * QB, :]
            zero = jnp.zeros_like(q)
            both = jnp.concatenate(
                [jnp.where(lane < HEAD_DIM, q, zero), jnp.where(lane < HEAD_DIM, zero, q)], axis=0
            )
            s = dot(k_ref[b * QB : b * QB + span, :], both, ((1,), (1,)))
            if masked:
                key = lax.broadcasted_iota(jnp.int32, s.shape, 0) + b * QB
                s = jnp.where(key >= WIN - place_ref[0] * count, s, NEG)
            s_ref[b] = s
            edge = jnp.where(last, s_ref[b, WIN:span, :], s_ref[b, 0:QB, :])
            top = jnp.maximum(
                jnp.max(edge, axis=0, keepdims=True),
                jnp.max(s_ref[b, QB:WIN, :], axis=0, keepdims=True),
            )
            edge = jnp.exp2(edge - top)
            p_ref[b, 0:QB, :] = jnp.where(last, 0.0, edge).astype(jnp.bfloat16)
            p_ref[b, WIN:span, :] = jnp.where(last, edge, 0.0).astype(jnp.bfloat16)
            p_ref[b, QB:WIN, :] = jnp.exp2(s_ref[b, QB:WIN, :] - top).astype(jnp.bfloat16)
            v = jnp.concatenate([v_ref[:, b * QB : b * QB + span], ones], axis=0)
            o = dot(v, p_ref[b], ((1,), (0,)))
            o = o[:PAIR] * (1.0 / o[PAIR : PAIR + 1])
            mixed = jnp.concatenate([o[:HEAD_DIM, :QB], o[HEAD_DIM:PAIR, QB:]], axis=0)
            out_ref[b * QB : (b + 1) * QB, :] = mixed.T.astype(jnp.bfloat16)

    @pl.when(place_ref[0] * count >= WIN)
    def _():
        units(False)

    @pl.when(place_ref[0] * count < WIN)
    def _():
        units(True)


def fine_attend(place, q, k, v):
    count, width = q.shape
    span = WIN + count
    blocks = count // QB
    return pl.pallas_call(
        fine_kernel,
        grid=(width // PAIR,),
        in_specs=[
            pl.BlockSpec(memory_space=pltpu.SMEM),
            pl.BlockSpec((count, PAIR), lambda i: (0, i)),
            pl.BlockSpec((span, PAIR), lambda i: (0, i)),
            pl.BlockSpec((PAIR, span), lambda i: (i, 0)),
        ],
        out_specs=pl.BlockSpec((count, PAIR), lambda i: (0, i)),
        out_shape=jax.ShapeDtypeStruct((count, width), jnp.bfloat16),
        scratch_shapes=[
            pltpu.VMEM((blocks, WIN + QB, 2 * QB), jnp.float32),
            pltpu.VMEM((blocks, WIN + QB, 2 * QB), jnp.bfloat16),
        ],
        compiler_params=pltpu.CompilerParams(vmem_limit_bytes=40 * 2**20),
        cost_estimate=pl.CostEstimate(flops=10 * 2**30, bytes_accessed=8 * 2**20, transcendentals=8 * 2**20),
    )(place.reshape(1), q, k, v)


def coarse_kernel(group_ref, q_ref, kv_ref, out_ref):
    parts, blocks, rows, _ = kv_ref.shape
    keys = parts * rows
    tile = 4 * rows
    tiles = q_ref.shape[0] // tile
    lane = lax.broadcasted_iota(jnp.int32, (1, tile), 1)
    row = lax.broadcasted_iota(jnp.int32, (keys, tile), 0)
    limit = (lane // rows) * keys + group_ref[0] * rows + lane % rows
    ones = jnp.ones((16, keys), jnp.bfloat16)
    queries = []
    for t in range(tiles):
        q = q_ref[t * tile : (t + 1) * tile, :]
        queries.append(jnp.concatenate([q, jnp.zeros_like(q)], axis=1))
    tops = [jnp.full((1, tile), NEG, jnp.float32)] * tiles
    accs = [jnp.zeros((16 + rows, tile), jnp.float32)] * tiles
    for g in range(blocks):
        kv = kv_ref[:, g].reshape(keys, 2 * HEAD_DIM)
        v = jnp.concatenate([ones, kv.T[HEAD_DIM:, :]], axis=0)
        for t in range(g // 4, tiles):
            s = dot(kv, queries[t], ((1,), (1,)))
            if t == g // 4:
                s = jnp.where(row <= limit - (g - 4 * t) * keys, s, NEG)
            top = jnp.maximum(tops[t], jnp.max(s, axis=0, keepdims=True))
            p = jnp.exp2(s - top).astype(jnp.bfloat16)
            accs[t] = accs[t] * jnp.exp2(tops[t] - top) + dot(v, p, ((1,), (0,)))
            tops[t] = top
    for t in range(tiles):
        o = accs[t][16:] * (1.0 / accs[t][0:1])
        out_ref[t * tile : (t + 1) * tile, :] = o.T.astype(jnp.bfloat16)


def coarse_attend(group, q, kv):
    return pl.pallas_call(
        coarse_kernel,
        in_specs=[
            pl.BlockSpec(memory_space=pltpu.SMEM),
            pl.BlockSpec(memory_space=pltpu.VMEM),
            pl.BlockSpec(memory_space=pltpu.VMEM),
        ],
        out_specs=pl.BlockSpec(memory_space=pltpu.VMEM),
        out_shape=jax.ShapeDtypeStruct(q.shape, jnp.bfloat16),
        compiler_params=pltpu.CompilerParams(vmem_limit_bytes=40 * 2**20),
        cost_estimate=pl.CostEstimate(flops=4 * 2**30, bytes_accessed=3 * 2**20, transcendentals=5 * 2**20),
    )(group.reshape(1), q, kv)


def body(
    tokens,
    fine_query,
    fine_key,
    fine_value,
    fine_out,
    short_weight,
    coarse_query,
    coarse_key,
    coarse_value,
    coarse_out,
):
    count, width = tokens.shape
    bf = jnp.bfloat16
    place = lax.axis_index(ALL).astype(jnp.int32)
    far = from_behind(tokens, 2)
    near = from_behind(tokens, 1)
    weight = lax.all_gather(short_weight, ("x", "c"), axis=0, tiled=True)

    window = jnp.concatenate([far, near, tokens], axis=0)
    fine_normed = normed(window)
    own = normed(tokens)
    query = (dot(own, fine_query, ((1,), (0,))) * SCALE).astype(bf)
    keys = dot(fine_normed, fine_key, ((1,), (0,))).astype(bf)
    values = dot(fine_value, fine_normed, ((0,), (1,))).astype(bf)
    fine_mixed = fine_attend(place, query, keys, values)
    hidden = (tokens.astype(jnp.float32) + dot(fine_mixed, fine_out, ((1,), (0,)))).astype(bf)
    tail = from_behind(hidden[count - (SHORT - 1) :], 1)
    delayed = jnp.concatenate([tail, hidden[: count - (SHORT - 1)]], axis=0)
    rows = count // SHORT
    grouped = delayed.reshape(rows, 4, 4, 2 * width // 4)
    grouped = jnp.transpose(grouped, (2, 0, 1, 3)).reshape(4, rows, 2 * width)
    grouped = lax.all_to_all(grouped, "y", 0, 0).reshape(4 * rows, 2 * width)
    partial = dot(grouped, weight, ((1,), (0,))).astype(bf).reshape(4, rows, width)
    partial = lax.all_to_all(partial, "y", 0, 0)
    shortened = jnp.sum(partial.astype(jnp.float32), axis=0).astype(bf)
    coarse_normed = normed(shortened)

    def heads(weights, scale=1.0):
        out = (dot(coarse_normed, weights, ((1,), (0,))) * scale).astype(bf)
        return out.reshape(rows, HEADS, HEAD_DIM)

    qkv = jnp.concatenate(
        [heads(coarse_query, SCALE), heads(coarse_key), heads(coarse_value)], axis=2
    )
    qkv = lax.all_to_all(jnp.transpose(qkv, (1, 0, 2)), ("z", "x"), 0, 0)
    q = qkv[:, :, :HEAD_DIM].reshape(HEADS * rows, HEAD_DIM)
    kv = lax.all_gather(qkv[:, :, HEAD_DIM:], ("y", "c"), axis=0)
    mixed = coarse_attend(lax.axis_index(("y", "c")).astype(jnp.int32), q, kv)
    mixed = lax.all_to_all(mixed.reshape(HEADS, rows, HEAD_DIM), ("z", "x"), 0, 0)
    coarse_mixed = jnp.transpose(mixed, (1, 0, 2)).reshape(rows, width)
    refined = shortened.astype(jnp.float32) + dot(coarse_mixed, coarse_out, ((1,), (0,)))
    return (hidden.astype(jnp.float32) + jnp.repeat(refined, SHORT, axis=0)).astype(bf)


def solution(mesh):
    fine = Mesh(mesh.devices.reshape(4, 4, 4, 2), ALL)
    return jax.shard_map(
        body,
        mesh=fine,
        in_specs=(P(ALL, None), P(), P(), P(), P(), P(("x", "y", "c"), None), P(), P(), P(), P()),
        out_specs=P(ALL, None),
        check_vma=False,
    )
```

```python
import functools
import math

import jax
import jax.numpy as jnp
from jax import lax
from jax.experimental import pallas as pl
from jax.experimental.pallas import tpu as pltpu
from jax.sharding import Mesh, PartitionSpec as P

HEAD_DIM = 64
HEADS = 16
SHORT = 8
WIN = 1024
SCALE = math.log2(math.e) / math.sqrt(HEAD_DIM)
ALL = ("z", "x", "y", "c")
QB = 128
PAIR = 2 * HEAD_DIM
NEG = -1e30


def from_behind(block, distance):
    devices = range(128)
    route = [(i - distance, i) for i in devices if i - distance in devices]
    return lax.ppermute(block, ALL, route)


def normed(rows):
    values = rows.astype(jnp.float32)
    scale = lax.rsqrt(jnp.mean(values * values, axis=-1, keepdims=True) + 1e-06)
    return (values * scale).astype(jnp.bfloat16)


def dot(a, b, contract):
    return lax.dot_general(a, b, (contract, ((), ())), preferred_element_type=jnp.float32)


def params():
    return pltpu.CompilerParams(vmem_limit_bytes=48 * 2**20)


def fine_kernel(place_ref, q_ref, kp_ref, ko_ref, vp_ref, vo_ref, out_ref, s_ref, p_ref):
    count = q_ref.shape[0]
    span = WIN + QB
    blocks = count // QB
    groups = QB // SHORT
    lane = lax.broadcasted_iota(jnp.int32, (QB, PAIR), 1)
    row = lax.broadcasted_iota(jnp.int32, (QB, 2 * QB), 0)
    col = lax.broadcasted_iota(jnp.int32, (QB, 2 * QB), 1) % QB
    last = row <= (col % groups) * SHORT + col // groups
    ones = jnp.ones((16, span), jnp.bfloat16)

    def scores(b, masked):
        q = q_ref[b * QB : (b + 1) * QB, :]
        zero = jnp.zeros_like(q)
        both = jnp.concatenate(
            [jnp.where(lane < HEAD_DIM, q, zero), jnp.where(lane < HEAD_DIM, zero, q)], axis=0
        )
        split = WIN - b * QB
        s = dot(kp_ref[b * QB :, :], both, ((1,), (1,)))
        if masked:
            key = lax.broadcasted_iota(jnp.int32, s.shape, 0) + b * QB
            s = jnp.where(key >= WIN - place_ref[0] * count, s, NEG)
        s_ref[b, :split, :] = s
        s_ref[b, split:, :] = dot(ko_ref[: (b + 1) * QB, :], both, ((1,), (1,)))

    def weights(b):
        edge = jnp.where(last, s_ref[b, WIN:span, :], s_ref[b, 0:QB, :])
        top = jnp.maximum(
            jnp.max(edge, axis=0, keepdims=True),
            jnp.max(s_ref[b, QB:WIN, :], axis=0, keepdims=True),
        )
        edge = jnp.exp2(edge - top).astype(jnp.bfloat16)
        zero = jnp.zeros_like(edge)
        p_ref[b, 0:QB, :] = jnp.where(last, zero, edge)
        p_ref[b, WIN:span, :] = jnp.where(last, edge, zero)
        p_ref[b, QB:WIN, :] = jnp.exp2(s_ref[b, QB:WIN, :] - top).astype(jnp.bfloat16)

    def mix(b):
        v = jnp.concatenate([vp_ref[:, b * QB :], vo_ref[:, : (b + 1) * QB]], axis=1)
        v = jnp.concatenate([v, ones], axis=0)
        o = dot(v, p_ref[b], ((1,), (0,)))
        o = o[:PAIR] * (1.0 / o[PAIR : PAIR + 1])
        mixed = jnp.concatenate([o[:HEAD_DIM, :QB], o[HEAD_DIM:PAIR, QB:]], axis=0)
        out_ref[b * QB : (b + 1) * QB, :] = mixed.T.astype(jnp.bfloat16)

    def units(masked):
        for b in range(blocks):
            scores(b, masked)
        for b in range(blocks):
            weights(b)
        for b in range(blocks):
            mix(b)

    @pl.when(place_ref[0] * count >= WIN)
    def _():
        units(False)

    @pl.when(place_ref[0] * count < WIN)
    def _():
        units(True)


def fine_attend(place, q, keys, values):
    count, width = q.shape
    blocks = count // QB
    return pl.pallas_call(
        fine_kernel,
        name="fine_attend",
        grid=(width // PAIR,),
        in_specs=[
            pl.BlockSpec(memory_space=pltpu.SMEM),
            pl.BlockSpec((count, PAIR), lambda i: (0, i)),
            pl.BlockSpec((WIN, PAIR), lambda i: (0, i)),
            pl.BlockSpec((count, PAIR), lambda i: (0, i)),
            pl.BlockSpec((PAIR, WIN), lambda i: (i, 0)),
            pl.BlockSpec((PAIR, count), lambda i: (i, 0)),
        ],
        out_specs=pl.BlockSpec((count, PAIR), lambda i: (0, i)),
        out_shape=jax.ShapeDtypeStruct((count, width), jnp.bfloat16),
        scratch_shapes=[
            pltpu.VMEM((blocks, WIN + QB, 2 * QB), jnp.float32),
            pltpu.VMEM((blocks, WIN + QB, 2 * QB), jnp.bfloat16),
        ],
        compiler_params=params(),
        cost_estimate=pl.CostEstimate(flops=10 * 2**30, bytes_accessed=8 * 2**20, transcendentals=8 * 2**20),
    )(place.reshape(1), q, *keys, *values)


def pack_kernel(hidden_ref, tail_ref, out_ref):
    blocks, places, groups, width = hidden_ref.shape
    rows = blocks * groups
    half = width // 2
    for j in range(SHORT):
        p = (j + 1) % SHORT
        part = hidden_ref[:, p].reshape(rows, width)
        if p > 0:
            wide = part.astype(jnp.float32)
            tail = tail_ref[p : p + 1, :].astype(jnp.float32)
            first = lax.broadcasted_iota(jnp.int32, wide.shape, 0) == 0
            wide = jnp.where(first, tail, pltpu.roll(wide, 1, 0))
            part = wide.astype(jnp.bfloat16)
        for f in range(2):
            out_ref[(j % 2) * 2 + f, j // 2] = part[:, f * half : (f + 1) * half]


def pack(hidden, tail):
    count, width = hidden.shape
    groups = QB // SHORT
    blocks = count // QB
    return pl.pallas_call(
        pack_kernel,
        name="pack",
        out_shape=jax.ShapeDtypeStruct((4, 4, count // SHORT, width // 2), jnp.bfloat16),
        compiler_params=params(),
    )(hidden.reshape(blocks, SHORT, groups, width), tail)


def shorten_kernel(grouped_ref, weight_ref, out_ref):
    owners, parts, rows, depth = grouped_ref.shape
    total = None
    for j in range(parts):
        part = grouped_ref[:, j].reshape(owners * rows, depth)
        term = dot(part, weight_ref[j], ((1,), (0,)))
        total = term if total is None else total + term
    out_ref[...] = total.reshape(owners, rows, -1).astype(jnp.bfloat16)


def shorten(grouped, weight):
    owners, parts, rows, depth = grouped.shape
    width = weight.shape[1]
    tile = width // 4
    return pl.pallas_call(
        shorten_kernel,
        name="shorten",
        grid=(4,),
        in_specs=[
            pl.BlockSpec(grouped.shape, lambda i: (0, 0, 0, 0)),
            pl.BlockSpec((parts, depth, tile), lambda i: (0, 0, i)),
        ],
        out_specs=pl.BlockSpec((owners, rows, tile), lambda i: (0, 0, i)),
        out_shape=jax.ShapeDtypeStruct((owners, rows, width), jnp.bfloat16),
        compiler_params=params(),
    )(grouped, weight.reshape(parts, depth, width))


def coarse_project_kernel(part_ref, q_ref, k_ref, v_ref, short_ref, qkv_ref, norm_ref):
    @pl.when(pl.program_id(0) == 0)
    def _():
        short = jnp.sum(part_ref[...].astype(jnp.float32), axis=0).astype(jnp.bfloat16)
        short_ref[...] = short
        norm_ref[...] = normed(short)

    rows = norm_ref[...]
    for i, (ref, scale) in enumerate(((q_ref, SCALE), (k_ref, None), (v_ref, None))):
        out = dot(rows, ref[...], ((1,), (0,)))
        if scale is not None:
            out = out * scale
        out = out.astype(jnp.bfloat16)
        for h in range(qkv_ref.shape[0]):
            qkv_ref[h, :, i * HEAD_DIM : (i + 1) * HEAD_DIM] = out[:, h * HEAD_DIM : (h + 1) * HEAD_DIM]


def coarse_project(partial, query, key, value):
    owners, rows, width = partial.shape
    tile = 4 * HEAD_DIM
    spec = pl.BlockSpec((width, tile), lambda i: (0, i))
    return pl.pallas_call(
        coarse_project_kernel,
        name="coarse_project",
        grid=(width // tile,),
        in_specs=[pl.BlockSpec(partial.shape, lambda i: (0, 0, 0)), spec, spec, spec],
        out_specs=[
            pl.BlockSpec((rows, width), lambda i: (0, 0)),
            pl.BlockSpec((4, rows, 3 * HEAD_DIM), lambda i: (i, 0, 0)),
        ],
        out_shape=[
            jax.ShapeDtypeStruct((rows, width), jnp.bfloat16),
            jax.ShapeDtypeStruct((HEADS, rows, 3 * HEAD_DIM), jnp.bfloat16),
        ],
        scratch_shapes=[pltpu.VMEM((rows, width), jnp.bfloat16)],
        compiler_params=params(),
    )(partial, query, key, value)


def finish_kernel(mixed_ref, out_weight_ref, short_ref, hidden_ref, out_ref):
    heads, rows, _ = mixed_ref.shape
    mixed = jnp.concatenate([mixed_ref[h] for h in range(heads)], axis=1)
    refined = short_ref[...].astype(jnp.float32) + dot(mixed, out_weight_ref[...], ((1,), (0,)))
    tile = refined.shape[1]
    spread = jnp.broadcast_to(refined[:, None, :], (rows, SHORT, tile)).reshape(rows * SHORT, tile)
    out_ref[...] = (hidden_ref[...].astype(jnp.float32) + spread).astype(jnp.bfloat16)


def finish(mixed, out_weight, short, hidden):
    count, width = hidden.shape
    heads, rows, _ = mixed.shape
    tile = width // 4
    return pl.pallas_call(
        finish_kernel,
        name="finish",
        grid=(4,),
        in_specs=[
            pl.BlockSpec(mixed.shape, lambda i: (0, 0, 0)),
            pl.BlockSpec((width, tile), lambda i: (0, i)),
            pl.BlockSpec((rows, tile), lambda i: (0, i)),
            pl.BlockSpec((count, tile), lambda i: (0, i)),
        ],
        out_specs=pl.BlockSpec((count, tile), lambda i: (0, i)),
        out_shape=jax.ShapeDtypeStruct((count, width), jnp.bfloat16),
        compiler_params=params(),
    )(mixed, out_weight, short, hidden)


def coarse_kernel(group_ref, q_ref, kv_ref, out_ref):
    parts, blocks, rows, _ = kv_ref.shape
    keys = parts * rows
    tile = 4 * rows
    tiles = q_ref.shape[0] // tile
    lane = lax.broadcasted_iota(jnp.int32, (1, tile), 1)
    row = lax.broadcasted_iota(jnp.int32, (keys, tile), 0)
    limit = (lane // rows) * keys + group_ref[0] * rows + lane % rows
    ones = jnp.ones((16, keys), jnp.bfloat16)
    queries = []
    for t in range(tiles):
        q = q_ref[t * tile : (t + 1) * tile, :]
        queries.append(jnp.concatenate([q, jnp.zeros_like(q)], axis=1))
    tops = [jnp.full((1, tile), NEG, jnp.float32)] * tiles
    accs = [jnp.zeros((16 + rows, tile), jnp.float32)] * tiles
    for g in range(blocks):
        kv = kv_ref[:, g].reshape(keys, 2 * HEAD_DIM)
        v = jnp.concatenate([ones, kv.T[HEAD_DIM:, :]], axis=0)
        live = range(g // 4, tiles)
        scores = [dot(kv, queries[t], ((1,), (1,))) for t in live]
        scores[0] = jnp.where(row <= limit - (g % 4) * keys, scores[0], NEG)
        news = [jnp.maximum(tops[t], jnp.max(s, axis=0, keepdims=True)) for t, s in zip(live, scores)]
        ps = [jnp.exp2(s - top).astype(jnp.bfloat16) for s, top in zip(scores, news)]
        for t, top, p in zip(live, news, ps):
            accs[t] = accs[t] * jnp.exp2(tops[t] - top) + dot(v, p, ((1,), (0,)))
            tops[t] = top
    for t in range(tiles):
        o = accs[t][16:] * (1.0 / accs[t][0:1])
        out_ref[t * tile : (t + 1) * tile, :] = o.T.astype(jnp.bfloat16)


def coarse_attend(group, q, kv):
    return pl.pallas_call(
        coarse_kernel,
        in_specs=[
            pl.BlockSpec(memory_space=pltpu.SMEM),
            pl.BlockSpec(memory_space=pltpu.VMEM),
            pl.BlockSpec(memory_space=pltpu.VMEM),
        ],
        out_specs=pl.BlockSpec(memory_space=pltpu.VMEM),
        out_shape=jax.ShapeDtypeStruct(q.shape, jnp.bfloat16),
        name="coarse_attend",
        compiler_params=params(),
        cost_estimate=pl.CostEstimate(flops=4 * 2**30, bytes_accessed=3 * 2**20, transcendentals=5 * 2**20),
    )(group.reshape(1), q, kv)


def body(
    tokens,
    fine_query,
    fine_key,
    fine_value,
    fine_out,
    short_weight,
    coarse_query,
    coarse_key,
    coarse_value,
    coarse_out,
):
    count, width = tokens.shape
    bf = jnp.bfloat16
    place = lax.axis_index(ALL).astype(jnp.int32)
    groups = QB // SHORT
    blocks = count // QB
    first_core = lax.axis_index("c") == 0
    far = from_behind(tokens, 2)
    mate = lax.ppermute(tokens, "c", [(0, 1)])
    weight = lax.all_gather(short_weight, ("x", "c"), axis=0, tiled=True)

    shuffled = tokens.reshape(blocks, groups, SHORT, width)
    shuffled = jnp.transpose(shuffled, (0, 2, 1, 3)).reshape(count, width)
    query = (dot(normed(shuffled), fine_query, ((1,), (0,))) * SCALE).astype(bf)
    own = normed(tokens)
    own_keys = dot(own, fine_key, ((1,), (0,))).astype(bf)
    own_values = dot(fine_value, own, ((0,), (1,))).astype(bf)
    far, own_keys, own_values, query = lax.optimization_barrier((far, own_keys, own_values, query))
    near = jnp.where(first_core, lax.ppermute(far, "c", [(1, 0)]), mate)
    before = normed(jnp.concatenate([far, near], axis=0))
    keys = dot(before, fine_key, ((1,), (0,))).astype(bf)
    values = dot(fine_value, before, ((0,), (1,))).astype(bf)
    fine_mixed = fine_attend(place, query, (keys, own_keys), (values, own_values))
    hidden = (shuffled.astype(jnp.float32) + dot(fine_mixed, fine_out, ((1,), (0,)))).astype(bf)
    tail = from_behind(hidden.reshape(blocks, SHORT, groups, width)[-1, :, -1], 1)
    rows = count // SHORT
    grouped = lax.all_to_all(pack(hidden, tail), "y", 0, 0)
    partial = lax.all_to_all(shorten(grouped, weight), "y", 0, 0)
    shortened, qkv = coarse_project(partial, coarse_query, coarse_key, coarse_value)
    natural = jnp.transpose(hidden.reshape(blocks, SHORT, groups, width), (0, 2, 1, 3)).reshape(count, width)
    qkv = lax.all_to_all(qkv, ("z", "x"), 0, 0)
    q = qkv[:, :, :HEAD_DIM].reshape(HEADS * rows, HEAD_DIM)
    kv = lax.all_gather(qkv[:, :, HEAD_DIM:], ("y", "c"), axis=0)
    mixed = coarse_attend(lax.axis_index(("y", "c")).astype(jnp.int32), q, kv)
    mixed = lax.all_to_all(mixed.reshape(HEADS, rows, HEAD_DIM), ("z", "x"), 0, 0)
    return finish(mixed, coarse_out, shortened, natural)


def solution(mesh):
    fine = Mesh(mesh.devices.reshape(4, 4, 4, 2), ALL)
    return jax.shard_map(
        body,
        mesh=fine,
        in_specs=(P(ALL, None), P(), P(), P(), P(), P(("x", "y", "c"), None), P(), P(), P(), P()),
        out_specs=P(ALL, None),
        check_vma=False,
    )
```

```python
import functools
import math

import jax
import jax.numpy as jnp
from jax import lax
from jax.experimental import pallas as pl
from jax.experimental.pallas import tpu as pltpu
from jax.sharding import Mesh, PartitionSpec as P

HEAD_DIM = 64
HEADS = 16
SHORT = 8
WIN = 1024
SCALE = math.log2(math.e) / math.sqrt(HEAD_DIM)
ALL = ("z", "x", "y", "c")
QB = 128
PAIR = 2 * HEAD_DIM
NEG = -1e30


def from_behind(block, distance):
    devices = range(128)
    route = [(i - distance, i) for i in devices if i - distance in devices]
    return lax.ppermute(block, ALL, route)


def normed(rows):
    values = rows.astype(jnp.float32)
    scale = lax.rsqrt(jnp.mean(values * values, axis=-1, keepdims=True) + 1e-06)
    return (values * scale).astype(jnp.bfloat16)


def dot(a, b, contract):
    return lax.dot_general(a, b, (contract, ((), ())), preferred_element_type=jnp.float32)


def params():
    return pltpu.CompilerParams(vmem_limit_bytes=48 * 2**20)


def fine_kernel(place_ref, q_ref, kf_ref, kn_ref, ko_ref, vf_ref, vn_ref, vo_ref, out_ref, s_ref, p_ref):
    count = q_ref.shape[0]
    span = WIN + QB
    blocks = count // QB
    groups = QB // SHORT
    lane = lax.broadcasted_iota(jnp.int32, (QB, PAIR), 1)
    row = lax.broadcasted_iota(jnp.int32, (QB, 2 * QB), 0)
    col = lax.broadcasted_iota(jnp.int32, (QB, 2 * QB), 1) % QB
    last = row <= (col % groups) * SHORT + col // groups
    ones = jnp.ones((16, span), jnp.bfloat16)

    def scores(b, masked):
        q = q_ref[b * QB : (b + 1) * QB, :]
        zero = jnp.zeros_like(q)
        both = jnp.concatenate(
            [jnp.where(lane < HEAD_DIM, q, zero), jnp.where(lane < HEAD_DIM, zero, q)], axis=0
        )
        start = 0
        for i, part in enumerate((kf_ref[b * QB :, :], kn_ref[...], ko_ref[: (b + 1) * QB, :])):
            s = dot(part, both, ((1,), (1,)))
            if masked and i < 2:
                s = jnp.where(place_ref[0] + i >= 2, s, NEG)
            s_ref[b, start : start + part.shape[0], :] = s
            start += part.shape[0]

    def weights(b):
        edge = jnp.where(last, s_ref[b, WIN:span, :], s_ref[b, 0:QB, :])
        top = jnp.maximum(
            jnp.max(edge, axis=0, keepdims=True),
            jnp.max(s_ref[b, QB:WIN, :], axis=0, keepdims=True),
        )
        edge = jnp.exp2(edge - top).astype(jnp.bfloat16)
        zero = jnp.zeros_like(edge)
        p_ref[b, 0:QB, :] = jnp.where(last, zero, edge)
        p_ref[b, WIN:span, :] = jnp.where(last, edge, zero)
        p_ref[b, QB:WIN, :] = jnp.exp2(s_ref[b, QB:WIN, :] - top).astype(jnp.bfloat16)

    def mix(b):
        v = jnp.concatenate([vf_ref[:, b * QB :], vn_ref[...], vo_ref[:, : (b + 1) * QB]], axis=1)
        v = jnp.concatenate([v, ones], axis=0)
        o = dot(v, p_ref[b], ((1,), (0,)))
        o = o[:PAIR] * (1.0 / o[PAIR : PAIR + 1])
        mixed = jnp.concatenate([o[:HEAD_DIM, :QB], o[HEAD_DIM:PAIR, QB:]], axis=0)
        out_ref[b * QB : (b + 1) * QB, :] = mixed.T.astype(jnp.bfloat16)

    def units(masked):
        for b in range(blocks):
            scores(b, masked)
        for b in range(blocks):
            weights(b)
        for b in range(blocks):
            mix(b)

    @pl.when(place_ref[0] * count >= WIN)
    def _():
        units(False)

    @pl.when(place_ref[0] * count < WIN)
    def _():
        units(True)


def fine_attend(place, q, keys, values):
    count, width = q.shape
    blocks = count // QB
    return pl.pallas_call(
        fine_kernel,
        name="fine_attend",
        grid=(width // PAIR,),
        in_specs=[
            pl.BlockSpec(memory_space=pltpu.SMEM),
            pl.BlockSpec((count, PAIR), lambda i: (0, i)),
        ]
        + [pl.BlockSpec((count, PAIR), lambda i: (0, i))] * 3
        + [pl.BlockSpec((PAIR, count), lambda i: (i, 0))] * 3,
        out_specs=pl.BlockSpec((count, PAIR), lambda i: (0, i)),
        out_shape=jax.ShapeDtypeStruct((count, width), jnp.bfloat16),
        scratch_shapes=[
            pltpu.VMEM((blocks, WIN + QB, 2 * QB), jnp.float32),
            pltpu.VMEM((blocks, WIN + QB, 2 * QB), jnp.bfloat16),
        ],
        compiler_params=params(),
        cost_estimate=pl.CostEstimate(flops=10 * 2**30, bytes_accessed=8 * 2**20, transcendentals=8 * 2**20),
    )(place.reshape(1), q, *keys, *values)


def pack_kernel(hidden_ref, tail_ref, out_ref):
    blocks, places, groups, width = hidden_ref.shape
    rows = blocks * groups
    half = width // 2
    for j in range(SHORT):
        p = (j + 1) % SHORT
        part = hidden_ref[:, p].reshape(rows, width)
        if p > 0:
            wide = part.astype(jnp.float32)
            tail = tail_ref[p : p + 1, :].astype(jnp.float32)
            first = lax.broadcasted_iota(jnp.int32, wide.shape, 0) == 0
            wide = jnp.where(first, tail, pltpu.roll(wide, 1, 0))
            part = wide.astype(jnp.bfloat16)
        for f in range(2):
            out_ref[(j % 2) * 2 + f, j // 2] = part[:, f * half : (f + 1) * half]


def pack(hidden, tail):
    count, width = hidden.shape
    groups = QB // SHORT
    blocks = count // QB
    return pl.pallas_call(
        pack_kernel,
        name="pack",
        out_shape=jax.ShapeDtypeStruct((4, 4, count // SHORT, width // 2), jnp.bfloat16),
        compiler_params=params(),
    )(hidden.reshape(blocks, SHORT, groups, width), tail)


def shorten_kernel(grouped_ref, weight_ref, out_ref):
    owners, parts, rows, depth = grouped_ref.shape
    total = None
    for j in range(parts):
        part = grouped_ref[:, j].reshape(owners * rows, depth)
        term = dot(part, weight_ref[j], ((1,), (0,)))
        total = term if total is None else total + term
    out_ref[...] = total.reshape(owners, rows, -1).astype(jnp.bfloat16)


def shorten(grouped, weight):
    owners, parts, rows, depth = grouped.shape
    width = weight.shape[1]
    tile = width // 4
    return pl.pallas_call(
        shorten_kernel,
        name="shorten",
        grid=(4,),
        in_specs=[
            pl.BlockSpec(grouped.shape, lambda i: (0, 0, 0, 0)),
            pl.BlockSpec((parts, depth, tile), lambda i: (0, 0, i)),
        ],
        out_specs=pl.BlockSpec((owners, rows, tile), lambda i: (0, 0, i)),
        out_shape=jax.ShapeDtypeStruct((owners, rows, width), jnp.bfloat16),
        compiler_params=params(),
    )(grouped, weight.reshape(parts, depth, width))


def coarse_project_kernel(part_ref, q_ref, k_ref, v_ref, short_ref, qkv_ref, norm_ref):
    @pl.when(pl.program_id(0) == 0)
    def _():
        short = jnp.sum(part_ref[...].astype(jnp.float32), axis=0).astype(jnp.bfloat16)
        short_ref[...] = short
        norm_ref[...] = normed(short)

    rows = norm_ref[...]
    for i, (ref, scale) in enumerate(((k_ref, None), (v_ref, None), (q_ref, SCALE))):
        out = dot(rows, ref[...], ((1,), (0,)))
        if scale is not None:
            out = out * scale
        out = out.astype(jnp.bfloat16)
        for h in range(qkv_ref.shape[0]):
            qkv_ref[h, :, i * HEAD_DIM : (i + 1) * HEAD_DIM] = out[:, h * HEAD_DIM : (h + 1) * HEAD_DIM]


def coarse_project(partial, query, key, value):
    owners, rows, width = partial.shape
    tile = 4 * HEAD_DIM
    spec = pl.BlockSpec((width, tile), lambda i: (0, i))
    return pl.pallas_call(
        coarse_project_kernel,
        name="coarse_project",
        grid=(width // tile,),
        in_specs=[pl.BlockSpec(partial.shape, lambda i: (0, 0, 0)), spec, spec, spec],
        out_specs=[
            pl.BlockSpec((rows, width), lambda i: (0, 0)),
            pl.BlockSpec((4, rows, 3 * HEAD_DIM), lambda i: (i, 0, 0)),
        ],
        out_shape=[
            jax.ShapeDtypeStruct((rows, width), jnp.bfloat16),
            jax.ShapeDtypeStruct((HEADS, rows, 3 * HEAD_DIM), jnp.bfloat16),
        ],
        scratch_shapes=[pltpu.VMEM((rows, width), jnp.bfloat16)],
        compiler_params=params(),
    )(partial, query, key, value)


def finish_kernel(mixed_ref, out_weight_ref, short_ref, hidden_ref, out_ref):
    heads, rows, _ = mixed_ref.shape
    mixed = jnp.concatenate([mixed_ref[h] for h in range(heads)], axis=1)
    refined = short_ref[...].astype(jnp.float32) + dot(mixed, out_weight_ref[...], ((1,), (0,)))
    tile = refined.shape[1]
    spread = jnp.broadcast_to(refined[:, None, :], (rows, SHORT, tile)).reshape(rows * SHORT, tile)
    out_ref[...] = (hidden_ref[...].astype(jnp.float32) + spread).astype(jnp.bfloat16)


def finish(mixed, out_weight, short, hidden):
    count, width = hidden.shape
    heads, rows, _ = mixed.shape
    tile = width // 4
    return pl.pallas_call(
        finish_kernel,
        name="finish",
        grid=(4,),
        in_specs=[
            pl.BlockSpec(mixed.shape, lambda i: (0, 0, 0)),
            pl.BlockSpec((width, tile), lambda i: (0, i)),
            pl.BlockSpec((rows, tile), lambda i: (0, i)),
            pl.BlockSpec((count, tile), lambda i: (0, i)),
        ],
        out_specs=pl.BlockSpec((count, tile), lambda i: (0, i)),
        out_shape=jax.ShapeDtypeStruct((count, width), jnp.bfloat16),
        compiler_params=params(),
    )(mixed, out_weight, short, hidden)


def coarse_kernel(group_ref, q_ref, kv_ref, out_ref):
    parts, blocks, rows, _ = kv_ref.shape
    keys = parts * rows
    tile = 4 * rows
    tiles = blocks // 4
    lane = lax.broadcasted_iota(jnp.int32, (1, tile), 1)
    row = lax.broadcasted_iota(jnp.int32, (keys, tile), 0)
    limit = (lane // rows) * keys + group_ref[0] * rows + lane % rows
    ones = jnp.ones((16, keys), jnp.bfloat16)
    queries = []
    for t in range(tiles):
        q = q_ref[4 * t : 4 * t + 4, :, 2 * HEAD_DIM :].reshape(tile, HEAD_DIM)
        queries.append(jnp.concatenate([q, jnp.zeros_like(q)], axis=1))
    tops = [jnp.full((1, tile), NEG, jnp.float32)] * tiles
    accs = [jnp.zeros((16 + rows, tile), jnp.float32)] * tiles
    for g in range(blocks):
        kv = kv_ref[:, g].reshape(keys, 2 * HEAD_DIM)
        v = jnp.concatenate([ones, kv.T[HEAD_DIM:, :]], axis=0)
        live = range(g // 4, tiles)
        scores = [dot(kv, queries[t], ((1,), (1,))) for t in live]
        scores[0] = jnp.where(row <= limit - (g % 4) * keys, scores[0], NEG)
        news = [jnp.maximum(tops[t], jnp.max(s, axis=0, keepdims=True)) for t, s in zip(live, scores)]
        ps = [jnp.exp2(s - top).astype(jnp.bfloat16) for s, top in zip(scores, news)]
        for t, top, p in zip(live, news, ps):
            accs[t] = accs[t] * jnp.exp2(tops[t] - top) + dot(v, p, ((1,), (0,)))
            tops[t] = top
    for t in range(tiles):
        o = accs[t][16:] * (1.0 / accs[t][0:1])
        out_ref[4 * t : 4 * t + 4] = o.T.astype(jnp.bfloat16).reshape(4, rows, HEAD_DIM)


def coarse_attend(group, q, kv):
    return pl.pallas_call(
        coarse_kernel,
        in_specs=[
            pl.BlockSpec(memory_space=pltpu.SMEM),
            pl.BlockSpec(memory_space=pltpu.VMEM),
            pl.BlockSpec(memory_space=pltpu.VMEM),
        ],
        out_specs=pl.BlockSpec(memory_space=pltpu.VMEM),
        out_shape=jax.ShapeDtypeStruct((*q.shape[:2], HEAD_DIM), jnp.bfloat16),
        name="coarse_attend",
        compiler_params=params(),
        cost_estimate=pl.CostEstimate(flops=4 * 2**30, bytes_accessed=3 * 2**20, transcendentals=5 * 2**20),
    )(group.reshape(1), q, kv)


def body(
    tokens,
    fine_query,
    fine_key,
    fine_value,
    fine_out,
    short_weight,
    coarse_query,
    coarse_key,
    coarse_value,
    coarse_out,
):
    count, width = tokens.shape
    bf = jnp.bfloat16
    place = lax.axis_index(ALL).astype(jnp.int32)
    groups = QB // SHORT
    blocks = count // QB
    first_core = lax.axis_index("c") == 0
    far = from_behind(tokens, 2)
    mate = lax.ppermute(tokens, "c", [(0, 1)])
    shuffled = tokens.reshape(blocks, groups, SHORT, width)
    shuffled = jnp.transpose(shuffled, (0, 2, 1, 3)).reshape(count, width)
    query = (dot(normed(shuffled), fine_query, ((1,), (0,))) * SCALE).astype(bf)

    def keys_values(rows):
        rows = normed(rows)
        keys = dot(rows, fine_key, ((1,), (0,))).astype(bf)
        return keys, dot(fine_value, rows, ((0,), (1,))).astype(bf)

    own = keys_values(tokens)
    far, own, query, short_weight = lax.optimization_barrier((far, own, query, short_weight))
    near = jnp.where(first_core, lax.ppermute(far, "c", [(1, 0)]), mate)
    weight = lax.all_gather(short_weight, ("x", "c"), axis=0, tiled=True)
    kinds = zip(keys_values(far), keys_values(near), own)
    fine_mixed = fine_attend(place, query, *kinds)
    hidden = (shuffled.astype(jnp.float32) + dot(fine_mixed, fine_out, ((1,), (0,)))).astype(bf)
    tail = from_behind(hidden.reshape(blocks, SHORT, groups, width)[-1, :, -1], 1)
    rows = count // SHORT
    grouped = lax.all_to_all(pack(hidden, tail), "y", 0, 0)
    partial = lax.all_to_all(shorten(grouped, weight), "y", 0, 0)
    shortened, qkv = coarse_project(partial, coarse_query, coarse_key, coarse_value)
    natural = jnp.transpose(hidden.reshape(blocks, SHORT, groups, width), (0, 2, 1, 3)).reshape(count, width)
    qkv = lax.all_to_all(qkv, ("z", "x"), 0, 0)
    kv = lax.all_gather(qkv[:, :, : 2 * HEAD_DIM], ("y", "c"), axis=0)
    mixed = coarse_attend(lax.axis_index(("y", "c")).astype(jnp.int32), qkv, kv)
    mixed = lax.all_to_all(mixed, ("z", "x"), 0, 0)
    return finish(mixed, coarse_out, shortened, natural)


def solution(mesh):
    fine = Mesh(mesh.devices.reshape(4, 4, 4, 2), ALL)
    return jax.shard_map(
        body,
        mesh=fine,
        in_specs=(P(ALL, None), P(), P(), P(), P(), P(("x", "y", "c"), None), P(), P(), P(), P()),
        out_specs=P(ALL, None),
        check_vma=False,
    )
```

```python
import functools
import math

import jax
import jax.numpy as jnp
from jax import lax
from jax.experimental import pallas as pl
from jax.experimental.pallas import tpu as pltpu
from jax.sharding import Mesh, PartitionSpec as P

HEAD_DIM = 64
HEADS = 16
SHORT = 8
WIN = 1024
SCALE = math.log2(math.e) / math.sqrt(HEAD_DIM)
ALL = ("z", "x", "y", "c")
QB = 128
PAIR = 2 * HEAD_DIM
NEG = -1e30


def from_behind(block, distance):
    devices = range(128)
    route = [(i - distance, i) for i in devices if i - distance in devices]
    return lax.ppermute(block, ALL, route)


def normed(rows):
    values = rows.astype(jnp.float32)
    scale = lax.rsqrt(jnp.mean(values * values, axis=-1, keepdims=True) + 1e-06)
    return (values * scale).astype(jnp.bfloat16)


def dot(a, b, contract):
    return lax.dot_general(a, b, (contract, ((), ())), preferred_element_type=jnp.float32)


def params():
    return pltpu.CompilerParams(vmem_limit_bytes=48 * 2**20)


def fine_kernel(place_ref, q_ref, kf_ref, kn_ref, ko_ref, vf_ref, vn_ref, vo_ref, out_ref, s_ref, p_ref):
    count = q_ref.shape[0]
    span = WIN + QB
    blocks = count // QB
    groups = QB // SHORT
    lane = lax.broadcasted_iota(jnp.int32, (QB, PAIR), 1)
    row = lax.broadcasted_iota(jnp.int32, (QB, 2 * QB), 0)
    col = lax.broadcasted_iota(jnp.int32, (QB, 2 * QB), 1) % QB
    last = row <= (col % groups) * SHORT + col // groups
    ones = jnp.ones((16, span), jnp.bfloat16)

    def scores(b, masked):
        q = q_ref[b * QB : (b + 1) * QB, :]
        zero = jnp.zeros_like(q)
        both = jnp.concatenate(
            [jnp.where(lane < HEAD_DIM, q, zero), jnp.where(lane < HEAD_DIM, zero, q)], axis=0
        )
        start = 0
        for i, part in enumerate((kf_ref[b * QB :, :], kn_ref[...], ko_ref[: (b + 1) * QB, :])):
            s = dot(part, both, ((1,), (1,)))
            if masked and i < 2:
                s = jnp.where(place_ref[0] + i >= 2, s, NEG)
            s_ref[b, start : start + part.shape[0], :] = s
            start += part.shape[0]

    def weights(b):
        edge = jnp.where(last, s_ref[b, WIN:span, :], s_ref[b, 0:QB, :])
        top = jnp.maximum(
            jnp.max(edge, axis=0, keepdims=True),
            jnp.max(s_ref[b, QB:WIN, :], axis=0, keepdims=True),
        )
        edge = jnp.exp2(edge - top).astype(jnp.bfloat16)
        zero = jnp.zeros_like(edge)
        p_ref[b, 0:QB, :] = jnp.where(last, zero, edge)
        p_ref[b, WIN:span, :] = jnp.where(last, edge, zero)
        p_ref[b, QB:WIN, :] = jnp.exp2(s_ref[b, QB:WIN, :] - top).astype(jnp.bfloat16)

    def mix(b):
        v = jnp.concatenate([vf_ref[:, b * QB :], vn_ref[...], vo_ref[:, : (b + 1) * QB]], axis=1)
        v = jnp.concatenate([v, ones], axis=0)
        o = dot(v, p_ref[b], ((1,), (0,)))
        o = o[:PAIR] * (1.0 / o[PAIR : PAIR + 1])
        mixed = jnp.concatenate([o[:HEAD_DIM, :QB], o[HEAD_DIM:PAIR, QB:]], axis=0)
        out_ref[b * QB : (b + 1) * QB, :] = mixed.T.astype(jnp.bfloat16)

    def units(masked):
        for b in range(blocks):
            scores(b, masked)
        for b in range(blocks):
            weights(b)
        for b in range(blocks):
            mix(b)

    @pl.when(place_ref[0] * count >= WIN)
    def _():
        units(False)

    @pl.when(place_ref[0] * count < WIN)
    def _():
        units(True)


def fine_attend(place, q, keys, values):
    count, width = q.shape
    blocks = count // QB
    return pl.pallas_call(
        fine_kernel,
        name="fine_attend",
        grid=(width // PAIR,),
        in_specs=[
            pl.BlockSpec(memory_space=pltpu.SMEM),
            pl.BlockSpec((count, PAIR), lambda i: (0, i)),
        ]
        + [pl.BlockSpec((count, PAIR), lambda i: (0, i))] * 3
        + [pl.BlockSpec((PAIR, count), lambda i: (i, 0))] * 3,
        out_specs=pl.BlockSpec((count, PAIR), lambda i: (0, i)),
        out_shape=jax.ShapeDtypeStruct((count, width), jnp.bfloat16),
        scratch_shapes=[
            pltpu.VMEM((blocks, WIN + QB, 2 * QB), jnp.float32),
            pltpu.VMEM((blocks, WIN + QB, 2 * QB), jnp.bfloat16),
        ],
        compiler_params=params(),
        cost_estimate=pl.CostEstimate(flops=10 * 2**30, bytes_accessed=8 * 2**20, transcendentals=8 * 2**20),
    )(place.reshape(1), q, *keys, *values)


def pack_kernel(hidden_ref, tail_ref, out_ref):
    blocks, places, groups, width = hidden_ref.shape
    rows = blocks * groups
    half = width // 2
    for j in range(SHORT):
        p = (j + 1) % SHORT
        part = hidden_ref[:, p].reshape(rows, width)
        if p > 0:
            wide = part.astype(jnp.float32)
            tail = tail_ref[p : p + 1, :].astype(jnp.float32)
            first = lax.broadcasted_iota(jnp.int32, wide.shape, 0) == 0
            wide = jnp.where(first, tail, pltpu.roll(wide, 1, 0))
            part = wide.astype(jnp.bfloat16)
        for f in range(2):
            out_ref[(j % 2) * 2 + f, j // 2] = part[:, f * half : (f + 1) * half]


def pack(hidden, tail):
    count, width = hidden.shape
    groups = QB // SHORT
    blocks = count // QB
    return pl.pallas_call(
        pack_kernel,
        name="pack",
        out_shape=jax.ShapeDtypeStruct((4, 4, count // SHORT, width // 2), jnp.bfloat16),
        compiler_params=params(),
    )(hidden.reshape(blocks, SHORT, groups, width), tail)


def shorten_kernel(grouped_ref, weight_ref, out_ref):
    owners, parts, rows, depth = grouped_ref.shape
    total = None
    for j in range(parts):
        part = grouped_ref[:, j].reshape(owners * rows, depth)
        term = dot(part, weight_ref[j], ((1,), (0,)))
        total = term if total is None else total + term
    out_ref[...] = total.reshape(owners, rows, -1).astype(jnp.bfloat16)


def shorten(grouped, weight):
    owners, parts, rows, depth = grouped.shape
    width = weight.shape[1]
    tile = width // 4
    return pl.pallas_call(
        shorten_kernel,
        name="shorten",
        grid=(4,),
        in_specs=[
            pl.BlockSpec(grouped.shape, lambda i: (0, 0, 0, 0)),
            pl.BlockSpec((parts, depth, tile), lambda i: (0, 0, i)),
        ],
        out_specs=pl.BlockSpec((owners, rows, tile), lambda i: (0, 0, i)),
        out_shape=jax.ShapeDtypeStruct((owners, rows, width), jnp.bfloat16),
        compiler_params=params(),
    )(grouped, weight.reshape(parts, depth, width))


def coarse_project_kernel(part_ref, q_ref, k_ref, v_ref, short_ref, qkv_ref, norm_ref):
    @pl.when(pl.program_id(0) == 0)
    def _():
        short = jnp.sum(part_ref[...].astype(jnp.float32), axis=0).astype(jnp.bfloat16)
        short_ref[...] = short
        norm_ref[...] = normed(short)

    rows = norm_ref[...]
    for i, (ref, scale) in enumerate(((k_ref, None), (v_ref, None), (q_ref, SCALE))):
        out = dot(rows, ref[...], ((1,), (0,)))
        if scale is not None:
            out = out * scale
        out = out.astype(jnp.bfloat16)
        for h in range(qkv_ref.shape[0]):
            qkv_ref[h, :, i * HEAD_DIM : (i + 1) * HEAD_DIM] = out[:, h * HEAD_DIM : (h + 1) * HEAD_DIM]


def coarse_project(partial, query, key, value):
    owners, rows, width = partial.shape
    tile = 4 * HEAD_DIM
    spec = pl.BlockSpec((width, tile), lambda i: (0, i))
    return pl.pallas_call(
        coarse_project_kernel,
        name="coarse_project",
        grid=(width // tile,),
        in_specs=[pl.BlockSpec(partial.shape, lambda i: (0, 0, 0)), spec, spec, spec],
        out_specs=[
            pl.BlockSpec((rows, width), lambda i: (0, 0)),
            pl.BlockSpec((4, rows, 3 * HEAD_DIM), lambda i: (i, 0, 0)),
        ],
        out_shape=[
            jax.ShapeDtypeStruct((rows, width), jnp.bfloat16),
            jax.ShapeDtypeStruct((HEADS, rows, 3 * HEAD_DIM), jnp.bfloat16),
        ],
        scratch_shapes=[pltpu.VMEM((rows, width), jnp.bfloat16)],
        compiler_params=params(),
    )(partial, query, key, value)


def finish_kernel(mixed_ref, out_weight_ref, short_ref, hidden_ref, out_ref):
    heads, rows, _ = mixed_ref.shape
    mixed = jnp.concatenate([mixed_ref[h] for h in range(heads)], axis=1)
    refined = short_ref[...].astype(jnp.float32) + dot(mixed, out_weight_ref[...], ((1,), (0,)))
    tile = refined.shape[1]
    spread = jnp.broadcast_to(refined[:, None, :], (rows, SHORT, tile)).reshape(rows * SHORT, tile)
    out_ref[...] = (hidden_ref[...].astype(jnp.float32) + spread).astype(jnp.bfloat16)


def finish(mixed, out_weight, short, hidden):
    count, width = hidden.shape
    heads, rows, _ = mixed.shape
    tile = width // 4
    return pl.pallas_call(
        finish_kernel,
        name="finish",
        grid=(4,),
        in_specs=[
            pl.BlockSpec(mixed.shape, lambda i: (0, 0, 0)),
            pl.BlockSpec((width, tile), lambda i: (0, i)),
            pl.BlockSpec((rows, tile), lambda i: (0, i)),
            pl.BlockSpec((count, tile), lambda i: (0, i)),
        ],
        out_specs=pl.BlockSpec((count, tile), lambda i: (0, i)),
        out_shape=jax.ShapeDtypeStruct((count, width), jnp.bfloat16),
        compiler_params=params(),
    )(mixed, out_weight, short, hidden)


def coarse_kernel(number, first, final, where_ref, q_ref, *refs):
    parts = refs[:number]
    old = None if first else refs[number : number + 2]
    outs = refs[number if first else number + 2 :]
    blocks, rows, _ = parts[0].shape
    tile = 4 * rows
    tiles = blocks // 4
    lane = lax.broadcasted_iota(jnp.int32, (1, tile), 1)
    row = lax.broadcasted_iota(jnp.int32, (tile, tile), 0)
    stride = 8 * rows
    place = (row // rows) * stride + row % rows
    limit = (lane // rows) * stride + where_ref[0] * rows + lane % rows
    ones = jnp.ones((16, number * tile), jnp.bfloat16)
    queries = []
    for t in range(tiles):
        q = q_ref[4 * t : 4 * t + 4, :, 2 * HEAD_DIM :].reshape(tile, HEAD_DIM)
        queries.append(jnp.concatenate([q, jnp.zeros_like(q)], axis=1))
    if first:
        tops = [jnp.full((1, tile), NEG, jnp.float32)] * tiles
        accs = [jnp.zeros((16 + HEAD_DIM, tile), jnp.float32)] * tiles
    else:
        tops = [old[0][t, 0:1, :] for t in range(tiles)]
        accs = [old[1][t] for t in range(tiles)]
    for g in range(tiles):
        kv = jnp.concatenate([part[4 * g : 4 * g + 4].reshape(tile, PAIR) for part in parts], axis=0)
        v = jnp.concatenate([ones, kv.T[HEAD_DIM:, :]], axis=0)
        live = range(g, tiles)
        scores = [dot(kv, queries[t], ((1,), (1,))) for t in live]
        keep = jnp.concatenate(
            [place <= limit - where_ref[1 + i] * rows for i in range(number)], axis=0
        )
        scores[0] = jnp.where(keep, scores[0], NEG)
        news = [jnp.maximum(tops[t], jnp.max(s, axis=0, keepdims=True)) for t, s in zip(live, scores)]
        ps = [jnp.exp2(s - top).astype(jnp.bfloat16) for s, top in zip(scores, news)]
        for t, top, p in zip(live, news, ps):
            accs[t] = accs[t] * jnp.exp2(tops[t] - top) + dot(v, p, ((1,), (0,)))
            tops[t] = top
    for t in range(tiles):
        if final:
            o = accs[t][16:] * (1.0 / accs[t][0:1])
            outs[0][4 * t : 4 * t + 4] = o.T.astype(jnp.bfloat16).reshape(4, rows, HEAD_DIM)
        else:
            outs[0][t] = jnp.broadcast_to(tops[t], (8, tile))
            outs[1][t] = accs[t]


def coarse_attend(places, q, parts, state, final):
    heads, rows, _ = q.shape
    tile = 4 * rows
    if final:
        out_shape = jax.ShapeDtypeStruct((heads, rows, HEAD_DIM), jnp.bfloat16)
    else:
        out_shape = [
            jax.ShapeDtypeStruct((heads // 4, 8, tile), jnp.float32),
            jax.ShapeDtypeStruct((heads // 4, 16 + HEAD_DIM, tile), jnp.float32),
        ]
    first = state is None
    arrays = [q, *parts] + ([] if first else list(state))
    share = len(parts) / 8
    return pl.pallas_call(
        functools.partial(coarse_kernel, len(parts), first, final),
        in_specs=[pl.BlockSpec(memory_space=pltpu.SMEM)]
        + [pl.BlockSpec(memory_space=pltpu.VMEM)] * len(arrays),
        out_shape=out_shape,
        name="coarse_attend",
        compiler_params=params(),
        cost_estimate=pl.CostEstimate(
            flops=int(share * 6 * 2**30), bytes_accessed=2 * 2**20, transcendentals=int(share * 5 * 2**20)
        ),
    )(jnp.stack(places).astype(jnp.int32), *arrays)


def body(
    tokens,
    fine_query,
    fine_key,
    fine_value,
    fine_out,
    short_weight,
    coarse_query,
    coarse_key,
    coarse_value,
    coarse_out,
):
    count, width = tokens.shape
    bf = jnp.bfloat16
    place = lax.axis_index(ALL).astype(jnp.int32)
    groups = QB // SHORT
    blocks = count // QB
    first_core = lax.axis_index("c") == 0
    far = from_behind(tokens, 2)
    mate = lax.ppermute(tokens, "c", [(0, 1)])
    shuffled = tokens.reshape(blocks, groups, SHORT, width)
    shuffled = jnp.transpose(shuffled, (0, 2, 1, 3)).reshape(count, width)
    query = (dot(normed(shuffled), fine_query, ((1,), (0,))) * SCALE).astype(bf)

    def keys_values(rows):
        rows = normed(rows)
        keys = dot(rows, fine_key, ((1,), (0,))).astype(bf)
        return keys, dot(fine_value, rows, ((0,), (1,))).astype(bf)

    own = keys_values(tokens)
    far, own, query, short_weight = lax.optimization_barrier((far, own, query, short_weight))
    near = jnp.where(first_core, lax.ppermute(far, "c", [(1, 0)]), mate)
    weight = lax.all_gather(short_weight, ("x", "c"), axis=0, tiled=True)
    kinds = zip(keys_values(far), keys_values(near), own)
    fine_mixed = fine_attend(place, query, *kinds)
    hidden = (shuffled.astype(jnp.float32) + dot(fine_mixed, fine_out, ((1,), (0,)))).astype(bf)
    tail = from_behind(hidden.reshape(blocks, SHORT, groups, width)[-1, :, -1], 1)
    rows = count // SHORT
    grouped = lax.all_to_all(pack(hidden, tail), "y", 0, 0)
    partial = lax.all_to_all(shorten(grouped, weight), "y", 0, 0)
    shortened, qkv = coarse_project(partial, coarse_query, coarse_key, coarse_value)
    natural = jnp.transpose(hidden.reshape(blocks, SHORT, groups, width), (0, 2, 1, 3)).reshape(count, width)
    qkv = lax.all_to_all(qkv, ("z", "x"), 0, 0)
    kv = qkv[:, :, : 2 * HEAD_DIM]
    y, c = lax.axis_index("y"), lax.axis_index("c")
    mine = y * 2 + c

    def around(block, distance):
        return lax.ppermute(block, "y", [(i, (i + distance) % 4) for i in range(4)])

    def across(block):
        return lax.ppermute(block, "c", [(0, 1), (1, 0)])

    def spot(distance, other=0):
        return ((y + distance) % 4) * 2 + (1 - c if other else c)

    mate_kv = across(kv)
    below, above, beyond = around(kv, 1), around(kv, 3), around(kv, 2)
    state = coarse_attend((mine, mine, spot(0, 1)), qkv, (kv, mate_kv), None, False)
    others = (below, above, beyond)
    state, *others = lax.optimization_barrier((state, *others))
    swapped = [across(block) for block in others]
    state = coarse_attend((mine, spot(3), spot(1), spot(2)), qkv, others, state, False)
    state, *swapped = lax.optimization_barrier((state, *swapped))
    mixed = coarse_attend((mine, spot(3, 1), spot(1, 1), spot(2, 1)), qkv, swapped, state, True)
    mixed = lax.all_to_all(mixed, ("z", "x"), 0, 0)
    return finish(mixed, coarse_out, shortened, natural)


def solution(mesh):
    fine = Mesh(mesh.devices.reshape(4, 4, 4, 2), ALL)
    return jax.shard_map(
        body,
        mesh=fine,
        in_specs=(P(ALL, None), P(), P(), P(), P(), P(("x", "y", "c"), None), P(), P(), P(), P()),
        out_specs=P(ALL, None),
        check_vma=False,
    )
```

```python
import functools
import math

import jax
import jax.numpy as jnp
from jax import lax
from jax.experimental import pallas as pl
from jax.experimental.pallas import tpu as pltpu
from jax.sharding import Mesh, PartitionSpec as P

HEAD_DIM = 64
HEADS = 16
SHORT = 8
WIN = 1024
SCALE = math.log2(math.e) / math.sqrt(HEAD_DIM)
ALL = ("z", "x", "y", "c")
QB = 128
PAIR = 2 * HEAD_DIM
NEG = -1e30


def from_behind(block, distance):
    devices = range(128)
    route = [(i - distance, i) for i in devices if i - distance in devices]
    return lax.ppermute(block, ALL, route)


def normed(rows):
    values = rows.astype(jnp.float32)
    scale = lax.rsqrt(jnp.mean(values * values, axis=-1, keepdims=True) + 1e-06)
    return (values * scale).astype(jnp.bfloat16)


def dot(a, b, contract):
    return lax.dot_general(a, b, (contract, ((), ())), preferred_element_type=jnp.float32)


def params(mib=48):
    return pltpu.CompilerParams(vmem_limit_bytes=mib * 2**20)


def spots(index):
    groups = QB // SHORT
    return (index % groups) * SHORT + index // groups


def two_heads(q_ref, b):
    lane = lax.broadcasted_iota(jnp.int32, (QB, PAIR), 1)
    q = q_ref[b * QB : (b + 1) * QB, :]
    zero = jnp.zeros_like(q)
    return jnp.concatenate(
        [jnp.where(lane < HEAD_DIM, q, zero), jnp.where(lane < HEAD_DIM, zero, q)], axis=0
    )


def with_sums(v):
    return jnp.concatenate([v, jnp.ones((16, v.shape[1]), jnp.bfloat16)], axis=0)


def fine_own_kernel(q_ref, k_ref, v_ref, top_ref, acc_ref, s_ref, p_ref):
    blocks = q_ref.shape[0] // QB
    row = lax.broadcasted_iota(jnp.int32, (QB, 2 * QB), 0)
    col = lax.broadcasted_iota(jnp.int32, (QB, 2 * QB), 1) % QB
    keep = spots(row) <= spots(col)
    for b in range(blocks):
        both = two_heads(q_ref, b)
        if b > 0:
            s_ref[b, : b * QB, :] = dot(k_ref[: b * QB, :], both, ((1,), (1,)))
        s = dot(k_ref[b * QB : (b + 1) * QB, :], both, ((1,), (1,)))
        s_ref[b, b * QB : (b + 1) * QB, :] = jnp.where(keep, s, NEG)
    for b in range(blocks):
        end = (b + 1) * QB
        top = jnp.max(s_ref[b, :end, :], axis=0, keepdims=True)
        p_ref[b, :end, :] = jnp.exp2(s_ref[b, :end, :] - top).astype(jnp.bfloat16)
        top_ref[0, b] = jnp.broadcast_to(top, (8, 2 * QB))
    for b in range(blocks):
        end = (b + 1) * QB
        o = dot(with_sums(v_ref[:, :end]), p_ref[b, :end, :], ((1,), (0,)))
        acc_ref[0, b, :16, :] = o[PAIR:]
        acc_ref[0, b, 16:, :QB] = o[:HEAD_DIM, :QB]
        acc_ref[0, b, 16:, QB:] = o[HEAD_DIM:PAIR, QB:]


def fine_before_kernel(
    where_ref, q_ref, kf_ref, kn_ref, vf_ref, vn_ref, top_ref, acc_ref, out_ref, k_ref, v_ref, s_ref, p_ref
):
    half = kf_ref.shape[0]
    blocks = q_ref.shape[0] // QB
    core = where_ref[0]
    row = lax.broadcasted_iota(jnp.int32, (QB, 2 * QB), 0)
    col = lax.broadcasted_iota(jnp.int32, (QB, 2 * QB), 1) % QB
    keep = row > spots(col)

    def store(b, total, o):
        o = o * (1.0 / total)
        mixed = jnp.concatenate([o[:, :QB], o[:, QB:]], axis=0)
        at = b * QB // half
        out_ref[(at + core) % 2, b * QB - at * half : (b + 1) * QB - at * half, :] = mixed.T.astype(jnp.bfloat16)

    @pl.when(where_ref[1] == 0)
    def _():
        for b in range(blocks):
            store(b, acc_ref[0, b, 0:1, :], acc_ref[0, b, 16:, :])

    @pl.when(where_ref[1] > 0)
    def _():
        mine = pl.ds(pl.multiple_of(core * half, half), half)
        other = pl.ds(pl.multiple_of((1 - core) * half, half), half)
        k_ref[mine, :] = kf_ref[...]
        k_ref[other, :] = kn_ref[...]
        v_ref[:, mine] = vf_ref[...]
        v_ref[:, other] = vn_ref[...]
        for b in range(blocks):
            both = two_heads(q_ref, b)
            s = dot(k_ref[b * QB : (b + 1) * QB, :], both, ((1,), (1,)))
            s_ref[b, b * QB : (b + 1) * QB, :] = jnp.where(keep, s, NEG)
            if b < blocks - 1:
                s_ref[b, (b + 1) * QB :, :] = dot(k_ref[(b + 1) * QB :, :], both, ((1,), (1,)))
        fades = []
        for b in range(blocks):
            old = top_ref[0, b, 0:1, :]
            top = jnp.maximum(old, jnp.max(s_ref[b, b * QB :, :], axis=0, keepdims=True))
            p_ref[b, b * QB :, :] = jnp.exp2(s_ref[b, b * QB :, :] - top).astype(jnp.bfloat16)
            fades.append(jnp.exp2(old - top))
        for b in range(blocks):
            o = dot(with_sums(v_ref[:, b * QB :]), p_ref[b, b * QB :, :], ((1,), (0,)))
            acc = acc_ref[0, b] * fades[b]
            new = jnp.concatenate([o[:HEAD_DIM, :QB], o[HEAD_DIM:PAIR, QB:]], axis=1)
            store(b, acc[0:1] + o[PAIR : PAIR + 1], acc[16:] + new)


def fine_own(q, k, v):
    count, width = q.shape
    blocks = count // QB
    pairs = width // PAIR
    return pl.pallas_call(
        fine_own_kernel,
        name="fine_own",
        grid=(pairs,),
        in_specs=[
            pl.BlockSpec((count, PAIR), lambda i: (0, i)),
            pl.BlockSpec((count, PAIR), lambda i: (0, i)),
            pl.BlockSpec((PAIR, count), lambda i: (i, 0)),
        ],
        out_specs=[
            pl.BlockSpec((1, blocks, 8, 2 * QB), lambda i: (i, 0, 0, 0)),
            pl.BlockSpec((1, blocks, 16 + HEAD_DIM, 2 * QB), lambda i: (i, 0, 0, 0)),
        ],
        out_shape=[
            jax.ShapeDtypeStruct((pairs, blocks, 8, 2 * QB), jnp.float32),
            jax.ShapeDtypeStruct((pairs, blocks, 16 + HEAD_DIM, 2 * QB), jnp.float32),
        ],
        scratch_shapes=[
            pltpu.VMEM((blocks, count, 2 * QB), jnp.float32),
            pltpu.VMEM((blocks, count, 2 * QB), jnp.bfloat16),
        ],
        compiler_params=params(),
        cost_estimate=pl.CostEstimate(flops=5 * 2**30, bytes_accessed=6 * 2**20, transcendentals=5 * 2**20),
    )(q, k, v)


def fine_before(where, q, keys, values, state):
    count, width = q.shape
    blocks = count // QB
    half = count // 2
    return pl.pallas_call(
        fine_before_kernel,
        name="fine_before",
        grid=(width // PAIR,),
        in_specs=[pl.BlockSpec(memory_space=pltpu.SMEM), pl.BlockSpec((count, PAIR), lambda i: (0, i))]
        + [pl.BlockSpec((half, PAIR), lambda i: (0, i))] * 2
        + [pl.BlockSpec((PAIR, half), lambda i: (i, 0))] * 2
        + [
            pl.BlockSpec((1, blocks, 8, 2 * QB), lambda i: (i, 0, 0, 0)),
            pl.BlockSpec((1, blocks, 16 + HEAD_DIM, 2 * QB), lambda i: (i, 0, 0, 0)),
        ],
        out_specs=pl.BlockSpec((2, half, PAIR), lambda i: (0, 0, i)),
        out_shape=jax.ShapeDtypeStruct((2, half, width), jnp.bfloat16),
        scratch_shapes=[
            pltpu.VMEM((count, PAIR), jnp.bfloat16),
            pltpu.VMEM((PAIR, count), jnp.bfloat16),
            pltpu.VMEM((blocks, count, 2 * QB), jnp.float32),
            pltpu.VMEM((blocks, count, 2 * QB), jnp.bfloat16),
        ],
        compiler_params=params(),
        cost_estimate=pl.CostEstimate(flops=5 * 2**30, bytes_accessed=6 * 2**20, transcendentals=5 * 2**20),
    )(where, q, *keys, *values, *state)


def pack_kernel(hidden_ref, tail_ref, out_ref):
    blocks, places, groups, width = hidden_ref.shape
    rows = blocks * groups
    half = width // 2
    for j in range(SHORT):
        p = (j + 1) % SHORT
        part = hidden_ref[:, p].reshape(rows, width)
        if p > 0:
            wide = part.astype(jnp.float32)
            tail = tail_ref[p : p + 1, :].astype(jnp.float32)
            first = lax.broadcasted_iota(jnp.int32, wide.shape, 0) == 0
            wide = jnp.where(first, tail, pltpu.roll(wide, 1, 0))
            part = wide.astype(jnp.bfloat16)
        for f in range(2):
            out_ref[(j % 2) * 2 + f, j // 2] = part[:, f * half : (f + 1) * half]


def pack(hidden, tail):
    count, width = hidden.shape
    groups = QB // SHORT
    blocks = count // QB
    return pl.pallas_call(
        pack_kernel,
        name="pack",
        out_shape=jax.ShapeDtypeStruct((4, 4, count // SHORT, width // 2), jnp.bfloat16),
        compiler_params=params(),
    )(hidden.reshape(blocks, SHORT, groups, width), tail)


def shorten_kernel(grouped_ref, weight_ref, out_ref):
    owners, parts, rows, depth = grouped_ref.shape
    total = None
    for j in range(parts):
        part = grouped_ref[:, j].reshape(owners * rows, depth)
        term = dot(part, weight_ref[j], ((1,), (0,)))
        total = term if total is None else total + term
    out_ref[...] = total.reshape(owners, rows, -1).astype(jnp.bfloat16)


def shorten(grouped, weight):
    owners, parts, rows, depth = grouped.shape
    width = weight.shape[1]
    tile = width // 4
    return pl.pallas_call(
        shorten_kernel,
        name="shorten",
        grid=(4,),
        in_specs=[
            pl.BlockSpec(grouped.shape, lambda i: (0, 0, 0, 0)),
            pl.BlockSpec((parts, depth, tile), lambda i: (0, 0, i)),
        ],
        out_specs=pl.BlockSpec((owners, rows, tile), lambda i: (0, 0, i)),
        out_shape=jax.ShapeDtypeStruct((owners, rows, width), jnp.bfloat16),
        compiler_params=params(60),
    )(grouped, weight.reshape(parts, depth, width))


def coarse_project_kernel(part_ref, q_ref, k_ref, v_ref, short_ref, qkv_ref, norm_ref):
    @pl.when(pl.program_id(0) == 0)
    def _():
        short = jnp.sum(part_ref[...].astype(jnp.float32), axis=0).astype(jnp.bfloat16)
        short_ref[...] = short
        norm_ref[...] = normed(short)

    rows = norm_ref[...]
    for i, (ref, scale) in enumerate(((k_ref, None), (v_ref, None), (q_ref, SCALE))):
        out = dot(rows, ref[...], ((1,), (0,)))
        if scale is not None:
            out = out * scale
        out = out.astype(jnp.bfloat16)
        for h in range(qkv_ref.shape[0]):
            qkv_ref[h, :, i * HEAD_DIM : (i + 1) * HEAD_DIM] = out[:, h * HEAD_DIM : (h + 1) * HEAD_DIM]


def coarse_project(partial, query, key, value):
    owners, rows, width = partial.shape
    tile = 4 * HEAD_DIM
    spec = pl.BlockSpec((width, tile), lambda i: (0, i))
    return pl.pallas_call(
        coarse_project_kernel,
        name="coarse_project",
        grid=(width // tile,),
        in_specs=[pl.BlockSpec(partial.shape, lambda i: (0, 0, 0)), spec, spec, spec],
        out_specs=[
            pl.BlockSpec((rows, width), lambda i: (0, 0)),
            pl.BlockSpec((4, rows, 3 * HEAD_DIM), lambda i: (i, 0, 0)),
        ],
        out_shape=[
            jax.ShapeDtypeStruct((rows, width), jnp.bfloat16),
            jax.ShapeDtypeStruct((HEADS, rows, 3 * HEAD_DIM), jnp.bfloat16),
        ],
        scratch_shapes=[pltpu.VMEM((rows, width), jnp.bfloat16)],
        compiler_params=params(),
    )(partial, query, key, value)


def finish_kernel(mixed_ref, out_weight_ref, short_ref, hidden_ref, out_ref):
    heads, rows, _ = mixed_ref.shape
    mixed = jnp.concatenate([mixed_ref[h] for h in range(heads)], axis=1)
    refined = short_ref[...].astype(jnp.float32) + dot(mixed, out_weight_ref[...], ((1,), (0,)))
    tile = refined.shape[1]
    spread = jnp.broadcast_to(refined[:, None, :], (rows, SHORT, tile)).reshape(rows * SHORT, tile)
    out_ref[...] = (hidden_ref[...].astype(jnp.float32) + spread).astype(jnp.bfloat16)


def finish(mixed, out_weight, short, hidden):
    count, width = hidden.shape
    heads, rows, _ = mixed.shape
    tile = width // 4
    return pl.pallas_call(
        finish_kernel,
        name="finish",
        grid=(4,),
        in_specs=[
            pl.BlockSpec(mixed.shape, lambda i: (0, 0, 0)),
            pl.BlockSpec((width, tile), lambda i: (0, i)),
            pl.BlockSpec((rows, tile), lambda i: (0, i)),
            pl.BlockSpec((count, tile), lambda i: (0, i)),
        ],
        out_specs=pl.BlockSpec((count, tile), lambda i: (0, i)),
        out_shape=jax.ShapeDtypeStruct((count, width), jnp.bfloat16),
        compiler_params=params(60),
    )(mixed, out_weight, short, hidden)


def coarse_kernel(number, first, final, where_ref, q_ref, *refs):
    parts = refs[:number]
    old = None if first else refs[number : number + 2]
    outs = refs[number if first else number + 2 :]
    blocks, rows, _ = parts[0].shape
    tile = 4 * rows
    tiles = blocks // 4
    lane = lax.broadcasted_iota(jnp.int32, (1, tile), 1)
    row = lax.broadcasted_iota(jnp.int32, (tile, tile), 0)
    stride = 8 * rows
    place = (row // rows) * stride + row % rows
    limit = (lane // rows) * stride + where_ref[0] * rows + lane % rows
    ones = jnp.ones((16, number * tile), jnp.bfloat16)
    queries = []
    for t in range(tiles):
        q = q_ref[4 * t : 4 * t + 4, :, 2 * HEAD_DIM :].reshape(tile, HEAD_DIM)
        queries.append(jnp.concatenate([q, jnp.zeros_like(q)], axis=1))
    if first:
        tops = [jnp.full((1, tile), NEG, jnp.float32)] * tiles
        accs = [jnp.zeros((16 + HEAD_DIM, tile), jnp.float32)] * tiles
    else:
        tops = [old[0][t, 0:1, :] for t in range(tiles)]
        accs = [old[1][t] for t in range(tiles)]
    for g in range(tiles):
        kv = jnp.concatenate([part[4 * g : 4 * g + 4].reshape(tile, PAIR) for part in parts], axis=0)
        v = jnp.concatenate([ones, kv.T[HEAD_DIM:, :]], axis=0)
        live = range(g, tiles)
        scores = [dot(kv, queries[t], ((1,), (1,))) for t in live]
        keep = jnp.concatenate(
            [place <= limit - where_ref[1 + i] * rows for i in range(number)], axis=0
        )
        scores[0] = jnp.where(keep, scores[0], NEG)
        news = [jnp.maximum(tops[t], jnp.max(s, axis=0, keepdims=True)) for t, s in zip(live, scores)]
        ps = [jnp.exp2(s - top).astype(jnp.bfloat16) for s, top in zip(scores, news)]
        for t, top, p in zip(live, news, ps):
            accs[t] = accs[t] * jnp.exp2(tops[t] - top) + dot(v, p, ((1,), (0,)))
            tops[t] = top
    for t in range(tiles):
        if final:
            o = accs[t][16:] * (1.0 / accs[t][0:1])
            outs[0][4 * t : 4 * t + 4] = o.T.astype(jnp.bfloat16).reshape(4, rows, HEAD_DIM)
        else:
            outs[0][t] = jnp.broadcast_to(tops[t], (8, tile))
            outs[1][t] = accs[t]


def coarse_attend(places, q, parts, state, final):
    heads, rows, _ = q.shape
    tile = 4 * rows
    if final:
        out_shape = jax.ShapeDtypeStruct((heads, rows, HEAD_DIM), jnp.bfloat16)
    else:
        out_shape = [
            jax.ShapeDtypeStruct((heads // 4, 8, tile), jnp.float32),
            jax.ShapeDtypeStruct((heads // 4, 16 + HEAD_DIM, tile), jnp.float32),
        ]
    first = state is None
    arrays = [q, *parts] + ([] if first else list(state))
    share = len(parts) / 8
    return pl.pallas_call(
        functools.partial(coarse_kernel, len(parts), first, final),
        in_specs=[pl.BlockSpec(memory_space=pltpu.SMEM)]
        + [pl.BlockSpec(memory_space=pltpu.VMEM)] * len(arrays),
        out_shape=out_shape,
        name="coarse_attend",
        compiler_params=params(),
        cost_estimate=pl.CostEstimate(
            flops=int(share * 6 * 2**30), bytes_accessed=2 * 2**20, transcendentals=int(share * 5 * 2**20)
        ),
    )(jnp.stack(places).astype(jnp.int32), *arrays)


def body(
    tokens,
    fine_query,
    fine_key,
    fine_value,
    fine_out,
    short_weight,
    coarse_query,
    coarse_key,
    coarse_value,
    coarse_out,
):
    count, width = tokens.shape
    bf = jnp.bfloat16
    place = lax.axis_index(ALL).astype(jnp.int32)
    groups = QB // SHORT
    blocks = count // QB
    core = lax.axis_index("c").astype(jnp.int32)

    def across(block):
        return lax.ppermute(block, "c", [(0, 1), (1, 0)])

    far = from_behind(tokens, 2)
    shuffled = tokens.reshape(blocks, groups, SHORT, width)
    shuffled = jnp.transpose(shuffled, (0, 2, 1, 3)).reshape(count, width)
    mate = across(shuffled)
    half = width // 2

    def own_heads(weight, axis):
        return lax.dynamic_slice_in_dim(weight, core * half, half, axis)

    query_weight, key_weight, value_weight = (
        own_heads(weight, 1) for weight in (fine_query, fine_key, fine_value)
    )
    out_weight = own_heads(fine_out, 0)
    out_weight_mate = lax.dynamic_slice_in_dim(fine_out, (1 - core) * half, half, 0)
    chip = normed(
        jnp.concatenate(
            [jnp.where(core == 0, shuffled, mate), jnp.where(core == 0, mate, shuffled)], axis=0
        )
    )

    def keys_values(rows):
        keys = dot(rows, key_weight, ((1,), (0,))).astype(bf)
        return keys, dot(value_weight, rows, ((0,), (1,))).astype(bf)

    query = (dot(chip, query_weight, ((1,), (0,))) * SCALE).astype(bf)
    state = fine_own(query, *keys_values(chip))
    far, state, query, short_weight, out_weight, out_weight_mate = lax.optimization_barrier(
        (far, state, query, short_weight, out_weight, out_weight_mate)
    )
    near = across(far)
    weight = lax.all_gather(short_weight, ("x", "c"), axis=0, tiled=True)
    keys, values = zip(keys_values(normed(far)), keys_values(normed(near)))
    where = jnp.stack([core, (place > 1).astype(jnp.int32)])
    fine_mixed = fine_before(where, query, keys, values, state)
    theirs = across(fine_mixed[1])
    hidden = shuffled.astype(jnp.float32) + dot(fine_mixed[0], out_weight, ((1,), (0,)))
    hidden = (hidden + dot(theirs, out_weight_mate, ((1,), (0,)))).astype(bf)
    tail = from_behind(hidden.reshape(blocks, SHORT, groups, width)[-1, :, -1], 1)
    rows = count // SHORT
    grouped = lax.all_to_all(pack(hidden, tail), "y", 0, 0)
    partial = lax.all_to_all(shorten(grouped, weight), "y", 0, 0)
    shortened, qkv = coarse_project(partial, coarse_query, coarse_key, coarse_value)
    natural = jnp.transpose(hidden.reshape(blocks, SHORT, groups, width), (0, 2, 1, 3)).reshape(count, width)
    qkv = lax.all_to_all(qkv, ("z", "x"), 0, 0)
    kv = qkv[:, :, : 2 * HEAD_DIM]
    y, c = lax.axis_index("y"), lax.axis_index("c")
    mine = y * 2 + c

    def around(block, distance):
        return lax.ppermute(block, "y", [(i, (i + distance) % 4) for i in range(4)])

    def spot(distance, other=0):
        return ((y + distance) % 4) * 2 + (1 - c if other else c)

    mate_kv = across(kv)
    below, above, beyond = around(kv, 1), around(kv, 3), around(kv, 2)
    state = coarse_attend((mine, mine, spot(0, 1)), qkv, (kv, mate_kv), None, False)
    others = (below, above, beyond)
    state, *others = lax.optimization_barrier((state, *others))
    swapped = [across(block) for block in others]
    state = coarse_attend((mine, spot(3), spot(1), spot(2)), qkv, others, state, False)
    state, *swapped = lax.optimization_barrier((state, *swapped))
    mixed = coarse_attend((mine, spot(3, 1), spot(1, 1), spot(2, 1)), qkv, swapped, state, True)
    mixed = lax.all_to_all(mixed, ("z", "x"), 0, 0)
    return finish(mixed, coarse_out, shortened, natural)


def solution(mesh):
    fine = Mesh(mesh.devices.reshape(4, 4, 4, 2), ALL)
    return jax.shard_map(
        body,
        mesh=fine,
        in_specs=(P(ALL, None), P(), P(), P(), P(), P(("x", "y", "c"), None), P(), P(), P(), P()),
        out_specs=P(ALL, None),
        check_vma=False,
    )
```

```python
import functools
import math

import jax
import jax.numpy as jnp
from jax import lax
from jax.experimental import pallas as pl
from jax.experimental.pallas import tpu as pltpu
from jax.sharding import Mesh, PartitionSpec as P

HEAD_DIM = 64
HEADS = 16
SHORT = 8
WIN = 1024
SCALE = math.log2(math.e) / math.sqrt(HEAD_DIM)
ALL = ("z", "x", "y", "c")
QB = 128
PAIR = 2 * HEAD_DIM
NEG = -1e30


def from_behind(block, distance):
    devices = range(128)
    route = [(i - distance, i) for i in devices if i - distance in devices]
    return lax.ppermute(block, ALL, route)


def normed(rows):
    values = rows.astype(jnp.float32)
    scale = lax.rsqrt(jnp.mean(values * values, axis=-1, keepdims=True) + 1e-06)
    return (values * scale).astype(jnp.bfloat16)


def dot(a, b, contract):
    return lax.dot_general(a, b, (contract, ((), ())), preferred_element_type=jnp.float32)


def params(mib=48):
    return pltpu.CompilerParams(vmem_limit_bytes=mib * 2**20)


def spots(index):
    groups = QB // SHORT
    return (index % groups) * SHORT + index // groups


def two_heads(q_ref, b):
    lane = lax.broadcasted_iota(jnp.int32, (QB, PAIR), 1)
    q = q_ref[b * QB : (b + 1) * QB, :]
    zero = jnp.zeros_like(q)
    return jnp.concatenate(
        [jnp.where(lane < HEAD_DIM, q, zero), jnp.where(lane < HEAD_DIM, zero, q)], axis=0
    )


def with_sums(v):
    return jnp.concatenate([v, jnp.ones((16, v.shape[1]), jnp.bfloat16)], axis=0)


def moves(rows, take):
    col = lax.broadcasted_iota(jnp.int32, (rows, QB), 1)
    row = lax.broadcasted_iota(jnp.int32, (rows, QB), 0)
    return jnp.where(take(row) == col, 1.0, 0.0).astype(jnp.bfloat16)


def reorder(move, rows):
    parts = [dot(move, rows[i : i + QB], ((1,), (0,))) for i in range(0, rows.shape[0], QB)]
    return jnp.concatenate(parts, axis=0)


def project_kernel(number, rows_ref, *refs):
    weights, outs = refs[:number], refs[number:]
    rows = normed(rows_ref[...])
    if number == 3:
        rows = reorder(moves(QB, spots), rows).astype(jnp.bfloat16)
        outs[2][...] = (dot(rows, weights[2][...], ((1,), (0,))) * SCALE).astype(jnp.bfloat16)
    outs[0][...] = dot(rows, weights[0][...], ((1,), (0,))).astype(jnp.bfloat16)
    outs[1][...] = dot(weights[1][...], rows, ((1,), (1,))).astype(jnp.bfloat16)


def project(rows, weights):
    count, width = rows.shape
    half = width // 2
    tile = 512
    by_row = pl.BlockSpec((tile, half), lambda i: (i, 0))
    number = len(weights)
    return pl.pallas_call(
        functools.partial(project_kernel, number),
        name="project",
        grid=(count // tile,),
        in_specs=[pl.BlockSpec((tile, width), lambda i: (i, 0))]
        + [pl.BlockSpec(weight.shape, lambda i: (0, 0)) for weight in weights],
        out_specs=[by_row, pl.BlockSpec((half, tile), lambda i: (0, i)), by_row][:number],
        out_shape=[
            jax.ShapeDtypeStruct((count, half), jnp.bfloat16),
            jax.ShapeDtypeStruct((half, count), jnp.bfloat16),
            jax.ShapeDtypeStruct((count, half), jnp.bfloat16),
        ][:number],
        compiler_params=params(20),
        cost_estimate=pl.CostEstimate(
            flops=2 * number * count * width * half, bytes_accessed=4 * 2**20, transcendentals=0
        ),
    )(rows, *weights)


def out_project_kernel(tokens_ref, mine_ref, theirs_ref, my_ref, their_ref, hidden_ref, natural_ref, tail_ref):
    total = reorder(moves(QB, spots), tokens_ref[...])
    total = total + dot(mine_ref[0], my_ref[...], ((1,), (0,)))
    total = total + dot(theirs_ref[...], their_ref[...], ((1,), (0,)))
    hidden = total.astype(jnp.bfloat16)
    hidden_ref[...] = hidden
    groups = QB // SHORT
    natural_ref[...] = reorder(moves(QB, lambda r: (r % SHORT) * groups + r // SHORT), hidden).astype(jnp.bfloat16)
    tail = dot(moves(16, lambda r: r * groups + groups - 1), hidden[-QB:], ((1,), (0,)))
    tail_ref[...] = tail.astype(jnp.bfloat16)


def out_project(tokens, mixed, theirs, my_weight, their_weight):
    count, width = tokens.shape
    half = width // 2
    tile = width // 2
    by_column = pl.BlockSpec((count, tile), lambda i: (0, i))
    return pl.pallas_call(
        out_project_kernel,
        name="out_project",
        grid=(width // tile,),
        in_specs=[
            by_column,
            pl.BlockSpec((1, count, half), lambda i: (0, 0, 0)),
            pl.BlockSpec((count, half), lambda i: (0, 0)),
            pl.BlockSpec((half, tile), lambda i: (0, i)),
            pl.BlockSpec((half, tile), lambda i: (0, i)),
        ],
        out_specs=[by_column, by_column, pl.BlockSpec((16, tile), lambda i: (0, i))],
        out_shape=[
            jax.ShapeDtypeStruct((count, width), jnp.bfloat16),
            jax.ShapeDtypeStruct((count, width), jnp.bfloat16),
            jax.ShapeDtypeStruct((16, width), jnp.bfloat16),
        ],
        compiler_params=params(20),
    )(tokens, mixed, theirs, my_weight, their_weight)


def fine_own_kernel(q_ref, k_ref, v_ref, top_ref, acc_ref, s_ref, p_ref):
    blocks = q_ref.shape[0] // QB
    row = lax.broadcasted_iota(jnp.int32, (QB, 2 * QB), 0)
    col = lax.broadcasted_iota(jnp.int32, (QB, 2 * QB), 1) % QB
    keep = spots(row) <= spots(col)
    for b in range(blocks):
        both = two_heads(q_ref, b)
        if b > 0:
            s_ref[b, : b * QB, :] = dot(k_ref[: b * QB, :], both, ((1,), (1,)))
        s = dot(k_ref[b * QB : (b + 1) * QB, :], both, ((1,), (1,)))
        s_ref[b, b * QB : (b + 1) * QB, :] = jnp.where(keep, s, NEG)
    for b in range(blocks):
        end = (b + 1) * QB
        top = jnp.max(s_ref[b, :end, :], axis=0, keepdims=True)
        p_ref[b, :end, :] = jnp.exp2(s_ref[b, :end, :] - top).astype(jnp.bfloat16)
        top_ref[0, b] = jnp.broadcast_to(top, (8, 2 * QB))
    for b in range(blocks):
        end = (b + 1) * QB
        o = dot(with_sums(v_ref[:, :end]), p_ref[b, :end, :], ((1,), (0,)))
        acc_ref[0, b, :16, :] = o[PAIR:]
        acc_ref[0, b, 16:, :QB] = o[:HEAD_DIM, :QB]
        acc_ref[0, b, 16:, QB:] = o[HEAD_DIM:PAIR, QB:]


def fine_before_kernel(
    where_ref, q_ref, kf_ref, kn_ref, vf_ref, vn_ref, top_ref, acc_ref, out_ref, k_ref, v_ref, s_ref, p_ref
):
    half = kf_ref.shape[0]
    blocks = q_ref.shape[0] // QB
    core = where_ref[0]
    row = lax.broadcasted_iota(jnp.int32, (QB, 2 * QB), 0)
    col = lax.broadcasted_iota(jnp.int32, (QB, 2 * QB), 1) % QB
    keep = row > spots(col)

    def store(b, total, o):
        o = o * (1.0 / total)
        mixed = jnp.concatenate([o[:, :QB], o[:, QB:]], axis=0)
        at = b * QB // half
        out_ref[(at + core) % 2, b * QB - at * half : (b + 1) * QB - at * half, :] = mixed.T.astype(jnp.bfloat16)

    @pl.when(where_ref[1] == 0)
    def _():
        for b in range(blocks):
            store(b, acc_ref[0, b, 0:1, :], acc_ref[0, b, 16:, :])

    @pl.when(where_ref[1] > 0)
    def _():
        mine = pl.ds(pl.multiple_of(core * half, half), half)
        other = pl.ds(pl.multiple_of((1 - core) * half, half), half)
        k_ref[mine, :] = kf_ref[...]
        k_ref[other, :] = kn_ref[...]
        v_ref[:, mine] = vf_ref[...]
        v_ref[:, other] = vn_ref[...]
        for b in range(blocks):
            both = two_heads(q_ref, b)
            s = dot(k_ref[b * QB : (b + 1) * QB, :], both, ((1,), (1,)))
            s_ref[b, b * QB : (b + 1) * QB, :] = jnp.where(keep, s, NEG)
            if b < blocks - 1:
                s_ref[b, (b + 1) * QB :, :] = dot(k_ref[(b + 1) * QB :, :], both, ((1,), (1,)))
        fades = []
        for b in range(blocks):
            old = top_ref[0, b, 0:1, :]
            top = jnp.maximum(old, jnp.max(s_ref[b, b * QB :, :], axis=0, keepdims=True))
            p_ref[b, b * QB :, :] = jnp.exp2(s_ref[b, b * QB :, :] - top).astype(jnp.bfloat16)
            fades.append(jnp.exp2(old - top))
        for b in range(blocks):
            o = dot(with_sums(v_ref[:, b * QB :]), p_ref[b, b * QB :, :], ((1,), (0,)))
            acc = acc_ref[0, b] * fades[b]
            new = jnp.concatenate([o[:HEAD_DIM, :QB], o[HEAD_DIM:PAIR, QB:]], axis=1)
            store(b, acc[0:1] + o[PAIR : PAIR + 1], acc[16:] + new)


def fine_own(q, k, v):
    count, width = q.shape
    blocks = count // QB
    pairs = width // PAIR
    return pl.pallas_call(
        fine_own_kernel,
        name="fine_own",
        grid=(pairs,),
        in_specs=[
            pl.BlockSpec((count, PAIR), lambda i: (0, i)),
            pl.BlockSpec((count, PAIR), lambda i: (0, i)),
            pl.BlockSpec((PAIR, count), lambda i: (i, 0)),
        ],
        out_specs=[
            pl.BlockSpec((1, blocks, 8, 2 * QB), lambda i: (i, 0, 0, 0)),
            pl.BlockSpec((1, blocks, 16 + HEAD_DIM, 2 * QB), lambda i: (i, 0, 0, 0)),
        ],
        out_shape=[
            jax.ShapeDtypeStruct((pairs, blocks, 8, 2 * QB), jnp.float32),
            jax.ShapeDtypeStruct((pairs, blocks, 16 + HEAD_DIM, 2 * QB), jnp.float32),
        ],
        scratch_shapes=[
            pltpu.VMEM((blocks, count, 2 * QB), jnp.float32),
            pltpu.VMEM((blocks, count, 2 * QB), jnp.bfloat16),
        ],
        compiler_params=params(),
        cost_estimate=pl.CostEstimate(flops=5 * 2**30, bytes_accessed=6 * 2**20, transcendentals=5 * 2**20),
    )(q, k, v)


def fine_before(where, q, keys, values, state):
    count, width = q.shape
    blocks = count // QB
    half = count // 2
    return pl.pallas_call(
        fine_before_kernel,
        name="fine_before",
        grid=(width // PAIR,),
        in_specs=[pl.BlockSpec(memory_space=pltpu.SMEM), pl.BlockSpec((count, PAIR), lambda i: (0, i))]
        + [pl.BlockSpec((half, PAIR), lambda i: (0, i))] * 2
        + [pl.BlockSpec((PAIR, half), lambda i: (i, 0))] * 2
        + [
            pl.BlockSpec((1, blocks, 8, 2 * QB), lambda i: (i, 0, 0, 0)),
            pl.BlockSpec((1, blocks, 16 + HEAD_DIM, 2 * QB), lambda i: (i, 0, 0, 0)),
        ],
        out_specs=pl.BlockSpec((2, half, PAIR), lambda i: (0, 0, i)),
        out_shape=jax.ShapeDtypeStruct((2, half, width), jnp.bfloat16),
        scratch_shapes=[
            pltpu.VMEM((count, PAIR), jnp.bfloat16),
            pltpu.VMEM((PAIR, count), jnp.bfloat16),
            pltpu.VMEM((blocks, count, 2 * QB), jnp.float32),
            pltpu.VMEM((blocks, count, 2 * QB), jnp.bfloat16),
        ],
        compiler_params=params(),
        cost_estimate=pl.CostEstimate(flops=5 * 2**30, bytes_accessed=6 * 2**20, transcendentals=5 * 2**20),
    )(where, q, *keys, *values, *state)


def pack_kernel(hidden_ref, tail_ref, out_ref):
    blocks, places, groups, width = hidden_ref.shape
    rows = blocks * groups
    half = width // 2
    for j in range(SHORT):
        p = (j + 1) % SHORT
        part = hidden_ref[:, p].reshape(rows, width)
        if p > 0:
            wide = part.astype(jnp.float32)
            tail = tail_ref[p : p + 1, :].astype(jnp.float32)
            first = lax.broadcasted_iota(jnp.int32, wide.shape, 0) == 0
            wide = jnp.where(first, tail, pltpu.roll(wide, 1, 0))
            part = wide.astype(jnp.bfloat16)
        for f in range(2):
            out_ref[(j % 2) * 2 + f, j // 2] = part[:, f * half : (f + 1) * half]


def pack(hidden, tail):
    count, width = hidden.shape
    groups = QB // SHORT
    blocks = count // QB
    return pl.pallas_call(
        pack_kernel,
        name="pack",
        out_shape=jax.ShapeDtypeStruct((4, 4, count // SHORT, width // 2), jnp.bfloat16),
        compiler_params=params(),
    )(hidden.reshape(blocks, SHORT, groups, width), tail)


def shorten_kernel(where_ref, grouped_ref, *refs):
    pieces, out_ref = refs[:-1], refs[-1]
    owners, parts, rows, depth = grouped_ref.shape
    size = depth // 2
    total = None
    for i, piece in enumerate(pieces):
        x = (where_ref[0] + parts - i % parts) % parts
        core = where_ref[1] if i < parts else 1 - where_ref[1]
        columns = pl.ds(pl.multiple_of(core * size, size), size)
        part = grouped_ref[:, x, :, columns].reshape(owners * rows, size)
        term = dot(part, piece[...], ((1,), (0,)))
        total = term if total is None else total + term
    out_ref[...] = total.reshape(owners, rows, -1).astype(jnp.bfloat16)


def shorten(where, grouped, pieces):
    owners, parts, rows, depth = grouped.shape
    width = pieces[0].shape[1]
    tile = width // 4
    return pl.pallas_call(
        shorten_kernel,
        name="shorten",
        grid=(4,),
        in_specs=[
            pl.BlockSpec(memory_space=pltpu.SMEM),
            pl.BlockSpec(grouped.shape, lambda i: (0, 0, 0, 0)),
        ]
        + [pl.BlockSpec((depth // 2, tile), lambda i: (0, i))] * len(pieces),
        out_specs=pl.BlockSpec((owners, rows, tile), lambda i: (0, 0, i)),
        out_shape=jax.ShapeDtypeStruct((owners, rows, width), jnp.bfloat16),
        compiler_params=params(60),
    )(where, grouped, *pieces)


def coarse_project_kernel(part_ref, q_ref, k_ref, v_ref, short_ref, qkv_ref, norm_ref):
    @pl.when(pl.program_id(0) == 0)
    def _():
        short = jnp.sum(part_ref[...].astype(jnp.float32), axis=0).astype(jnp.bfloat16)
        short_ref[...] = short
        norm_ref[...] = normed(short)

    rows = norm_ref[...]
    for i, (ref, scale) in enumerate(((k_ref, None), (v_ref, None), (q_ref, SCALE))):
        out = dot(rows, ref[...], ((1,), (0,)))
        if scale is not None:
            out = out * scale
        out = out.astype(jnp.bfloat16)
        for h in range(qkv_ref.shape[0]):
            qkv_ref[h, :, i * HEAD_DIM : (i + 1) * HEAD_DIM] = out[:, h * HEAD_DIM : (h + 1) * HEAD_DIM]


def coarse_project(partial, query, key, value):
    owners, rows, width = partial.shape
    tile = 4 * HEAD_DIM
    spec = pl.BlockSpec((width, tile), lambda i: (0, i))
    return pl.pallas_call(
        coarse_project_kernel,
        name="coarse_project",
        grid=(width // tile,),
        in_specs=[pl.BlockSpec(partial.shape, lambda i: (0, 0, 0)), spec, spec, spec],
        out_specs=[
            pl.BlockSpec((rows, width), lambda i: (0, 0)),
            pl.BlockSpec((4, rows, 3 * HEAD_DIM), lambda i: (i, 0, 0)),
        ],
        out_shape=[
            jax.ShapeDtypeStruct((rows, width), jnp.bfloat16),
            jax.ShapeDtypeStruct((HEADS, rows, 3 * HEAD_DIM), jnp.bfloat16),
        ],
        scratch_shapes=[pltpu.VMEM((rows, width), jnp.bfloat16)],
        compiler_params=params(60),
    )(partial, query, key, value)


def finish_kernel(mixed_ref, out_weight_ref, short_ref, hidden_ref, out_ref, rows_ref):
    heads, rows, _ = mixed_ref.shape
    rows = 2 * rows

    @pl.when(pl.program_id(0) == 0)
    def _():
        for h in range(heads):
            m = mixed_ref[h]
            rows_ref[:, h * HEAD_DIM : (h + 1) * HEAD_DIM] = jnp.concatenate(
                [m[:, :HEAD_DIM], m[:, HEAD_DIM:]], axis=0
            )

    refined = short_ref[...].astype(jnp.float32) + dot(rows_ref[...], out_weight_ref[...], ((1,), (0,)))
    tile = refined.shape[1]
    spread = jnp.broadcast_to(refined[:, None, :], (rows, SHORT, tile)).reshape(rows * SHORT, tile)
    out_ref[...] = (hidden_ref[...].astype(jnp.float32) + spread).astype(jnp.bfloat16)


def finish(mixed, out_weight, short, hidden):
    count, width = hidden.shape
    rows = count // SHORT
    tile = width // 4
    return pl.pallas_call(
        finish_kernel,
        name="finish",
        grid=(4,),
        in_specs=[
            pl.BlockSpec(mixed.shape, lambda i: (0, 0, 0)),
            pl.BlockSpec((width, tile), lambda i: (0, i)),
            pl.BlockSpec((rows, tile), lambda i: (0, i)),
            pl.BlockSpec((count, tile), lambda i: (0, i)),
        ],
        out_specs=pl.BlockSpec((count, tile), lambda i: (0, i)),
        out_shape=jax.ShapeDtypeStruct((count, width), jnp.bfloat16),
        scratch_shapes=[pltpu.VMEM((rows, width), jnp.bfloat16)],
        compiler_params=params(60),
    )(mixed, out_weight, short, hidden)


def coarse_kernel(number, first, final, where_ref, q_ref, *refs):
    parts = refs[:number]
    old = None if first else refs[number : number + 2]
    outs = refs[number if first else number + 2 :]
    blocks, rows, _ = parts[0].shape
    tile = 4 * rows
    tiles = blocks // 4
    lane = lax.broadcasted_iota(jnp.int32, (1, tile), 1)
    row = lax.broadcasted_iota(jnp.int32, (tile, tile), 0)
    stride = 8 * rows
    place = (row // rows) * stride + row % rows
    limit = (lane // rows) * stride + where_ref[0] * rows + lane % rows
    ones = jnp.ones((16, number * tile), jnp.bfloat16)
    queries = []
    for t in range(tiles):
        q = q_ref[4 * t : 4 * t + 4, :, 2 * HEAD_DIM :].reshape(tile, HEAD_DIM)
        queries.append(jnp.concatenate([q, jnp.zeros_like(q)], axis=1))
    if first:
        tops = [jnp.full((1, tile), NEG, jnp.float32)] * tiles
        accs = [jnp.zeros((16 + HEAD_DIM, tile), jnp.float32)] * tiles
    else:
        tops = [old[0][t, 0:1, :] for t in range(tiles)]
        accs = [old[1][t] for t in range(tiles)]
    for g in range(tiles):
        kv = jnp.concatenate([part[4 * g : 4 * g + 4].reshape(tile, PAIR) for part in parts], axis=0)
        v = jnp.concatenate([ones, kv.T[HEAD_DIM:, :]], axis=0)
        live = range(g, tiles)
        scores = [dot(kv, queries[t], ((1,), (1,))) for t in live]
        keep = jnp.concatenate(
            [place <= limit - where_ref[1 + i] * rows for i in range(number)], axis=0
        )
        scores[0] = jnp.where(keep, scores[0], NEG)
        news = [jnp.maximum(tops[t], jnp.max(s, axis=0, keepdims=True)) for t, s in zip(live, scores)]
        ps = [jnp.exp2(s - top).astype(jnp.bfloat16) for s, top in zip(scores, news)]
        for t, top, p in zip(live, news, ps):
            accs[t] = accs[t] * jnp.exp2(tops[t] - top) + dot(v, p, ((1,), (0,)))
            tops[t] = top
    for t in range(tiles):
        if final:
            o = accs[t][16:] * (1.0 / accs[t][0:1])
            o = o.T.astype(jnp.bfloat16)
            for i in range(0, tile, rows):
                low, high = o[i : i + rows // 2], o[i + rows // 2 : i + rows]
                outs[0][4 * t + i // rows] = jnp.concatenate([low, high], axis=1)
        else:
            outs[0][t] = jnp.broadcast_to(tops[t], (8, tile))
            outs[1][t] = accs[t]


def coarse_attend(places, q, parts, state, final):
    heads, rows, _ = q.shape
    tile = 4 * rows
    if final:
        out_shape = jax.ShapeDtypeStruct((heads, rows // 2, PAIR), jnp.bfloat16)
    else:
        out_shape = [
            jax.ShapeDtypeStruct((heads // 4, 8, tile), jnp.float32),
            jax.ShapeDtypeStruct((heads // 4, 16 + HEAD_DIM, tile), jnp.float32),
        ]
    first = state is None
    arrays = [q, *parts] + ([] if first else list(state))
    share = len(parts) / 8
    return pl.pallas_call(
        functools.partial(coarse_kernel, len(parts), first, final),
        in_specs=[pl.BlockSpec(memory_space=pltpu.SMEM)]
        + [pl.BlockSpec(memory_space=pltpu.VMEM)] * len(arrays),
        out_shape=out_shape,
        name="coarse_attend",
        compiler_params=params(),
        cost_estimate=pl.CostEstimate(
            flops=int(share * 6 * 2**30), bytes_accessed=2 * 2**20, transcendentals=int(share * 5 * 2**20)
        ),
    )(jnp.stack(places).astype(jnp.int32), *arrays)


def body(
    tokens,
    fine_query,
    fine_key,
    fine_value,
    fine_out,
    short_weight,
    coarse_query,
    coarse_key,
    coarse_value,
    coarse_out,
):
    count, width = tokens.shape
    bf = jnp.bfloat16
    place = lax.axis_index(ALL).astype(jnp.int32)
    core = lax.axis_index("c").astype(jnp.int32)

    def across(block):
        return lax.ppermute(block, "c", [(0, 1), (1, 0)])

    far = from_behind(tokens, 2)
    mate = across(tokens)
    half = width // 2

    def own_heads(weight, axis):
        return lax.dynamic_slice_in_dim(weight, core * half, half, axis)

    query_weight, key_weight, value_weight = (
        own_heads(weight, 1) for weight in (fine_query, fine_key, fine_value)
    )
    weights = [key_weight, value_weight.T]
    out_weight = own_heads(fine_out, 0)
    out_weight_mate = lax.dynamic_slice_in_dim(fine_out, (1 - core) * half, half, 0)
    chip = jnp.concatenate(
        [jnp.where(core == 0, tokens, mate), jnp.where(core == 0, mate, tokens)], axis=0
    )
    keys, values, query = project(chip, [*weights, query_weight])
    state = fine_own(query, keys, values)
    state, short_weight = lax.optimization_barrier((state, short_weight))
    pieces = [short_weight] + [
        lax.ppermute(short_weight, "x", [(i, (i + d) % 4) for i in range(4)]) for d in (1, 2, 3)
    ]
    far, state, query, out_weight, out_weight_mate = lax.optimization_barrier(
        (far, state, query, out_weight, out_weight_mate)
    )
    near = across(far)
    keys, values = zip(project(far, weights), project(near, weights))
    where = jnp.stack([core, (place > 1).astype(jnp.int32)])
    fine_mixed = fine_before(where, query, keys, values, state)
    theirs = across(fine_mixed[1])
    hidden, natural, tail = out_project(tokens, fine_mixed, theirs, out_weight, out_weight_mate)
    tail = from_behind(tail, 1)
    pieces = pieces + [across(piece) for piece in pieces]
    rows = count // SHORT
    grouped = lax.all_to_all(pack(hidden, tail), "y", 0, 0)
    where = jnp.stack([lax.axis_index("x").astype(jnp.int32), core])
    partial = lax.all_to_all(shorten(where, grouped, pieces), "y", 0, 0)
    shortened, qkv = coarse_project(partial, coarse_query, coarse_key, coarse_value)
    qkv = lax.all_to_all(qkv, ("z", "x"), 0, 0)
    kv = qkv[:, :, : 2 * HEAD_DIM]
    y, c = lax.axis_index("y"), lax.axis_index("c")
    mine = y * 2 + c

    def around(block, distance):
        return lax.ppermute(block, "y", [(i, (i + distance) % 4) for i in range(4)])

    def spot(distance, other=0):
        return ((y + distance) % 4) * 2 + (1 - c if other else c)

    mate_kv = across(kv)
    below, above, beyond = around(kv, 1), around(kv, 3), around(kv, 2)
    state = coarse_attend((mine, mine, spot(0, 1)), qkv, (kv, mate_kv), None, False)
    others = (below, above, beyond)
    state, *others = lax.optimization_barrier((state, *others))
    swapped = [across(block) for block in others]
    state = coarse_attend((mine, spot(3), spot(1), spot(2)), qkv, others, state, False)
    state, *swapped = lax.optimization_barrier((state, *swapped))
    mixed = coarse_attend((mine, spot(3, 1), spot(1, 1), spot(2, 1)), qkv, swapped, state, True)
    mixed = lax.all_to_all(mixed, ("z", "x"), 0, 0)
    return finish(mixed, coarse_out, shortened, natural)


def solution(mesh):
    fine = Mesh(mesh.devices.reshape(4, 4, 4, 2), ALL)
    return jax.shard_map(
        body,
        mesh=fine,
        in_specs=(P(ALL, None), P(), P(), P(), P(), P(("x", "y", "c"), None), P(), P(), P(), P()),
        out_specs=P(ALL, None),
        check_vma=False,
    )
```

```python
import functools
import math

import jax
import jax.numpy as jnp
from jax import lax
from jax.experimental import pallas as pl
from jax.experimental.pallas import tpu as pltpu
from jax.sharding import Mesh, PartitionSpec as P

HEAD_DIM = 64
HEADS = 16
SHORT = 8
WIN = 1024
SCALE = math.log2(math.e) / math.sqrt(HEAD_DIM)
ALL = ("z", "x", "y", "c")
QB = 128
PAIR = 2 * HEAD_DIM
NEG = -1e30


def from_behind(block, distance):
    devices = range(128)
    route = [(i - distance, i) for i in devices if i - distance in devices]
    return lax.ppermute(block, ALL, route)


def normed(rows):
    values = rows.astype(jnp.float32)
    scale = lax.rsqrt(jnp.mean(values * values, axis=-1, keepdims=True) + 1e-06)
    return (values * scale).astype(jnp.bfloat16)


def dot(a, b, contract):
    return lax.dot_general(a, b, (contract, ((), ())), preferred_element_type=jnp.float32)


def params(mib=24):
    return pltpu.CompilerParams(vmem_limit_bytes=mib * 2**20)


def spots(index):
    groups = QB // SHORT
    return (index % groups) * SHORT + index // groups


def two_heads(q_ref, b):
    lane = lax.broadcasted_iota(jnp.int32, (QB, PAIR), 1)
    q = q_ref[b * QB : (b + 1) * QB, :]
    zero = jnp.zeros_like(q)
    return jnp.concatenate(
        [jnp.where(lane < HEAD_DIM, q, zero), jnp.where(lane < HEAD_DIM, zero, q)], axis=0
    )


def with_sums(v):
    return jnp.concatenate([v, jnp.ones((16, v.shape[1]), jnp.bfloat16)], axis=0)


def moves(rows, take):
    col = lax.broadcasted_iota(jnp.int32, (rows, QB), 1)
    row = lax.broadcasted_iota(jnp.int32, (rows, QB), 0)
    return jnp.where(take(row) == col, 1.0, 0.0).astype(jnp.bfloat16)


def reorder(move, rows):
    parts = [dot(move, rows[i : i + QB], ((1,), (0,))) for i in range(0, rows.shape[0], QB)]
    return jnp.concatenate(parts, axis=0)


def project_kernel(number, rows_ref, *refs):
    weights, outs = refs[:number], refs[number:]
    rows = normed(rows_ref[...])
    if number == 3:
        rows = reorder(moves(QB, spots), rows).astype(jnp.bfloat16)
        outs[2][...] = (dot(rows, weights[2][...], ((1,), (0,))) * SCALE).astype(jnp.bfloat16)
    outs[0][...] = dot(rows, weights[0][...], ((1,), (0,))).astype(jnp.bfloat16)
    outs[1][...] = dot(weights[1][...], rows, ((1,), (1,))).astype(jnp.bfloat16)


def project(rows, weights):
    count, width = rows.shape
    half = width // 2
    tile = 512
    by_row = pl.BlockSpec((tile, half), lambda i: (i, 0))
    number = len(weights)
    return pl.pallas_call(
        functools.partial(project_kernel, number),
        name="project",
        grid=(count // tile,),
        in_specs=[pl.BlockSpec((tile, width), lambda i: (i, 0))]
        + [pl.BlockSpec(weight.shape, lambda i: (0, 0)) for weight in weights],
        out_specs=[by_row, pl.BlockSpec((half, tile), lambda i: (0, i)), by_row][:number],
        out_shape=[
            jax.ShapeDtypeStruct((count, half), jnp.bfloat16),
            jax.ShapeDtypeStruct((half, count), jnp.bfloat16),
            jax.ShapeDtypeStruct((count, half), jnp.bfloat16),
        ][:number],
        compiler_params=params(20),
        cost_estimate=pl.CostEstimate(flops=1, bytes_accessed=1, transcendentals=0)
    )(rows, *weights)


def out_project_kernel(tokens_ref, mine_ref, theirs_ref, my_ref, their_ref, hidden_ref, natural_ref, tail_ref):
    total = reorder(moves(QB, spots), tokens_ref[...])
    total = total + dot(mine_ref[0], my_ref[...], ((1,), (0,)))
    total = total + dot(theirs_ref[...], their_ref[...], ((1,), (0,)))
    hidden = total.astype(jnp.bfloat16)
    hidden_ref[...] = hidden
    groups = QB // SHORT
    natural_ref[...] = reorder(moves(QB, lambda r: (r % SHORT) * groups + r // SHORT), hidden).astype(jnp.bfloat16)
    tail = dot(moves(16, lambda r: r * groups + groups - 1), hidden[-QB:], ((1,), (0,)))
    tail_ref[...] = tail.astype(jnp.bfloat16)


def out_project(tokens, mixed, theirs, my_weight, their_weight):
    count, width = tokens.shape
    half = width // 2
    tile = width // 2
    by_column = pl.BlockSpec((count, tile), lambda i: (0, i))
    return pl.pallas_call(
        out_project_kernel,
        name="out_project",
        grid=(width // tile,),
        in_specs=[
            by_column,
            pl.BlockSpec((1, count, half), lambda i: (0, 0, 0)),
            pl.BlockSpec((count, half), lambda i: (0, 0)),
            pl.BlockSpec((half, tile), lambda i: (0, i)),
            pl.BlockSpec((half, tile), lambda i: (0, i)),
        ],
        out_specs=[by_column, by_column, pl.BlockSpec((16, tile), lambda i: (0, i))],
        out_shape=[
            jax.ShapeDtypeStruct((count, width), jnp.bfloat16),
            jax.ShapeDtypeStruct((count, width), jnp.bfloat16),
            jax.ShapeDtypeStruct((16, width), jnp.bfloat16),
        ],
        compiler_params=params(20),
    )(tokens, mixed, theirs, my_weight, their_weight)


def fine_own_kernel(q_ref, k_ref, v_ref, top_ref, acc_ref, s_ref, p_ref):
    blocks = q_ref.shape[0] // QB
    row = lax.broadcasted_iota(jnp.int32, (QB, 2 * QB), 0)
    col = lax.broadcasted_iota(jnp.int32, (QB, 2 * QB), 1) % QB
    keep = spots(row) <= spots(col)
    for b in range(blocks):
        both = two_heads(q_ref, b)
        if b > 0:
            s_ref[b, : b * QB, :] = dot(k_ref[: b * QB, :], both, ((1,), (1,)))
        s = dot(k_ref[b * QB : (b + 1) * QB, :], both, ((1,), (1,)))
        s_ref[b, b * QB : (b + 1) * QB, :] = jnp.where(keep, s, NEG)
    for b in range(blocks):
        end = (b + 1) * QB
        top = jnp.max(s_ref[b, :end, :], axis=0, keepdims=True)
        p_ref[b, :end, :] = jnp.exp2(s_ref[b, :end, :] - top).astype(jnp.bfloat16)
        top_ref[0, b] = jnp.broadcast_to(top, (8, 2 * QB))
    for b in range(blocks):
        end = (b + 1) * QB
        o = dot(with_sums(v_ref[:, :end]), p_ref[b, :end, :], ((1,), (0,)))
        acc_ref[0, b, :16, :] = o[PAIR:]
        acc_ref[0, b, 16:, :QB] = o[:HEAD_DIM, :QB]
        acc_ref[0, b, 16:, QB:] = o[HEAD_DIM:PAIR, QB:]


def fine_before_kernel(
    where_ref, q_ref, kf_ref, kn_ref, vf_ref, vn_ref, top_ref, acc_ref, out_ref, s_ref, p_ref
):
    half = kf_ref.shape[0]
    blocks = q_ref.shape[0] // QB
    core = where_ref[0]
    row = lax.broadcasted_iota(jnp.int32, (QB, 2 * QB), 0)
    col = lax.broadcasted_iota(jnp.int32, (QB, 2 * QB), 1) % QB
    keep = row > spots(col)

    def store(b, total, o):
        o = o * (1.0 / total)
        mixed = jnp.concatenate([o[:, :QB], o[:, QB:]], axis=0)
        at = b * QB // half
        out_ref[(at + core) % 2, b * QB - at * half : (b + 1) * QB - at * half, :] = mixed.T.astype(jnp.bfloat16)

    @pl.when(where_ref[1] == 0)
    def _():
        for b in range(blocks):
            store(b, acc_ref[0, b, 0:1, :], acc_ref[0, b, 16:, :])

    def units(low, high):
        def spans(b):
            if b * QB < half:
                return [(low, b * QB, half - b * QB), (high, 0, half)]
            return [(high, b * QB - half, 2 * half - b * QB)]

        for b in range(blocks):
            both = two_heads(q_ref, b)
            at = b * QB
            for (k_ref, _), first, size in spans(b):
                if at == b * QB:
                    s = dot(k_ref[first : first + QB, :], both, ((1,), (1,)))
                    s_ref[b, at : at + QB, :] = jnp.where(keep, s, NEG)
                    at, first, size = at + QB, first + QB, size - QB
                if size > 0:
                    s_ref[b, at : at + size, :] = dot(k_ref[first : first + size, :], both, ((1,), (1,)))
                at += size
        fades = []
        for b in range(blocks):
            old = top_ref[0, b, 0:1, :]
            top = jnp.maximum(old, jnp.max(s_ref[b, b * QB :, :], axis=0, keepdims=True))
            p_ref[b, b * QB :, :] = jnp.exp2(s_ref[b, b * QB :, :] - top).astype(jnp.bfloat16)
            fades.append(jnp.exp2(old - top))
        for b in range(blocks):
            v = [v_ref[:, first : first + size] for (_, v_ref), first, size in spans(b)]
            o = dot(with_sums(jnp.concatenate(v, axis=1)), p_ref[b, b * QB :, :], ((1,), (0,)))
            acc = acc_ref[0, b] * fades[b]
            new = jnp.concatenate([o[:HEAD_DIM, :QB], o[HEAD_DIM:PAIR, QB:]], axis=1)
            store(b, acc[0:1] + o[PAIR : PAIR + 1], acc[16:] + new)

    @pl.when((where_ref[1] > 0) & (core == 0))
    def _():
        units((kf_ref, vf_ref), (kn_ref, vn_ref))

    @pl.when((where_ref[1] > 0) & (core == 1))
    def _():
        units((kn_ref, vn_ref), (kf_ref, vf_ref))


def fine_own(q, k, v):
    count, width = q.shape
    blocks = count // QB
    pairs = width // PAIR
    return pl.pallas_call(
        fine_own_kernel,
        name="fine_own",
        grid=(pairs,),
        in_specs=[
            pl.BlockSpec((count, PAIR), lambda i: (0, i)),
            pl.BlockSpec((count, PAIR), lambda i: (0, i)),
            pl.BlockSpec((PAIR, count), lambda i: (i, 0)),
        ],
        out_specs=[
            pl.BlockSpec((1, blocks, 8, 2 * QB), lambda i: (i, 0, 0, 0)),
            pl.BlockSpec((1, blocks, 16 + HEAD_DIM, 2 * QB), lambda i: (i, 0, 0, 0)),
        ],
        out_shape=[
            jax.ShapeDtypeStruct((pairs, blocks, 8, 2 * QB), jnp.float32),
            jax.ShapeDtypeStruct((pairs, blocks, 16 + HEAD_DIM, 2 * QB), jnp.float32),
        ],
        scratch_shapes=[
            pltpu.VMEM((blocks, count, 2 * QB), jnp.float32),
            pltpu.VMEM((blocks, count, 2 * QB), jnp.bfloat16),
        ],
        compiler_params=params(),
        cost_estimate=pl.CostEstimate(flops=5 * 2**30, bytes_accessed=6 * 2**20, transcendentals=5 * 2**20),
    )(q, k, v)


def fine_before(where, q, keys, values, state):
    count, width = q.shape
    blocks = count // QB
    half = count // 2
    return pl.pallas_call(
        fine_before_kernel,
        name="fine_before",
        grid=(width // PAIR,),
        in_specs=[pl.BlockSpec(memory_space=pltpu.SMEM), pl.BlockSpec((count, PAIR), lambda i: (0, i))]
        + [pl.BlockSpec((half, PAIR), lambda i: (0, i))] * 2
        + [pl.BlockSpec((PAIR, half), lambda i: (i, 0))] * 2
        + [
            pl.BlockSpec((1, blocks, 8, 2 * QB), lambda i: (i, 0, 0, 0)),
            pl.BlockSpec((1, blocks, 16 + HEAD_DIM, 2 * QB), lambda i: (i, 0, 0, 0)),
        ],
        out_specs=pl.BlockSpec((2, half, PAIR), lambda i: (0, 0, i)),
        out_shape=jax.ShapeDtypeStruct((2, half, width), jnp.bfloat16),
        scratch_shapes=[
            pltpu.VMEM((blocks, count, 2 * QB), jnp.float32),
            pltpu.VMEM((blocks, count, 2 * QB), jnp.bfloat16),
        ],
        compiler_params=params(),
        cost_estimate=pl.CostEstimate(flops=1, bytes_accessed=1, transcendentals=0),
    )(where, q, *keys, *values, *state)


def pack_kernel(hidden_ref, tail_ref, out_ref):
    blocks, places, groups, width = hidden_ref.shape
    rows = blocks * groups
    half = width // 2
    for j in range(SHORT):
        p = (j + 1) % SHORT
        part = hidden_ref[:, p].reshape(rows, width)
        if p > 0:
            wide = part.astype(jnp.float32)
            tail = tail_ref[p : p + 1, :].astype(jnp.float32)
            first = lax.broadcasted_iota(jnp.int32, wide.shape, 0) == 0
            wide = jnp.where(first, tail, pltpu.roll(wide, 1, 0))
            part = wide.astype(jnp.bfloat16)
        for f in range(2):
            out_ref[(j % 2) * 2 + f, j // 2] = part[:, f * half : (f + 1) * half]


def pack(hidden, tail):
    count, width = hidden.shape
    groups = QB // SHORT
    blocks = count // QB
    return pl.pallas_call(
        pack_kernel,
        name="pack",
        out_shape=jax.ShapeDtypeStruct((4, 4, count // SHORT, width // 2), jnp.bfloat16),
        compiler_params=params(),
    )(hidden.reshape(blocks, SHORT, groups, width), tail)


def shorten_kernel(spots_of, where_ref, grouped_ref, *refs):
    pieces, out_ref = refs[:-1], refs[-1]
    owners, parts, rows, depth = grouped_ref.shape
    total = None
    for (distance, other, first), piece in zip(spots_of, pieces):
        size = piece.shape[0]
        x = (where_ref[0] + parts - distance) % parts
        core = 1 - where_ref[1] if other else where_ref[1]
        columns = pl.ds(pl.multiple_of(core * (depth // 2) + first, 128), size)
        part = grouped_ref[:, x, :, columns].reshape(owners * rows, size)
        term = dot(part, piece[...], ((1,), (0,)))
        total = term if total is None else total + term
    out_ref[...] = total.reshape(owners, rows, -1).astype(jnp.bfloat16)


def shorten(where, grouped, pieces, spots_of):
    owners, parts, rows, depth = grouped.shape
    width = pieces[0].shape[1]
    tile = width // 4
    return pl.pallas_call(
        functools.partial(shorten_kernel, spots_of),
        name="shorten",
        grid=(4,),
        in_specs=[
            pl.BlockSpec(memory_space=pltpu.SMEM),
            pl.BlockSpec(grouped.shape, lambda i: (0, 0, 0, 0)),
        ]
        + [pl.BlockSpec((piece.shape[0], tile), lambda i: (0, i)) for piece in pieces],
        out_specs=pl.BlockSpec((owners, rows, tile), lambda i: (0, 0, i)),
        out_shape=jax.ShapeDtypeStruct((owners, rows, width), jnp.bfloat16),
        compiler_params=params(60),
    )(where, grouped, *pieces)


def coarse_project_kernel(part_ref, q_ref, k_ref, v_ref, short_ref, qkv_ref, norm_ref):
    @pl.when(pl.program_id(0) == 0)
    def _():
        short = jnp.sum(part_ref[...].astype(jnp.float32), axis=0).astype(jnp.bfloat16)
        short_ref[...] = short
        norm_ref[...] = normed(short)

    rows = norm_ref[...]
    for i, (ref, scale) in enumerate(((k_ref, None), (v_ref, None), (q_ref, SCALE))):
        out = dot(rows, ref[...], ((1,), (0,)))
        if scale is not None:
            out = out * scale
        out = out.astype(jnp.bfloat16)
        for h in range(qkv_ref.shape[0]):
            qkv_ref[h, :, i * HEAD_DIM : (i + 1) * HEAD_DIM] = out[:, h * HEAD_DIM : (h + 1) * HEAD_DIM]


def coarse_project(partial, query, key, value):
    owners, rows, width = partial.shape
    tile = 4 * HEAD_DIM
    spec = pl.BlockSpec((width, tile), lambda i: (0, i))
    return pl.pallas_call(
        coarse_project_kernel,
        name="coarse_project",
        grid=(width // tile,),
        in_specs=[pl.BlockSpec(partial.shape, lambda i: (0, 0, 0)), spec, spec, spec],
        out_specs=[
            pl.BlockSpec((rows, width), lambda i: (0, 0)),
            pl.BlockSpec((4, rows, 3 * HEAD_DIM), lambda i: (i, 0, 0)),
        ],
        out_shape=[
            jax.ShapeDtypeStruct((rows, width), jnp.bfloat16),
            jax.ShapeDtypeStruct((HEADS, rows, 3 * HEAD_DIM), jnp.bfloat16),
        ],
        scratch_shapes=[pltpu.VMEM((rows, width), jnp.bfloat16)],
        compiler_params=params(60),
    )(partial, query, key, value)


def finish_kernel(mixed_ref, out_weight_ref, short_ref, hidden_ref, out_ref, rows_ref):
    heads, rows, _ = mixed_ref.shape
    rows = 2 * rows

    @pl.when(pl.program_id(0) == 0)
    def _():
        for h in range(heads):
            m = mixed_ref[h]
            rows_ref[:, h * HEAD_DIM : (h + 1) * HEAD_DIM] = jnp.concatenate(
                [m[:, :HEAD_DIM], m[:, HEAD_DIM:]], axis=0
            )

    refined = short_ref[...].astype(jnp.float32) + dot(rows_ref[...], out_weight_ref[...], ((1,), (0,)))
    tile = refined.shape[1]
    spread = jnp.broadcast_to(refined[:, None, :], (rows, SHORT, tile)).reshape(rows * SHORT, tile)
    out_ref[...] = (hidden_ref[...].astype(jnp.float32) + spread).astype(jnp.bfloat16)


def finish(mixed, out_weight, short, hidden):
    count, width = hidden.shape
    rows = count // SHORT
    tile = width // 4
    return pl.pallas_call(
        finish_kernel,
        name="finish",
        grid=(4,),
        in_specs=[
            pl.BlockSpec(mixed.shape, lambda i: (0, 0, 0)),
            pl.BlockSpec((width, tile), lambda i: (0, i)),
            pl.BlockSpec((rows, tile), lambda i: (0, i)),
            pl.BlockSpec((count, tile), lambda i: (0, i)),
        ],
        out_specs=pl.BlockSpec((count, tile), lambda i: (0, i)),
        out_shape=jax.ShapeDtypeStruct((count, width), jnp.bfloat16),
        scratch_shapes=[pltpu.VMEM((rows, width), jnp.bfloat16)],
        compiler_params=params(60),
    )(mixed, out_weight, short, hidden)


def coarse_kernel(number, first, final, where_ref, q_ref, *refs):
    parts = refs[:number]
    old = None if first else refs[number : number + 2]
    outs = refs[number if first else number + 2 :]
    blocks, rows, _ = parts[0].shape
    tile = 4 * rows
    tiles = blocks // 4
    lane = lax.broadcasted_iota(jnp.int32, (1, tile), 1)
    row = lax.broadcasted_iota(jnp.int32, (tile, tile), 0)
    stride = 8 * rows
    place = (row // rows) * stride + row % rows
    limit = (lane // rows) * stride + where_ref[0] * rows + lane % rows
    ones = jnp.ones((16, number * tile), jnp.bfloat16)
    queries = []
    for t in range(tiles):
        q = q_ref[4 * t : 4 * t + 4, :, 2 * HEAD_DIM :].reshape(tile, HEAD_DIM)
        queries.append(jnp.concatenate([q, jnp.zeros_like(q)], axis=1))
    if first:
        tops = [jnp.full((1, tile), NEG, jnp.float32)] * tiles
        accs = [jnp.zeros((16 + HEAD_DIM, tile), jnp.float32)] * tiles
    else:
        tops = [old[0][t, 0:1, :] for t in range(tiles)]
        accs = [old[1][t] for t in range(tiles)]
    for g in range(tiles):
        kv = jnp.concatenate([part[4 * g : 4 * g + 4].reshape(tile, PAIR) for part in parts], axis=0)
        v = jnp.concatenate([ones, kv.T[HEAD_DIM:, :]], axis=0)
        live = range(g, tiles)
        scores = [dot(kv, queries[t], ((1,), (1,))) for t in live]
        keep = jnp.concatenate(
            [place <= limit - where_ref[1 + i] * rows for i in range(number)], axis=0
        )
        scores[0] = jnp.where(keep, scores[0], NEG)
        news = [jnp.maximum(tops[t], jnp.max(s, axis=0, keepdims=True)) for t, s in zip(live, scores)]
        ps = [jnp.exp2(s - top).astype(jnp.bfloat16) for s, top in zip(scores, news)]
        for t, top, p in zip(live, news, ps):
            accs[t] = accs[t] * jnp.exp2(tops[t] - top) + dot(v, p, ((1,), (0,)))
            tops[t] = top
    for t in range(tiles):
        if final:
            o = accs[t][16:] * (1.0 / accs[t][0:1])
            o = o.T.astype(jnp.bfloat16)
            for i in range(0, tile, rows):
                low, high = o[i : i + rows // 2], o[i + rows // 2 : i + rows]
                outs[0][4 * t + i // rows] = jnp.concatenate([low, high], axis=1)
        else:
            outs[0][t] = jnp.broadcast_to(tops[t], (8, tile))
            outs[1][t] = accs[t]


def coarse_attend(places, q, parts, state, final):
    heads, rows, _ = q.shape
    tile = 4 * rows
    if final:
        out_shape = jax.ShapeDtypeStruct((heads, rows // 2, PAIR), jnp.bfloat16)
    else:
        out_shape = [
            jax.ShapeDtypeStruct((heads // 4, 8, tile), jnp.float32),
            jax.ShapeDtypeStruct((heads // 4, 16 + HEAD_DIM, tile), jnp.float32),
        ]
    first = state is None
    arrays = [q, *parts] + ([] if first else list(state))
    share = len(parts) / 8
    return pl.pallas_call(
        functools.partial(coarse_kernel, len(parts), first, final),
        in_specs=[pl.BlockSpec(memory_space=pltpu.SMEM)]
        + [pl.BlockSpec(memory_space=pltpu.VMEM)] * len(arrays),
        out_shape=out_shape,
        name="coarse_attend",
        compiler_params=params(),
        cost_estimate=pl.CostEstimate(
            flops=int(share * 6 * 2**30), bytes_accessed=2 * 2**20, transcendentals=int(share * 5 * 2**20)
        ),
    )(jnp.stack(places).astype(jnp.int32), *arrays)


def body(
    tokens,
    fine_query,
    fine_key,
    fine_value,
    fine_out,
    short_weight,
    coarse_query,
    coarse_key,
    coarse_value,
    coarse_out,
):
    count, width = tokens.shape
    bf = jnp.bfloat16
    place = lax.axis_index(ALL).astype(jnp.int32)
    core = lax.axis_index("c").astype(jnp.int32)

    def across(block):
        return lax.ppermute(block, "c", [(0, 1), (1, 0)])

    far = from_behind(tokens, 2)
    mate = across(tokens)
    half = width // 2

    def own_heads(weight, axis):
        return lax.dynamic_slice_in_dim(weight, core * half, half, axis)

    query_weight, key_weight, value_weight = (
        own_heads(weight, 1) for weight in (fine_query, fine_key, fine_value)
    )
    weights = [key_weight, value_weight.T]
    out_weight = own_heads(fine_out, 0)
    out_weight_mate = lax.dynamic_slice_in_dim(fine_out, (1 - core) * half, half, 0)
    chip = jnp.concatenate(
        [jnp.where(core == 0, tokens, mate), jnp.where(core == 0, mate, tokens)], axis=0
    )
    keys, values, query = project(chip, [*weights, query_weight])
    state = fine_own(query, keys, values)
    state, short_weight = lax.optimization_barrier((state, short_weight))
    def along_x(block, distance):
        return lax.ppermute(block, "x", [(i, (i + distance) % 4) for i in range(4)])

    behind, ahead = along_x(short_weight, 1), along_x(short_weight, 3)
    far, state, query, out_weight, out_weight_mate = lax.optimization_barrier(
        (far, state, query, out_weight, out_weight_mate)
    )
    near = across(far)
    keys, values = zip(project(far, weights), project(near, weights))
    where = jnp.stack([core, (place > 1).astype(jnp.int32)])
    fine_mixed = fine_before(where, query, keys, values, state)
    fine_mixed, behind, ahead = lax.optimization_barrier((fine_mixed, behind, ahead))
    part = short_weight.shape[0] // 2
    halves = along_x(behind[:part], 1), along_x(ahead[part:], 3)
    theirs = across(fine_mixed[1])
    hidden, natural, tail = out_project(tokens, fine_mixed, theirs, out_weight, out_weight_mate)
    tail, halves = lax.optimization_barrier((tail, halves))
    tail = from_behind(tail, 1)
    pieces = [short_weight, behind, ahead, *halves]
    pieces = pieces + [across(piece) for piece in pieces]
    spots_of = [(d, other, at) for other in (0, 1) for d, at in ((0, 0), (1, 0), (3, 0), (2, 0), (2, part))]
    rows = count // SHORT
    grouped = lax.all_to_all(pack(hidden, tail), "y", 0, 0)
    where = jnp.stack([lax.axis_index("x").astype(jnp.int32), core])
    partial = lax.all_to_all(shorten(where, grouped, pieces, spots_of), "y", 0, 0)
    shortened, qkv = coarse_project(partial, coarse_query, coarse_key, coarse_value)
    qkv = lax.all_to_all(qkv, ("z", "x"), 0, 0)
    kv = qkv[:, :, : 2 * HEAD_DIM]
    y, c = lax.axis_index("y"), lax.axis_index("c")
    mine = y * 2 + c

    def around(block, distance):
        return lax.ppermute(block, "y", [(i, (i + distance) % 4) for i in range(4)])

    def spot(distance, other=0):
        return ((y + distance) % 4) * 2 + (1 - c if other else c)

    mate_kv = across(kv)
    below, above, beyond = around(kv, 1), around(kv, 3), around(kv, 2)
    state = coarse_attend((mine, mine, spot(0, 1)), qkv, (kv, mate_kv), None, False)
    others = (below, above, beyond)
    state, *others = lax.optimization_barrier((state, *others))
    swapped = [across(block) for block in others]
    state = coarse_attend((mine, spot(3), spot(1), spot(2)), qkv, others, state, False)
    state, *swapped = lax.optimization_barrier((state, *swapped))
    mixed = coarse_attend((mine, spot(3, 1), spot(1, 1), spot(2, 1)), qkv, swapped, state, True)
    mixed = lax.all_to_all(mixed, ("z", "x"), 0, 0)
    return finish(mixed, coarse_out, shortened, natural)


def solution(mesh):
    fine = Mesh(mesh.devices.reshape(4, 4, 4, 2), ALL)
    return jax.shard_map(
        body,
        mesh=fine,
        in_specs=(P(ALL, None), P(), P(), P(), P(), P(("x", "y", "c"), None), P(), P(), P(), P()),
        out_specs=P(ALL, None),
        check_vma=False,
    )
```

```python
import functools
import math

import jax
import jax.numpy as jnp
from jax import lax
from jax.experimental import pallas as pl
from jax.experimental.pallas import tpu as pltpu
from jax.sharding import Mesh, PartitionSpec as P

HEAD_DIM = 64
HEADS = 16
SHORT = 8
WIN = 1024
SCALE = math.log2(math.e) / math.sqrt(HEAD_DIM)
ALL = ("z", "x", "y", "c")
QB = 128
PAIR = 2 * HEAD_DIM
NEG = -1e30


def from_behind(block, distance):
    devices = range(128)
    route = [(i - distance, i) for i in devices if i - distance in devices]
    return lax.ppermute(block, ALL, route)


def normed(rows):
    values = rows.astype(jnp.float32)
    scale = lax.rsqrt(jnp.mean(values * values, axis=-1, keepdims=True) + 1e-06)
    return (values * scale).astype(jnp.bfloat16)


def dot(a, b, contract):
    return lax.dot_general(a, b, (contract, ((), ())), preferred_element_type=jnp.float32)


def params(mib=24):
    return pltpu.CompilerParams(vmem_limit_bytes=mib * 2**20)


def spots(index):
    groups = QB // SHORT
    return (index % groups) * SHORT + index // groups


def two_heads(q_ref, b):
    lane = lax.broadcasted_iota(jnp.int32, (QB, PAIR), 1)
    q = q_ref[b * QB : (b + 1) * QB, :]
    zero = jnp.zeros_like(q)
    return jnp.concatenate(
        [jnp.where(lane < HEAD_DIM, q, zero), jnp.where(lane < HEAD_DIM, zero, q)], axis=0
    )


def with_sums(v):
    return jnp.concatenate([v, jnp.ones((16, v.shape[1]), jnp.bfloat16)], axis=0)


def moves(rows, take):
    col = lax.broadcasted_iota(jnp.int32, (rows, QB), 1)
    row = lax.broadcasted_iota(jnp.int32, (rows, QB), 0)
    return jnp.where(take(row) == col, 1.0, 0.0).astype(jnp.bfloat16)


def reorder(move, rows):
    parts = [dot(move, rows[i : i + QB], ((1,), (0,))) for i in range(0, rows.shape[0], QB)]
    return jnp.concatenate(parts, axis=0)


def project_kernel(number, core_ref, rows_ref, *refs):
    weights, outs = refs[:number], refs[number:]
    rows = normed(rows_ref[...])
    if number == 3:
        rows = reorder(moves(QB, spots), rows).astype(jnp.bfloat16)
        outs[2][...] = (dot(rows, weights[2][...], ((1,), (0,))) * SCALE).astype(jnp.bfloat16)
    outs[0][...] = dot(rows, weights[0][...], ((1,), (0,))).astype(jnp.bfloat16)
    outs[1][...] = dot(weights[1][...], rows, ((1,), (1,))).astype(jnp.bfloat16)


def project(core, rows, weights):
    count, width = rows.shape
    half = width // 2
    tile = 512
    by_row = pl.BlockSpec((tile, half), lambda i, c: (i, 0))
    columns = pl.BlockSpec((width, half), lambda i, c: (0, c[0]))
    number = len(weights)
    return pl.pallas_call(
        functools.partial(project_kernel, number),
        name="project",
        grid_spec=pltpu.PrefetchScalarGridSpec(
            num_scalar_prefetch=1,
            grid=(count // tile,),
            in_specs=[pl.BlockSpec((tile, width), lambda i, c: (i, 0))]
            + [columns, pl.BlockSpec((half, width), lambda i, c: (c[0], 0)), columns][:number],
            out_specs=[by_row, pl.BlockSpec((half, tile), lambda i, c: (0, i)), by_row][:number],
        ),
        out_shape=[
            jax.ShapeDtypeStruct((count, half), jnp.bfloat16),
            jax.ShapeDtypeStruct((half, count), jnp.bfloat16),
            jax.ShapeDtypeStruct((count, half), jnp.bfloat16),
        ][:number],
        compiler_params=params(20),
        cost_estimate=pl.CostEstimate(flops=1, bytes_accessed=1, transcendentals=0),
    )(core.reshape(1), *[rows, *weights])


def out_project_kernel(
    core_ref, tokens_ref, mine_ref, theirs_ref, my_ref, their_ref, natural_ref, grouped_ref, tail_ref
):
    total = reorder(moves(QB, spots), tokens_ref[...])
    total = total + dot(mine_ref[0], my_ref[...], ((1,), (0,)))
    total = total + dot(theirs_ref[...], their_ref[...], ((1,), (0,)))
    hidden = total.astype(jnp.bfloat16)
    groups = QB // SHORT
    natural_ref[...] = reorder(moves(QB, lambda r: (r % SHORT) * groups + r // SHORT), hidden).astype(jnp.bfloat16)
    tail = dot(moves(16, lambda r: r * groups + groups - 1), hidden[-QB:], ((1,), (0,)))
    tail_ref[...] = tail.astype(jnp.bfloat16)
    count, tile = hidden.shape
    rows = count // SHORT
    blocks = hidden.reshape(count // QB, SHORT, groups, tile)
    for j in range(SHORT):
        p = (j + 1) % SHORT
        part = blocks[:, p].reshape(rows, tile)
        if p > 0:
            part = pltpu.roll(part.astype(jnp.float32), 1, 0).astype(jnp.bfloat16)
        grouped_ref[j % 2, 0, j // 2] = part


def out_project(core, tokens, mixed, theirs, weight):
    count, width = tokens.shape
    half = width // 2
    rows = count // SHORT
    by_column = pl.BlockSpec((count, half), lambda i, c: (0, i))
    return pl.pallas_call(
        out_project_kernel,
        name="out_project",
        grid_spec=pltpu.PrefetchScalarGridSpec(
            num_scalar_prefetch=1,
            grid=(2,),
            in_specs=[
                by_column,
                pl.BlockSpec((1, count, half), lambda i, c: (0, 0, 0)),
                pl.BlockSpec((count, half), lambda i, c: (0, 0)),
                pl.BlockSpec((half, half), lambda i, c: (c[0], i)),
                pl.BlockSpec((half, half), lambda i, c: (1 - c[0], i)),
            ],
            out_specs=[
                by_column,
                pl.BlockSpec((2, 1, 4, rows, half), lambda i, c: (0, i, 0, 0, 0)),
                pl.BlockSpec((16, half), lambda i, c: (0, i)),
            ],
        ),
        out_shape=[
            jax.ShapeDtypeStruct((count, width), jnp.bfloat16),
            jax.ShapeDtypeStruct((2, 2, 4, rows, half), jnp.bfloat16),
            jax.ShapeDtypeStruct((16, width), jnp.bfloat16),
        ],
        compiler_params=params(20),
    )(core.reshape(1), tokens, mixed, theirs, weight, weight)


def fix_first_kernel(grouped_ref, tail_ref, out_ref):
    half = grouped_ref.shape[-1]
    for j in range(SHORT):
        for f in range(2):
            old = grouped_ref[j % 2, f, j // 2].astype(jnp.float32)
            if j < SHORT - 1:
                row = tail_ref[j + 1 : j + 2, f * half : (f + 1) * half].astype(jnp.float32)
                first = lax.broadcasted_iota(jnp.int32, old.shape, 0) == 0
                old = jnp.where(first, row, old)
            out_ref[j % 2, f, j // 2] = old.astype(jnp.bfloat16)


def fix_first(grouped, tail):
    block = (*grouped.shape[:3], 16, grouped.shape[4])
    spec = pl.BlockSpec(block, lambda i: (0, 0, 0, 0, 0))
    return pl.pallas_call(
        fix_first_kernel,
        name="fix_first",
        grid=(1,),
        in_specs=[spec, pl.BlockSpec(tail.shape, lambda i: (0, 0))],
        out_specs=spec,
        out_shape=jax.ShapeDtypeStruct(grouped.shape, jnp.bfloat16),
        input_output_aliases={0: 0},
        compiler_params=params(20),
    )(grouped, tail)


def fine_own_kernel(q_ref, k_ref, v_ref, top_ref, acc_ref, s_ref, p_ref):
    blocks = q_ref.shape[0] // QB
    row = lax.broadcasted_iota(jnp.int32, (QB, 2 * QB), 0)
    col = lax.broadcasted_iota(jnp.int32, (QB, 2 * QB), 1) % QB
    keep = spots(row) <= spots(col)
    for b in range(blocks):
        both = two_heads(q_ref, b)
        if b > 0:
            s_ref[b, : b * QB, :] = dot(k_ref[: b * QB, :], both, ((1,), (1,)))
        s = dot(k_ref[b * QB : (b + 1) * QB, :], both, ((1,), (1,)))
        s_ref[b, b * QB : (b + 1) * QB, :] = jnp.where(keep, s, NEG)
    for b in range(blocks):
        end = (b + 1) * QB
        top = jnp.max(s_ref[b, :end, :], axis=0, keepdims=True)
        p_ref[b, :end, :] = jnp.exp2(s_ref[b, :end, :] - top).astype(jnp.bfloat16)
        top_ref[0, b] = jnp.broadcast_to(top, (8, 2 * QB))
    for b in range(blocks):
        end = (b + 1) * QB
        o = dot(with_sums(v_ref[:, :end]), p_ref[b, :end, :], ((1,), (0,)))
        acc_ref[0, b, :16, :] = o[PAIR:]
        acc_ref[0, b, 16:, :QB] = o[:HEAD_DIM, :QB]
        acc_ref[0, b, 16:, QB:] = o[HEAD_DIM:PAIR, QB:]


def fine_before_kernel(
    where_ref, q_ref, kf_ref, kn_ref, vf_ref, vn_ref, top_ref, acc_ref, out_ref, s_ref, p_ref
):
    half = kf_ref.shape[0]
    blocks = q_ref.shape[0] // QB
    core = where_ref[0]
    row = lax.broadcasted_iota(jnp.int32, (QB, 2 * QB), 0)
    col = lax.broadcasted_iota(jnp.int32, (QB, 2 * QB), 1) % QB
    keep = row > spots(col)

    def store(b, total, o):
        o = o * (1.0 / total)
        mixed = jnp.concatenate([o[:, :QB], o[:, QB:]], axis=0)
        at = b * QB // half
        out_ref[(at + core) % 2, b * QB - at * half : (b + 1) * QB - at * half, :] = mixed.T.astype(jnp.bfloat16)

    @pl.when(where_ref[1] == 0)
    def _():
        for b in range(blocks):
            store(b, acc_ref[0, b, 0:1, :], acc_ref[0, b, 16:, :])

    def units(low, high):
        def spans(b):
            if b * QB < half:
                return [(low, b * QB, half - b * QB), (high, 0, half)]
            return [(high, b * QB - half, 2 * half - b * QB)]

        for b in range(blocks):
            both = two_heads(q_ref, b)
            at = b * QB
            for (k_ref, _), first, size in spans(b):
                if at == b * QB:
                    s = dot(k_ref[first : first + QB, :], both, ((1,), (1,)))
                    s_ref[b, at : at + QB, :] = jnp.where(keep, s, NEG)
                    at, first, size = at + QB, first + QB, size - QB
                if size > 0:
                    s_ref[b, at : at + size, :] = dot(k_ref[first : first + size, :], both, ((1,), (1,)))
                at += size
        fades = []
        for b in range(blocks):
            old = top_ref[0, b, 0:1, :]
            top = jnp.maximum(old, jnp.max(s_ref[b, b * QB :, :], axis=0, keepdims=True))
            p_ref[b, b * QB :, :] = jnp.exp2(s_ref[b, b * QB :, :] - top).astype(jnp.bfloat16)
            fades.append(jnp.exp2(old - top))
        for b in range(blocks):
            v = [v_ref[:, first : first + size] for (_, v_ref), first, size in spans(b)]
            o = dot(with_sums(jnp.concatenate(v, axis=1)), p_ref[b, b * QB :, :], ((1,), (0,)))
            acc = acc_ref[0, b] * fades[b]
            new = jnp.concatenate([o[:HEAD_DIM, :QB], o[HEAD_DIM:PAIR, QB:]], axis=1)
            store(b, acc[0:1] + o[PAIR : PAIR + 1], acc[16:] + new)

    @pl.when((where_ref[1] > 0) & (core == 0))
    def _():
        units((kf_ref, vf_ref), (kn_ref, vn_ref))

    @pl.when((where_ref[1] > 0) & (core == 1))
    def _():
        units((kn_ref, vn_ref), (kf_ref, vf_ref))


def fine_own(q, k, v):
    count, width = q.shape
    blocks = count // QB
    pairs = width // PAIR
    return pl.pallas_call(
        fine_own_kernel,
        name="fine_own",
        grid=(pairs,),
        in_specs=[
            pl.BlockSpec((count, PAIR), lambda i: (0, i)),
            pl.BlockSpec((count, PAIR), lambda i: (0, i)),
            pl.BlockSpec((PAIR, count), lambda i: (i, 0)),
        ],
        out_specs=[
            pl.BlockSpec((1, blocks, 8, 2 * QB), lambda i: (i, 0, 0, 0)),
            pl.BlockSpec((1, blocks, 16 + HEAD_DIM, 2 * QB), lambda i: (i, 0, 0, 0)),
        ],
        out_shape=[
            jax.ShapeDtypeStruct((pairs, blocks, 8, 2 * QB), jnp.float32),
            jax.ShapeDtypeStruct((pairs, blocks, 16 + HEAD_DIM, 2 * QB), jnp.float32),
        ],
        scratch_shapes=[
            pltpu.VMEM((blocks, count, 2 * QB), jnp.float32),
            pltpu.VMEM((blocks, count, 2 * QB), jnp.bfloat16),
        ],
        compiler_params=params(),
        cost_estimate=pl.CostEstimate(flops=1, bytes_accessed=1, transcendentals=0),
    )(q, k, v)


def fine_before(where, q, keys, values, state):
    count, width = q.shape
    blocks = count // QB
    half = count // 2
    return pl.pallas_call(
        fine_before_kernel,
        name="fine_before",
        grid=(width // PAIR,),
        in_specs=[pl.BlockSpec(memory_space=pltpu.SMEM), pl.BlockSpec((count, PAIR), lambda i: (0, i))]
        + [pl.BlockSpec((half, PAIR), lambda i: (0, i))] * 2
        + [pl.BlockSpec((PAIR, half), lambda i: (i, 0))] * 2
        + [
            pl.BlockSpec((1, blocks, 8, 2 * QB), lambda i: (i, 0, 0, 0)),
            pl.BlockSpec((1, blocks, 16 + HEAD_DIM, 2 * QB), lambda i: (i, 0, 0, 0)),
        ],
        out_specs=pl.BlockSpec((2, half, PAIR), lambda i: (0, 0, i)),
        out_shape=jax.ShapeDtypeStruct((2, half, width), jnp.bfloat16),
        scratch_shapes=[
            pltpu.VMEM((blocks, count, 2 * QB), jnp.float32),
            pltpu.VMEM((blocks, count, 2 * QB), jnp.bfloat16),
        ],
        compiler_params=params(),
        cost_estimate=pl.CostEstimate(flops=1, bytes_accessed=1, transcendentals=0),
    )(where, q, *keys, *values, *state)


def shorten_kernel(spots_of, where_ref, grouped_ref, *refs):
    pieces, out_ref = refs[:-1], refs[-1]
    owners, parts, rows, depth = grouped_ref.shape
    total = None
    for (distance, other, first), piece in zip(spots_of, pieces):
        size = piece.shape[0]
        x = (where_ref[0] + parts - distance) % parts
        core = 1 - where_ref[1] if other else where_ref[1]
        columns = pl.ds(pl.multiple_of(core * (depth // 2) + first, 128), size)
        part = grouped_ref[:, x, :, columns].reshape(owners * rows, size)
        term = dot(part, piece[...], ((1,), (0,)))
        total = term if total is None else total + term
    out_ref[...] = total.reshape(owners, rows, -1).astype(jnp.bfloat16)


def shorten(where, grouped, pieces, spots_of):
    owners, parts, rows, depth = grouped.shape
    width = pieces[0].shape[1]
    tile = width // 2
    return pl.pallas_call(
        functools.partial(shorten_kernel, spots_of),
        name="shorten",
        grid=(2,),
        in_specs=[
            pl.BlockSpec(memory_space=pltpu.SMEM),
            pl.BlockSpec(grouped.shape, lambda i: (0, 0, 0, 0)),
        ]
        + [pl.BlockSpec((piece.shape[0], tile), lambda i: (0, i)) for piece in pieces],
        out_specs=pl.BlockSpec((owners, rows, tile), lambda i: (0, 0, i)),
        out_shape=jax.ShapeDtypeStruct((owners, rows, width), jnp.bfloat16),
        compiler_params=params(60),
    )(where, grouped, *pieces)


def coarse_project_kernel(part_ref, q_ref, k_ref, v_ref, short_ref, qkv_ref, norm_ref):
    @pl.when(pl.program_id(0) == 0)
    def _():
        short = jnp.sum(part_ref[...].astype(jnp.float32), axis=0).astype(jnp.bfloat16)
        short_ref[...] = short
        norm_ref[...] = normed(short)

    rows = norm_ref[...]
    for i, (ref, scale) in enumerate(((k_ref, None), (v_ref, None), (q_ref, SCALE))):
        out = dot(rows, ref[...], ((1,), (0,)))
        if scale is not None:
            out = out * scale
        out = out.astype(jnp.bfloat16)
        for h in range(qkv_ref.shape[0]):
            qkv_ref[h, :, i * HEAD_DIM : (i + 1) * HEAD_DIM] = out[:, h * HEAD_DIM : (h + 1) * HEAD_DIM]


def coarse_project(partial, query, key, value):
    owners, rows, width = partial.shape
    tile = 4 * HEAD_DIM
    spec = pl.BlockSpec((width, tile), lambda i: (0, i))
    return pl.pallas_call(
        coarse_project_kernel,
        name="coarse_project",
        grid=(width // tile,),
        in_specs=[pl.BlockSpec(partial.shape, lambda i: (0, 0, 0)), spec, spec, spec],
        out_specs=[
            pl.BlockSpec((rows, width), lambda i: (0, 0)),
            pl.BlockSpec((4, rows, 3 * HEAD_DIM), lambda i: (i, 0, 0)),
        ],
        out_shape=[
            jax.ShapeDtypeStruct((rows, width), jnp.bfloat16),
            jax.ShapeDtypeStruct((HEADS, rows, 3 * HEAD_DIM), jnp.bfloat16),
        ],
        scratch_shapes=[pltpu.VMEM((rows, width), jnp.bfloat16)],
        compiler_params=params(60),
    )(partial, query, key, value)


def finish_kernel(mixed_ref, out_weight_ref, short_ref, hidden_ref, out_ref, rows_ref):
    heads, rows, _ = mixed_ref.shape
    rows = 2 * rows

    @pl.when(pl.program_id(0) == 0)
    def _():
        for h in range(heads):
            m = mixed_ref[h]
            rows_ref[:, h * HEAD_DIM : (h + 1) * HEAD_DIM] = jnp.concatenate(
                [m[:, :HEAD_DIM], m[:, HEAD_DIM:]], axis=0
            )

    refined = short_ref[...].astype(jnp.float32) + dot(rows_ref[...], out_weight_ref[...], ((1,), (0,)))
    tile = refined.shape[1]
    spread = jnp.broadcast_to(refined[:, None, :], (rows, SHORT, tile)).reshape(rows * SHORT, tile)
    out_ref[...] = (hidden_ref[...].astype(jnp.float32) + spread).astype(jnp.bfloat16)


def finish(mixed, out_weight, short, hidden):
    count, width = hidden.shape
    rows = count // SHORT
    tile = width // 4
    return pl.pallas_call(
        finish_kernel,
        name="finish",
        grid=(4,),
        in_specs=[
            pl.BlockSpec(mixed.shape, lambda i: (0, 0, 0)),
            pl.BlockSpec((width, tile), lambda i: (0, i)),
            pl.BlockSpec((rows, tile), lambda i: (0, i)),
            pl.BlockSpec((count, tile), lambda i: (0, i)),
        ],
        out_specs=pl.BlockSpec((count, tile), lambda i: (0, i)),
        out_shape=jax.ShapeDtypeStruct((count, width), jnp.bfloat16),
        scratch_shapes=[pltpu.VMEM((rows, width), jnp.bfloat16)],
        compiler_params=params(60),
    )(mixed, out_weight, short, hidden)


def coarse_kernel(number, first, final, where_ref, q_ref, *refs):
    parts = refs[:number]
    old = None if first else refs[number : number + 2]
    outs = refs[number if first else number + 2 :]
    blocks, rows, _ = parts[0].shape
    tile = 4 * rows
    tiles = blocks // 4
    lane = lax.broadcasted_iota(jnp.int32, (1, tile), 1)
    row = lax.broadcasted_iota(jnp.int32, (tile, tile), 0)
    stride = 8 * rows
    place = (row // rows) * stride + row % rows
    limit = (lane // rows) * stride + where_ref[0] * rows + lane % rows
    ones = jnp.ones((16, number * tile), jnp.bfloat16)
    queries = []
    for t in range(tiles):
        q = q_ref[4 * t : 4 * t + 4, :, 2 * HEAD_DIM :].reshape(tile, HEAD_DIM)
        queries.append(jnp.concatenate([q, jnp.zeros_like(q)], axis=1))
    if first:
        tops = [jnp.full((1, tile), NEG, jnp.float32)] * tiles
        accs = [jnp.zeros((16 + HEAD_DIM, tile), jnp.float32)] * tiles
    else:
        tops = [old[0][t, 0:1, :] for t in range(tiles)]
        accs = [old[1][t] for t in range(tiles)]
    for g in range(tiles):
        kv = jnp.concatenate([part[4 * g : 4 * g + 4].reshape(tile, PAIR) for part in parts], axis=0)
        v = jnp.concatenate([ones, kv.T[HEAD_DIM:, :]], axis=0)
        live = range(g, tiles)
        scores = [dot(kv, queries[t], ((1,), (1,))) for t in live]
        keep = jnp.concatenate(
            [place <= limit - where_ref[1 + i] * rows for i in range(number)], axis=0
        )
        scores[0] = jnp.where(keep, scores[0], NEG)
        news = [jnp.maximum(tops[t], jnp.max(s, axis=0, keepdims=True)) for t, s in zip(live, scores)]
        ps = [jnp.exp2(s - top).astype(jnp.bfloat16) for s, top in zip(scores, news)]
        for t, top, p in zip(live, news, ps):
            accs[t] = accs[t] * jnp.exp2(tops[t] - top) + dot(v, p, ((1,), (0,)))
            tops[t] = top
    for t in range(tiles):
        if final:
            o = accs[t][16:] * (1.0 / accs[t][0:1])
            o = o.T.astype(jnp.bfloat16)
            for i in range(0, tile, rows):
                low, high = o[i : i + rows // 2], o[i + rows // 2 : i + rows]
                outs[0][4 * t + i // rows] = jnp.concatenate([low, high], axis=1)
        else:
            outs[0][t] = jnp.broadcast_to(tops[t], (8, tile))
            outs[1][t] = accs[t]


def coarse_attend(places, q, parts, state, final):
    heads, rows, _ = q.shape
    tile = 4 * rows
    if final:
        out_shape = jax.ShapeDtypeStruct((heads, rows // 2, PAIR), jnp.bfloat16)
    else:
        out_shape = [
            jax.ShapeDtypeStruct((heads // 4, 8, tile), jnp.float32),
            jax.ShapeDtypeStruct((heads // 4, 16 + HEAD_DIM, tile), jnp.float32),
        ]
    first = state is None
    arrays = [q, *parts] + ([] if first else list(state))
    share = len(parts) / 8
    return pl.pallas_call(
        functools.partial(coarse_kernel, len(parts), first, final),
        in_specs=[pl.BlockSpec(memory_space=pltpu.SMEM)]
        + [pl.BlockSpec(memory_space=pltpu.VMEM)] * len(arrays),
        out_shape=out_shape,
        name="coarse_attend",
        compiler_params=params(),
        cost_estimate=pl.CostEstimate(
            flops=int(share * 6 * 2**30), bytes_accessed=2 * 2**20, transcendentals=int(share * 5 * 2**20)
        ),
    )(jnp.stack(places).astype(jnp.int32), *arrays)


def body(
    tokens,
    fine_query,
    fine_key,
    fine_value,
    fine_out,
    short_weight,
    coarse_query,
    coarse_key,
    coarse_value,
    coarse_out,
):
    count, width = tokens.shape
    bf = jnp.bfloat16
    place = lax.axis_index(ALL).astype(jnp.int32)
    core = lax.axis_index("c").astype(jnp.int32)

    def across(block):
        return lax.ppermute(block, "c", [(0, 1), (1, 0)])

    far = from_behind(tokens, 2)
    mate = across(tokens)
    weights = [fine_key, fine_value.T]
    chip = jnp.concatenate(
        [jnp.where(core == 0, tokens, mate), jnp.where(core == 0, mate, tokens)], axis=0
    )

    def from_ahead(block):
        return lax.ppermute(block, "x", [(i, (i + 3) % 4) for i in range(4)])

    together = lax.optimization_barrier
    pieces = [short_weight, from_ahead(short_weight)]
    keys, values, query = project(core, chip, [*weights, fine_query])
    keys, pieces[1] = together((keys, pieces[1]))
    pieces.append(from_ahead(pieces[1]))
    state = fine_own(query, keys, values)
    far, state, query, pieces[2] = together((far, state, query, pieces[2]))
    pieces.append(from_ahead(pieces[2]))
    near = across(far)
    far_keys, far_values = project(core, far, weights)
    near_keys, near_values = project(core, near, weights)
    where = jnp.stack([core, (place > 1).astype(jnp.int32)])
    fine_mixed = fine_before(where, query, (far_keys, near_keys), (far_values, near_values), state)
    fine_mixed, pieces[3] = together((fine_mixed, pieces[3]))
    theirs = across(fine_mixed[1])
    natural, grouped, tail = out_project(core, tokens, fine_mixed, theirs, fine_out)
    tail = from_behind(tail, 1)
    grouped = fix_first(grouped, tail).reshape(4, 4, count // SHORT, width // 2)
    grouped = lax.all_to_all(grouped, "y", 0, 0)
    pieces = pieces + [across(piece) for piece in pieces]
    spots_of = [(-d % 4, other, 0) for other in (0, 1) for d in range(4)]
    where = jnp.stack([lax.axis_index("x").astype(jnp.int32), core])
    partial = lax.all_to_all(shorten(where, grouped, pieces, spots_of), "y", 0, 0)
    shortened, qkv = coarse_project(partial, coarse_query, coarse_key, coarse_value)
    qkv = lax.all_to_all(qkv, ("z", "x"), 0, 0)
    kv = qkv[:, :, : 2 * HEAD_DIM]
    y, c = lax.axis_index("y"), lax.axis_index("c")
    mine = y * 2 + c

    def around(block, distance):
        return lax.ppermute(block, "y", [(i, (i + distance) % 4) for i in range(4)])

    def spot(distance, other=0):
        return ((y + distance) % 4) * 2 + (1 - c if other else c)

    mate_kv = across(kv)
    below, above, beyond = around(kv, 1), around(kv, 3), around(kv, 2)
    state = coarse_attend((mine, mine, spot(0, 1)), qkv, (kv, mate_kv), None, False)
    others = (below, above, beyond)
    state, *others = lax.optimization_barrier((state, *others))
    swapped = [across(block) for block in others]
    state = coarse_attend((mine, spot(3), spot(1), spot(2)), qkv, others, state, False)
    state, *swapped = lax.optimization_barrier((state, *swapped))
    mixed = coarse_attend((mine, spot(3, 1), spot(1, 1), spot(2, 1)), qkv, swapped, state, True)
    mixed = lax.all_to_all(mixed, ("z", "x"), 0, 0)
    return finish(mixed, coarse_out, shortened, natural)


def solution(mesh):
    fine = Mesh(mesh.devices.reshape(4, 4, 4, 2), ALL)
    return jax.shard_map(
        body,
        mesh=fine,
        in_specs=(P(ALL, None), P(), P(), P(), P(), P(("x", "y", "c"), None), P(), P(), P(), P()),
        out_specs=P(ALL, None),
        check_vma=False,
    )
```

```python
import functools
import math

import jax
import jax.numpy as jnp
from jax import lax
from jax.experimental import pallas as pl
from jax.experimental.pallas import tpu as pltpu
from jax.sharding import Mesh, PartitionSpec as P

HEAD_DIM = 64
HEADS = 16
SHORT = 8
WIN = 1024
SCALE = math.log2(math.e) / math.sqrt(HEAD_DIM)
ALL = ("z", "x", "y", "c")
QB = 128
PAIR = 2 * HEAD_DIM
NEG = -1e30


def from_behind(block, distance):
    devices = range(128)
    route = [(i - distance, i) for i in devices if i - distance in devices]
    return lax.ppermute(block, ALL, route)


def normed(rows):
    values = rows.astype(jnp.float32)
    scale = lax.rsqrt(jnp.mean(values * values, axis=-1, keepdims=True) + 1e-06)
    return (values * scale).astype(jnp.bfloat16)


def dot(a, b, contract):
    return lax.dot_general(a, b, (contract, ((), ())), preferred_element_type=jnp.float32)


def params(mib=24):
    return pltpu.CompilerParams(vmem_limit_bytes=mib * 2**20)


def spots(index):
    groups = QB // SHORT
    return (index % groups) * SHORT + index // groups


def two_heads(q_ref, b):
    lane = lax.broadcasted_iota(jnp.int32, (QB, PAIR), 1)
    q = q_ref[b * QB : (b + 1) * QB, :]
    zero = jnp.zeros_like(q)
    return jnp.concatenate(
        [jnp.where(lane < HEAD_DIM, q, zero), jnp.where(lane < HEAD_DIM, zero, q)], axis=0
    )


def with_sums(v):
    return jnp.concatenate([v, jnp.ones((16, v.shape[1]), jnp.bfloat16)], axis=0)


def moves(rows, take):
    col = lax.broadcasted_iota(jnp.int32, (rows, QB), 1)
    row = lax.broadcasted_iota(jnp.int32, (rows, QB), 0)
    return jnp.where(take(row) == col, 1.0, 0.0).astype(jnp.bfloat16)


def reorder(move, rows):
    parts = [dot(move, rows[i : i + QB], ((1,), (0,))) for i in range(0, rows.shape[0], QB)]
    return jnp.concatenate(parts, axis=0)


def project_kernel(number, core_ref, rows_ref, *refs):
    weights, outs = refs[:number], refs[number:]
    rows = normed(rows_ref[...])
    if number == 3:
        rows = reorder(moves(QB, spots), rows).astype(jnp.bfloat16)
        outs[2][...] = (dot(rows, weights[2][...], ((1,), (0,))) * SCALE).astype(jnp.bfloat16)
    outs[0][...] = dot(rows, weights[0][...], ((1,), (0,))).astype(jnp.bfloat16)
    outs[1][...] = dot(weights[1][...], rows, ((1,), (1,))).astype(jnp.bfloat16)


def project(core, rows, weights):
    count, width = rows.shape
    half = width // 2
    tile = 512
    by_row = pl.BlockSpec((tile, half), lambda i, c: (i, 0))
    columns = pl.BlockSpec((width, half), lambda i, c: (0, c[0]))
    number = len(weights)
    return pl.pallas_call(
        functools.partial(project_kernel, number),
        name="project",
        grid_spec=pltpu.PrefetchScalarGridSpec(
            num_scalar_prefetch=1,
            grid=(count // tile,),
            in_specs=[pl.BlockSpec((tile, width), lambda i, c: (i, 0))]
            + [columns, pl.BlockSpec((half, width), lambda i, c: (c[0], 0)), columns][:number],
            out_specs=[by_row, pl.BlockSpec((half, tile), lambda i, c: (0, i)), by_row][:number],
        ),
        out_shape=[
            jax.ShapeDtypeStruct((count, half), jnp.bfloat16),
            jax.ShapeDtypeStruct((half, count), jnp.bfloat16),
            jax.ShapeDtypeStruct((count, half), jnp.bfloat16),
        ][:number],
        compiler_params=params(20),
        cost_estimate=pl.CostEstimate(flops=1, bytes_accessed=1, transcendentals=0),
    )(core.reshape(1), *[rows, *weights])


def tail_project_kernel(core_ref, tokens_ref, mine_ref, theirs_ref, my_ref, their_ref, tail_ref):
    groups = QB // SHORT
    total = dot(moves(16, lambda r: r + QB - SHORT), tokens_ref[...], ((1,), (0,)))
    take = moves(16, lambda r: r * groups + groups - 1)
    mine = dot(take, mine_ref[0], ((1,), (0,))).astype(jnp.bfloat16)
    theirs = dot(take, theirs_ref[...], ((1,), (0,))).astype(jnp.bfloat16)
    total = total + dot(mine, my_ref[...], ((1,), (0,))) + dot(theirs, their_ref[...], ((1,), (0,)))
    tail_ref[...] = total.astype(jnp.bfloat16)


def tail_project(core, tokens, mixed, theirs, weight):
    count, width = tokens.shape
    half = width // 2
    last = count // QB - 1
    tile = width // 2
    return pl.pallas_call(
        tail_project_kernel,
        name="tail_project",
        grid_spec=pltpu.PrefetchScalarGridSpec(
            num_scalar_prefetch=1,
            grid=(2,),
            in_specs=[
                pl.BlockSpec((QB, tile), lambda i, c: (last, i)),
                pl.BlockSpec((1, QB, half), lambda i, c: (0, last, 0)),
                pl.BlockSpec((QB, half), lambda i, c: (last, 0)),
                pl.BlockSpec((half, tile), lambda i, c: (c[0], i)),
                pl.BlockSpec((half, tile), lambda i, c: (1 - c[0], i)),
            ],
            out_specs=pl.BlockSpec((16, tile), lambda i, c: (0, i)),
        ),
        out_shape=jax.ShapeDtypeStruct((16, width), jnp.bfloat16),
        compiler_params=params(20),
    )(core.reshape(1), tokens, mixed, theirs, weight, weight)


def out_project_kernel(core_ref, tokens_ref, mine_ref, theirs_ref, my_ref, their_ref, hidden_ref, natural_ref):
    total = reorder(moves(QB, spots), tokens_ref[...])
    total = total + dot(mine_ref[0], my_ref[...], ((1,), (0,)))
    total = total + dot(theirs_ref[...], their_ref[...], ((1,), (0,)))
    hidden = total.astype(jnp.bfloat16)
    hidden_ref[...] = hidden
    groups = QB // SHORT
    natural_ref[...] = reorder(moves(QB, lambda r: (r % SHORT) * groups + r // SHORT), hidden).astype(jnp.bfloat16)


def out_project(core, tokens, mixed, theirs, weight):
    count, width = tokens.shape
    half = width // 2
    by_column = pl.BlockSpec((count, half), lambda i, c: (0, i))
    return pl.pallas_call(
        out_project_kernel,
        name="out_project",
        grid_spec=pltpu.PrefetchScalarGridSpec(
            num_scalar_prefetch=1,
            grid=(2,),
            in_specs=[
                by_column,
                pl.BlockSpec((1, count, half), lambda i, c: (0, 0, 0)),
                pl.BlockSpec((count, half), lambda i, c: (0, 0)),
                pl.BlockSpec((half, half), lambda i, c: (c[0], i)),
                pl.BlockSpec((half, half), lambda i, c: (1 - c[0], i)),
            ],
            out_specs=[by_column, by_column],
        ),
        out_shape=[jax.ShapeDtypeStruct((count, width), jnp.bfloat16)] * 2,
        compiler_params=params(20),
    )(core.reshape(1), tokens, mixed, theirs, weight, weight)


def pack_kernel(hidden_ref, tail_ref, out_ref):
    blocks, places, groups, width = hidden_ref.shape
    rows = blocks * groups
    half = width // 2
    for j in range(SHORT):
        p = (j + 1) % SHORT
        part = hidden_ref[:, p].reshape(rows, width)
        if p > 0:
            wide = part.astype(jnp.float32)
            tail = tail_ref[p : p + 1, :].astype(jnp.float32)
            first = lax.broadcasted_iota(jnp.int32, wide.shape, 0) == 0
            wide = jnp.where(first, tail, pltpu.roll(wide, 1, 0))
            part = wide.astype(jnp.bfloat16)
        for f in range(2):
            out_ref[(j % 2) * 2 + f, j // 2] = part[:, f * half : (f + 1) * half]


def pack(hidden, tail):
    count, width = hidden.shape
    groups = QB // SHORT
    blocks = count // QB
    return pl.pallas_call(
        pack_kernel,
        name="pack",
        out_shape=jax.ShapeDtypeStruct((4, 4, count // SHORT, width // 2), jnp.bfloat16),
        compiler_params=params(),
    )(hidden.reshape(blocks, SHORT, groups, width), tail)


def fine_own_kernel(q_ref, k_ref, v_ref, top_ref, acc_ref, s_ref, p_ref):
    blocks = q_ref.shape[0] // QB
    row = lax.broadcasted_iota(jnp.int32, (QB, 2 * QB), 0)
    col = lax.broadcasted_iota(jnp.int32, (QB, 2 * QB), 1) % QB
    keep = spots(row) <= spots(col)
    for b in range(blocks):
        both = two_heads(q_ref, b)
        if b > 0:
            s_ref[b, : b * QB, :] = dot(k_ref[: b * QB, :], both, ((1,), (1,)))
        s = dot(k_ref[b * QB : (b + 1) * QB, :], both, ((1,), (1,)))
        s_ref[b, b * QB : (b + 1) * QB, :] = jnp.where(keep, s, NEG)
    for b in range(blocks):
        end = (b + 1) * QB
        top = jnp.max(s_ref[b, :end, :], axis=0, keepdims=True)
        p_ref[b, :end, :] = jnp.exp2(s_ref[b, :end, :] - top).astype(jnp.bfloat16)
        top_ref[0, b] = jnp.broadcast_to(top, (8, 2 * QB))
    for b in range(blocks):
        end = (b + 1) * QB
        o = dot(with_sums(v_ref[:, :end]), p_ref[b, :end, :], ((1,), (0,)))
        acc_ref[0, b, :16, :] = o[PAIR:]
        acc_ref[0, b, 16:, :QB] = o[:HEAD_DIM, :QB]
        acc_ref[0, b, 16:, QB:] = o[HEAD_DIM:PAIR, QB:]


def fine_before_kernel(
    where_ref, q_ref, kf_ref, kn_ref, vf_ref, vn_ref, top_ref, acc_ref, out_ref, s_ref, p_ref
):
    half = kf_ref.shape[0]
    blocks = q_ref.shape[0] // QB
    core = where_ref[0]
    row = lax.broadcasted_iota(jnp.int32, (QB, 2 * QB), 0)
    col = lax.broadcasted_iota(jnp.int32, (QB, 2 * QB), 1) % QB
    keep = row > spots(col)

    def store(b, total, o):
        o = o * (1.0 / total)
        mixed = jnp.concatenate([o[:, :QB], o[:, QB:]], axis=0)
        at = b * QB // half
        out_ref[(at + core) % 2, b * QB - at * half : (b + 1) * QB - at * half, :] = mixed.T.astype(jnp.bfloat16)

    @pl.when(where_ref[1] == 0)
    def _():
        for b in range(blocks):
            store(b, acc_ref[0, b, 0:1, :], acc_ref[0, b, 16:, :])

    def units(low, high):
        def spans(b):
            if b * QB < half:
                return [(low, b * QB, half - b * QB), (high, 0, half)]
            return [(high, b * QB - half, 2 * half - b * QB)]

        for b in range(blocks):
            both = two_heads(q_ref, b)
            at = b * QB
            for (k_ref, _), first, size in spans(b):
                if at == b * QB:
                    s = dot(k_ref[first : first + QB, :], both, ((1,), (1,)))
                    s_ref[b, at : at + QB, :] = jnp.where(keep, s, NEG)
                    at, first, size = at + QB, first + QB, size - QB
                if size > 0:
                    s_ref[b, at : at + size, :] = dot(k_ref[first : first + size, :], both, ((1,), (1,)))
                at += size
        fades = []
        for b in range(blocks):
            old = top_ref[0, b, 0:1, :]
            top = jnp.maximum(old, jnp.max(s_ref[b, b * QB :, :], axis=0, keepdims=True))
            p_ref[b, b * QB :, :] = jnp.exp2(s_ref[b, b * QB :, :] - top).astype(jnp.bfloat16)
            fades.append(jnp.exp2(old - top))
        for b in range(blocks):
            v = [v_ref[:, first : first + size] for (_, v_ref), first, size in spans(b)]
            o = dot(with_sums(jnp.concatenate(v, axis=1)), p_ref[b, b * QB :, :], ((1,), (0,)))
            acc = acc_ref[0, b] * fades[b]
            new = jnp.concatenate([o[:HEAD_DIM, :QB], o[HEAD_DIM:PAIR, QB:]], axis=1)
            store(b, acc[0:1] + o[PAIR : PAIR + 1], acc[16:] + new)

    @pl.when((where_ref[1] > 0) & (core == 0))
    def _():
        units((kf_ref, vf_ref), (kn_ref, vn_ref))

    @pl.when((where_ref[1] > 0) & (core == 1))
    def _():
        units((kn_ref, vn_ref), (kf_ref, vf_ref))


def fine_own(q, k, v):
    count, width = q.shape
    blocks = count // QB
    pairs = width // PAIR
    return pl.pallas_call(
        fine_own_kernel,
        name="fine_own",
        grid=(pairs,),
        in_specs=[
            pl.BlockSpec((count, PAIR), lambda i: (0, i)),
            pl.BlockSpec((count, PAIR), lambda i: (0, i)),
            pl.BlockSpec((PAIR, count), lambda i: (i, 0)),
        ],
        out_specs=[
            pl.BlockSpec((1, blocks, 8, 2 * QB), lambda i: (i, 0, 0, 0)),
            pl.BlockSpec((1, blocks, 16 + HEAD_DIM, 2 * QB), lambda i: (i, 0, 0, 0)),
        ],
        out_shape=[
            jax.ShapeDtypeStruct((pairs, blocks, 8, 2 * QB), jnp.float32),
            jax.ShapeDtypeStruct((pairs, blocks, 16 + HEAD_DIM, 2 * QB), jnp.float32),
        ],
        scratch_shapes=[
            pltpu.VMEM((blocks, count, 2 * QB), jnp.float32),
            pltpu.VMEM((blocks, count, 2 * QB), jnp.bfloat16),
        ],
        compiler_params=params(),
        cost_estimate=pl.CostEstimate(flops=1, bytes_accessed=1, transcendentals=0),
    )(q, k, v)


def fine_before(where, q, keys, values, state):
    count, width = q.shape
    blocks = count // QB
    half = count // 2
    return pl.pallas_call(
        fine_before_kernel,
        name="fine_before",
        grid=(width // PAIR,),
        in_specs=[pl.BlockSpec(memory_space=pltpu.SMEM), pl.BlockSpec((count, PAIR), lambda i: (0, i))]
        + [pl.BlockSpec((half, PAIR), lambda i: (0, i))] * 2
        + [pl.BlockSpec((PAIR, half), lambda i: (i, 0))] * 2
        + [
            pl.BlockSpec((1, blocks, 8, 2 * QB), lambda i: (i, 0, 0, 0)),
            pl.BlockSpec((1, blocks, 16 + HEAD_DIM, 2 * QB), lambda i: (i, 0, 0, 0)),
        ],
        out_specs=pl.BlockSpec((2, half, PAIR), lambda i: (0, 0, i)),
        out_shape=jax.ShapeDtypeStruct((2, half, width), jnp.bfloat16),
        scratch_shapes=[
            pltpu.VMEM((blocks, count, 2 * QB), jnp.float32),
            pltpu.VMEM((blocks, count, 2 * QB), jnp.bfloat16),
        ],
        compiler_params=params(),
        cost_estimate=pl.CostEstimate(flops=1, bytes_accessed=1, transcendentals=0),
    )(where, q, *keys, *values, *state)


def shorten_kernel(spots_of, where_ref, grouped_ref, *refs):
    pieces, out_ref = refs[:-1], refs[-1]
    owners, parts, rows, depth = grouped_ref.shape
    total = None
    for (distance, other, first), piece in zip(spots_of, pieces):
        size = piece.shape[0]
        x = (where_ref[0] + parts - distance) % parts
        core = 1 - where_ref[1] if other else where_ref[1]
        columns = pl.ds(pl.multiple_of(core * (depth // 2) + first, 128), size)
        part = grouped_ref[:, x, :, columns].reshape(owners * rows, size)
        term = dot(part, piece[...], ((1,), (0,)))
        total = term if total is None else total + term
    out_ref[...] = total.reshape(owners, rows, -1).astype(jnp.bfloat16)


def shorten(where, grouped, pieces, spots_of):
    owners, parts, rows, depth = grouped.shape
    width = pieces[0].shape[1]
    tile = width // 2
    return pl.pallas_call(
        functools.partial(shorten_kernel, spots_of),
        name="shorten",
        grid=(2,),
        in_specs=[
            pl.BlockSpec(memory_space=pltpu.SMEM),
            pl.BlockSpec(grouped.shape, lambda i: (0, 0, 0, 0)),
        ]
        + [pl.BlockSpec((piece.shape[0], tile), lambda i: (0, i)) for piece in pieces],
        out_specs=pl.BlockSpec((owners, rows, tile), lambda i: (0, 0, i)),
        out_shape=jax.ShapeDtypeStruct((owners, rows, width), jnp.bfloat16),
        compiler_params=params(60),
    )(where, grouped, *pieces)


def coarse_project_kernel(part_ref, q_ref, k_ref, v_ref, short_ref, qkv_ref, norm_ref):
    @pl.when(pl.program_id(0) == 0)
    def _():
        short = jnp.sum(part_ref[...].astype(jnp.float32), axis=0).astype(jnp.bfloat16)
        short_ref[...] = short
        norm_ref[...] = normed(short)

    rows = norm_ref[...]
    for i, (ref, scale) in enumerate(((k_ref, None), (v_ref, None), (q_ref, SCALE))):
        out = dot(rows, ref[...], ((1,), (0,)))
        if scale is not None:
            out = out * scale
        out = out.astype(jnp.bfloat16)
        for h in range(qkv_ref.shape[0]):
            qkv_ref[h, :, i * HEAD_DIM : (i + 1) * HEAD_DIM] = out[:, h * HEAD_DIM : (h + 1) * HEAD_DIM]


def coarse_project(partial, query, key, value):
    owners, rows, width = partial.shape
    tile = 4 * HEAD_DIM
    spec = pl.BlockSpec((width, tile), lambda i: (0, i))
    return pl.pallas_call(
        coarse_project_kernel,
        name="coarse_project",
        grid=(width // tile,),
        in_specs=[pl.BlockSpec(partial.shape, lambda i: (0, 0, 0)), spec, spec, spec],
        out_specs=[
            pl.BlockSpec((rows, width), lambda i: (0, 0)),
            pl.BlockSpec((4, rows, 3 * HEAD_DIM), lambda i: (i, 0, 0)),
        ],
        out_shape=[
            jax.ShapeDtypeStruct((rows, width), jnp.bfloat16),
            jax.ShapeDtypeStruct((HEADS, rows, 3 * HEAD_DIM), jnp.bfloat16),
        ],
        scratch_shapes=[pltpu.VMEM((rows, width), jnp.bfloat16)],
        compiler_params=params(60),
    )(partial, query, key, value)


def finish_kernel(mixed_ref, out_weight_ref, short_ref, hidden_ref, out_ref, rows_ref):
    heads, rows, _ = mixed_ref.shape
    rows = 2 * rows

    @pl.when(pl.program_id(0) == 0)
    def _():
        for h in range(heads):
            m = mixed_ref[h]
            rows_ref[:, h * HEAD_DIM : (h + 1) * HEAD_DIM] = jnp.concatenate(
                [m[:, :HEAD_DIM], m[:, HEAD_DIM:]], axis=0
            )

    refined = short_ref[...].astype(jnp.float32) + dot(rows_ref[...], out_weight_ref[...], ((1,), (0,)))
    tile = refined.shape[1]
    spread = jnp.broadcast_to(refined[:, None, :], (rows, SHORT, tile)).reshape(rows * SHORT, tile)
    out_ref[...] = (hidden_ref[...].astype(jnp.float32) + spread).astype(jnp.bfloat16)


def finish(mixed, out_weight, short, hidden):
    count, width = hidden.shape
    rows = count // SHORT
    tile = width // 4
    return pl.pallas_call(
        finish_kernel,
        name="finish",
        grid=(4,),
        in_specs=[
            pl.BlockSpec(mixed.shape, lambda i: (0, 0, 0)),
            pl.BlockSpec((width, tile), lambda i: (0, i)),
            pl.BlockSpec((rows, tile), lambda i: (0, i)),
            pl.BlockSpec((count, tile), lambda i: (0, i)),
        ],
        out_specs=pl.BlockSpec((count, tile), lambda i: (0, i)),
        out_shape=jax.ShapeDtypeStruct((count, width), jnp.bfloat16),
        scratch_shapes=[pltpu.VMEM((rows, width), jnp.bfloat16)],
        compiler_params=params(60),
    )(mixed, out_weight, short, hidden)


def coarse_kernel(number, first, final, where_ref, q_ref, *refs):
    parts = refs[:number]
    old = None if first else refs[number : number + 2]
    outs = refs[number if first else number + 2 :]
    blocks, rows, _ = parts[0].shape
    tile = 4 * rows
    tiles = blocks // 4
    lane = lax.broadcasted_iota(jnp.int32, (1, tile), 1)
    row = lax.broadcasted_iota(jnp.int32, (tile, tile), 0)
    stride = 8 * rows
    place = (row // rows) * stride + row % rows
    limit = (lane // rows) * stride + where_ref[0] * rows + lane % rows
    ones = jnp.ones((16, number * tile), jnp.bfloat16)
    queries = []
    for t in range(tiles):
        q = q_ref[4 * t : 4 * t + 4, :, 2 * HEAD_DIM :].reshape(tile, HEAD_DIM)
        queries.append(jnp.concatenate([q, jnp.zeros_like(q)], axis=1))
    if first:
        tops = [jnp.full((1, tile), NEG, jnp.float32)] * tiles
        accs = [jnp.zeros((16 + HEAD_DIM, tile), jnp.float32)] * tiles
    else:
        tops = [old[0][t, 0:1, :] for t in range(tiles)]
        accs = [old[1][t] for t in range(tiles)]
    for g in range(tiles):
        kv = jnp.concatenate([part[4 * g : 4 * g + 4].reshape(tile, PAIR) for part in parts], axis=0)
        v = jnp.concatenate([ones, kv.T[HEAD_DIM:, :]], axis=0)
        live = range(g, tiles)
        scores = [dot(kv, queries[t], ((1,), (1,))) for t in live]
        keep = jnp.concatenate(
            [place <= limit - where_ref[1 + i] * rows for i in range(number)], axis=0
        )
        scores[0] = jnp.where(keep, scores[0], NEG)
        news = [jnp.maximum(tops[t], jnp.max(s, axis=0, keepdims=True)) for t, s in zip(live, scores)]
        ps = [jnp.exp2(s - top).astype(jnp.bfloat16) for s, top in zip(scores, news)]
        for t, top, p in zip(live, news, ps):
            accs[t] = accs[t] * jnp.exp2(tops[t] - top) + dot(v, p, ((1,), (0,)))
            tops[t] = top
    for t in range(tiles):
        if final:
            o = accs[t][16:] * (1.0 / accs[t][0:1])
            o = o.T.astype(jnp.bfloat16)
            for i in range(0, tile, rows):
                low, high = o[i : i + rows // 2], o[i + rows // 2 : i + rows]
                outs[0][4 * t + i // rows] = jnp.concatenate([low, high], axis=1)
        else:
            outs[0][t] = jnp.broadcast_to(tops[t], (8, tile))
            outs[1][t] = accs[t]


def coarse_attend(places, q, parts, state, final):
    heads, rows, _ = q.shape
    tile = 4 * rows
    if final:
        out_shape = jax.ShapeDtypeStruct((heads, rows // 2, PAIR), jnp.bfloat16)
    else:
        out_shape = [
            jax.ShapeDtypeStruct((heads // 4, 8, tile), jnp.float32),
            jax.ShapeDtypeStruct((heads // 4, 16 + HEAD_DIM, tile), jnp.float32),
        ]
    first = state is None
    arrays = [q, *parts] + ([] if first else list(state))
    share = len(parts) / 8
    return pl.pallas_call(
        functools.partial(coarse_kernel, len(parts), first, final),
        in_specs=[pl.BlockSpec(memory_space=pltpu.SMEM)]
        + [pl.BlockSpec(memory_space=pltpu.VMEM)] * len(arrays),
        out_shape=out_shape,
        name="coarse_attend",
        compiler_params=params(),
        cost_estimate=pl.CostEstimate(
            flops=int(share * 6 * 2**30), bytes_accessed=2 * 2**20, transcendentals=int(share * 5 * 2**20)
        ),
    )(jnp.stack(places).astype(jnp.int32), *arrays)


def body(
    tokens,
    fine_query,
    fine_key,
    fine_value,
    fine_out,
    short_weight,
    coarse_query,
    coarse_key,
    coarse_value,
    coarse_out,
):
    count, width = tokens.shape
    bf = jnp.bfloat16
    place = lax.axis_index(ALL).astype(jnp.int32)
    core = lax.axis_index("c").astype(jnp.int32)

    def across(block):
        return lax.ppermute(block, "c", [(0, 1), (1, 0)])

    far = from_behind(tokens, 2)
    mate = across(tokens)
    weights = [fine_key, fine_value.T]
    chip = jnp.concatenate(
        [jnp.where(core == 0, tokens, mate), jnp.where(core == 0, mate, tokens)], axis=0
    )

    def along_x(block, distance):
        return lax.ppermute(block, "x", [(i, (i + distance) % 4) for i in range(4)])

    together = lax.optimization_barrier
    keys, values, query = project(core, chip, [*weights, fine_query])
    state = fine_own(query, keys, values)
    far, state, query, short_weight = together((far, state, query, short_weight))
    near = across(far)
    behind, ahead = along_x(short_weight, 1), along_x(short_weight, 3)
    far_keys, far_values = project(core, far, weights)
    near_keys, near_values = project(core, near, weights)
    where = jnp.stack([core, (place > 1).astype(jnp.int32)])
    fine_mixed = fine_before(where, query, (far_keys, near_keys), (far_values, near_values), state)
    fine_mixed, behind, ahead = together((fine_mixed, behind, ahead))
    two_away = along_x(ahead, 3)
    theirs = across(fine_mixed[1])
    tail = from_behind(tail_project(core, tokens, fine_mixed, theirs, fine_out), 1)
    hidden, natural = out_project(core, tokens, fine_mixed, theirs, fine_out)
    grouped, two_away = together((pack(hidden, tail), two_away))
    grouped = lax.all_to_all(grouped, "y", 0, 0)
    pieces = [short_weight, behind, two_away, ahead]
    pieces = pieces + [across(piece) for piece in pieces]
    spots_of = [(distance, other, 0) for other in (0, 1) for distance in range(4)]
    where = jnp.stack([lax.axis_index("x").astype(jnp.int32), core])
    partial = lax.all_to_all(shorten(where, grouped, pieces, spots_of), "y", 0, 0)
    shortened, qkv = coarse_project(partial, coarse_query, coarse_key, coarse_value)
    qkv = lax.all_to_all(qkv, ("z", "x"), 0, 0)
    kv = qkv[:, :, : 2 * HEAD_DIM]
    y, c = lax.axis_index("y"), lax.axis_index("c")
    mine = y * 2 + c

    def around(block, distance):
        return lax.ppermute(block, "y", [(i, (i + distance) % 4) for i in range(4)])

    def spot(distance, other=0):
        return ((y + distance) % 4) * 2 + (1 - c if other else c)

    mate_kv = across(kv)
    below, above, beyond = around(kv, 1), around(kv, 3), around(kv, 2)
    state = coarse_attend((mine, mine, spot(0, 1)), qkv, (kv, mate_kv), None, False)
    others = (below, above, beyond)
    state, *others = lax.optimization_barrier((state, *others))
    swapped = [across(block) for block in others]
    state = coarse_attend((mine, spot(3), spot(1), spot(2)), qkv, others, state, False)
    state, *swapped = lax.optimization_barrier((state, *swapped))
    mixed = coarse_attend((mine, spot(3, 1), spot(1, 1), spot(2, 1)), qkv, swapped, state, True)
    mixed = lax.all_to_all(mixed, ("z", "x"), 0, 0)
    return finish(mixed, coarse_out, shortened, natural)


def solution(mesh):
    fine = Mesh(mesh.devices.reshape(4, 4, 4, 2), ALL)
    return jax.shard_map(
        body,
        mesh=fine,
        in_specs=(P(ALL, None), P(), P(), P(), P(), P(("x", "y", "c"), None), P(), P(), P(), P()),
        out_specs=P(ALL, None),
        check_vma=False,
    )
```

```python
import functools
import math

import jax
import jax.numpy as jnp
from jax import lax
from jax.experimental import pallas as pl
from jax.experimental.pallas import tpu as pltpu
from jax.sharding import Mesh, PartitionSpec as P

HEAD_DIM = 64
HEADS = 16
SHORT = 8
WIN = 1024
SCALE = math.log2(math.e) / math.sqrt(HEAD_DIM)
ALL = ("z", "x", "y", "c")
QB = 128
PAIR = 2 * HEAD_DIM
NEG = -1e30


def from_behind(block, distance):
    devices = range(128)
    route = [(i - distance, i) for i in devices if i - distance in devices]
    return lax.ppermute(block, ALL, route)


def normed(rows):
    values = rows.astype(jnp.float32)
    scale = lax.rsqrt(jnp.mean(values * values, axis=-1, keepdims=True) + 1e-06)
    return (values * scale).astype(jnp.bfloat16)


def dot(a, b, contract):
    return lax.dot_general(a, b, (contract, ((), ())), preferred_element_type=jnp.float32)


def params(mib=24):
    return pltpu.CompilerParams(vmem_limit_bytes=mib * 2**20)


def spots(index):
    groups = QB // SHORT
    return (index % groups) * SHORT + index // groups


def two_heads(q_ref, b):
    lane = lax.broadcasted_iota(jnp.int32, (QB, PAIR), 1)
    q = q_ref[b * QB : (b + 1) * QB, :]
    zero = jnp.zeros_like(q)
    return jnp.concatenate(
        [jnp.where(lane < HEAD_DIM, q, zero), jnp.where(lane < HEAD_DIM, zero, q)], axis=0
    )


def with_sums(v):
    return jnp.concatenate([v, jnp.ones((16, v.shape[1]), jnp.bfloat16)], axis=0)


def moves(rows, take):
    col = lax.broadcasted_iota(jnp.int32, (rows, QB), 1)
    row = lax.broadcasted_iota(jnp.int32, (rows, QB), 0)
    return jnp.where(take(row) == col, 1.0, 0.0).astype(jnp.bfloat16)


def reorder(move, rows):
    parts = [dot(move, rows[i : i + QB], ((1,), (0,))) for i in range(0, rows.shape[0], QB)]
    return jnp.concatenate(parts, axis=0)


def project_kernel(number, core_ref, rows_ref, *refs):
    weights, outs = refs[:number], refs[number:]
    rows = normed(rows_ref[...])
    if number == 3:
        rows = reorder(moves(QB, spots), rows).astype(jnp.bfloat16)
        outs[2][...] = (dot(rows, weights[2][...], ((1,), (0,))) * SCALE).astype(jnp.bfloat16)
    outs[0][...] = dot(rows, weights[0][...], ((1,), (0,))).astype(jnp.bfloat16)
    outs[1][...] = dot(weights[1][...], rows, ((1,), (1,))).astype(jnp.bfloat16)


def project(core, rows, weights):
    count, width = rows.shape
    half = width // 2
    tile = 512
    by_row = pl.BlockSpec((tile, half), lambda i, c: (i, 0))
    columns = pl.BlockSpec((width, half), lambda i, c: (0, c[0]))
    number = len(weights)
    return pl.pallas_call(
        functools.partial(project_kernel, number),
        name="project",
        grid_spec=pltpu.PrefetchScalarGridSpec(
            num_scalar_prefetch=1,
            grid=(count // tile,),
            in_specs=[pl.BlockSpec((tile, width), lambda i, c: (i, 0))]
            + [columns, pl.BlockSpec((half, width), lambda i, c: (c[0], 0)), columns][:number],
            out_specs=[by_row, pl.BlockSpec((half, tile), lambda i, c: (0, i)), by_row][:number],
        ),
        out_shape=[
            jax.ShapeDtypeStruct((count, half), jnp.bfloat16),
            jax.ShapeDtypeStruct((half, count), jnp.bfloat16),
            jax.ShapeDtypeStruct((count, half), jnp.bfloat16),
        ][:number],
        compiler_params=params(20),
        cost_estimate=pl.CostEstimate(flops=1, bytes_accessed=1, transcendentals=0),
    )(core.reshape(1), *[rows, *weights])


def tail_project_kernel(core_ref, tokens_ref, mine_ref, theirs_ref, my_ref, their_ref, tail_ref):
    groups = QB // SHORT
    total = dot(moves(16, lambda r: r + QB - SHORT), tokens_ref[...], ((1,), (0,)))
    take = moves(16, lambda r: r * groups + groups - 1)
    mine = dot(take, mine_ref[0], ((1,), (0,))).astype(jnp.bfloat16)
    theirs = dot(take, theirs_ref[...], ((1,), (0,))).astype(jnp.bfloat16)
    total = total + dot(mine, my_ref[...], ((1,), (0,))) + dot(theirs, their_ref[...], ((1,), (0,)))
    tail_ref[...] = total.astype(jnp.bfloat16)


def tail_project(core, tokens, mixed, theirs, weight):
    count, width = tokens.shape
    half = width // 2
    last = count // QB - 1
    tile = width // 2
    return pl.pallas_call(
        tail_project_kernel,
        name="tail_project",
        grid_spec=pltpu.PrefetchScalarGridSpec(
            num_scalar_prefetch=1,
            grid=(2,),
            in_specs=[
                pl.BlockSpec((QB, tile), lambda i, c: (last, i)),
                pl.BlockSpec((1, QB, half), lambda i, c: (0, last, 0)),
                pl.BlockSpec((QB, half), lambda i, c: (last, 0)),
                pl.BlockSpec((half, tile), lambda i, c: (c[0], i)),
                pl.BlockSpec((half, tile), lambda i, c: (1 - c[0], i)),
            ],
            out_specs=pl.BlockSpec((16, tile), lambda i, c: (0, i)),
        ),
        out_shape=jax.ShapeDtypeStruct((16, width), jnp.bfloat16),
        compiler_params=params(20),
    )(core.reshape(1), tokens, mixed, theirs, weight, weight)


def out_project_kernel(core_ref, tokens_ref, mine_ref, theirs_ref, my_ref, their_ref, hidden_ref, natural_ref):
    total = reorder(moves(QB, spots), tokens_ref[...])
    total = total + dot(mine_ref[0], my_ref[...], ((1,), (0,)))
    total = total + dot(theirs_ref[...], their_ref[...], ((1,), (0,)))
    hidden = total.astype(jnp.bfloat16)
    hidden_ref[...] = hidden
    groups = QB // SHORT
    natural_ref[...] = reorder(moves(QB, lambda r: (r % SHORT) * groups + r // SHORT), hidden).astype(jnp.bfloat16)


def out_project(core, tokens, mixed, theirs, weight):
    count, width = tokens.shape
    half = width // 2
    by_column = pl.BlockSpec((count, half), lambda i, c: (0, i))
    return pl.pallas_call(
        out_project_kernel,
        name="out_project",
        grid_spec=pltpu.PrefetchScalarGridSpec(
            num_scalar_prefetch=1,
            grid=(2,),
            in_specs=[
                by_column,
                pl.BlockSpec((1, count, half), lambda i, c: (0, 0, 0)),
                pl.BlockSpec((count, half), lambda i, c: (0, 0)),
                pl.BlockSpec((half, half), lambda i, c: (c[0], i)),
                pl.BlockSpec((half, half), lambda i, c: (1 - c[0], i)),
            ],
            out_specs=[by_column, by_column],
        ),
        out_shape=[jax.ShapeDtypeStruct((count, width), jnp.bfloat16)] * 2,
        compiler_params=params(20),
    )(core.reshape(1), tokens, mixed, theirs, weight, weight)


def pack_kernel(y_ref, hidden_ref, tail_ref, *refs):
    outs, all_ref = refs[:4], refs[4]
    blocks, places, groups, width = hidden_ref.shape
    rows = blocks * groups
    half = width // 2
    for j in range(SHORT):
        p = (j + 1) % SHORT
        part = hidden_ref[:, p].reshape(rows, width)
        if p > 0:
            wide = part.astype(jnp.float32)
            tail = tail_ref[p : p + 1, :].astype(jnp.float32)
            first = lax.broadcasted_iota(jnp.int32, wide.shape, 0) == 0
            wide = jnp.where(first, tail, pltpu.roll(wide, 1, 0))
            part = wide.astype(jnp.bfloat16)
        for f in range(2):
            all_ref[(j % 2) * 2 + f, j // 2] = part[:, f * half : (f + 1) * half]
    for r in range(4):
        outs[r][...] = all_ref[(y_ref[0] + r) % 4]


def pack(y, hidden, tail):
    count, width = hidden.shape
    groups = QB // SHORT
    blocks = count // QB
    shape = (4, count // SHORT, width // 2)
    return pl.pallas_call(
        pack_kernel,
        name="pack",
        in_specs=[pl.BlockSpec(memory_space=pltpu.SMEM)] + [pl.BlockSpec(memory_space=pltpu.VMEM)] * 2,
        out_shape=[jax.ShapeDtypeStruct(shape, jnp.bfloat16)] * 4,
        scratch_shapes=[pltpu.VMEM((4, *shape), jnp.bfloat16)],
        compiler_params=params(),
    )(y.reshape(1), hidden.reshape(blocks, SHORT, groups, width), tail)


def fine_own_kernel(q_ref, k_ref, v_ref, top_ref, acc_ref, s_ref, p_ref):
    blocks = q_ref.shape[0] // QB
    row = lax.broadcasted_iota(jnp.int32, (QB, 2 * QB), 0)
    col = lax.broadcasted_iota(jnp.int32, (QB, 2 * QB), 1) % QB
    keep = spots(row) <= spots(col)
    for b in range(blocks):
        both = two_heads(q_ref, b)
        if b > 0:
            s_ref[b, : b * QB, :] = dot(k_ref[: b * QB, :], both, ((1,), (1,)))
        s = dot(k_ref[b * QB : (b + 1) * QB, :], both, ((1,), (1,)))
        s_ref[b, b * QB : (b + 1) * QB, :] = jnp.where(keep, s, NEG)
    for b in range(blocks):
        end = (b + 1) * QB
        top = jnp.max(s_ref[b, :end, :], axis=0, keepdims=True)
        p_ref[b, :end, :] = jnp.exp2(s_ref[b, :end, :] - top).astype(jnp.bfloat16)
        top_ref[0, b] = jnp.broadcast_to(top, (8, 2 * QB))
    for b in range(blocks):
        end = (b + 1) * QB
        o = dot(with_sums(v_ref[:, :end]), p_ref[b, :end, :], ((1,), (0,)))
        acc_ref[0, b, :16, :] = o[PAIR:]
        acc_ref[0, b, 16:, :QB] = o[:HEAD_DIM, :QB]
        acc_ref[0, b, 16:, QB:] = o[HEAD_DIM:PAIR, QB:]


def fine_before_kernel(
    where_ref, q_ref, kf_ref, kn_ref, vf_ref, vn_ref, top_ref, acc_ref, out_ref, s_ref, p_ref
):
    half = kf_ref.shape[0]
    blocks = q_ref.shape[0] // QB
    core = where_ref[0]
    row = lax.broadcasted_iota(jnp.int32, (QB, 2 * QB), 0)
    col = lax.broadcasted_iota(jnp.int32, (QB, 2 * QB), 1) % QB
    keep = row > spots(col)

    def store(b, total, o):
        o = o * (1.0 / total)
        mixed = jnp.concatenate([o[:, :QB], o[:, QB:]], axis=0)
        at = b * QB // half
        out_ref[(at + core) % 2, b * QB - at * half : (b + 1) * QB - at * half, :] = mixed.T.astype(jnp.bfloat16)

    @pl.when(where_ref[1] == 0)
    def _():
        for b in range(blocks):
            store(b, acc_ref[0, b, 0:1, :], acc_ref[0, b, 16:, :])

    def units(low, high):
        def spans(b):
            if b * QB < half:
                return [(low, b * QB, half - b * QB), (high, 0, half)]
            return [(high, b * QB - half, 2 * half - b * QB)]

        for b in range(blocks):
            both = two_heads(q_ref, b)
            at = b * QB
            for (k_ref, _), first, size in spans(b):
                if at == b * QB:
                    s = dot(k_ref[first : first + QB, :], both, ((1,), (1,)))
                    s_ref[b, at : at + QB, :] = jnp.where(keep, s, NEG)
                    at, first, size = at + QB, first + QB, size - QB
                if size > 0:
                    s_ref[b, at : at + size, :] = dot(k_ref[first : first + size, :], both, ((1,), (1,)))
                at += size
        fades = []
        for b in range(blocks):
            old = top_ref[0, b, 0:1, :]
            top = jnp.maximum(old, jnp.max(s_ref[b, b * QB :, :], axis=0, keepdims=True))
            p_ref[b, b * QB :, :] = jnp.exp2(s_ref[b, b * QB :, :] - top).astype(jnp.bfloat16)
            fades.append(jnp.exp2(old - top))
        for b in range(blocks):
            v = [v_ref[:, first : first + size] for (_, v_ref), first, size in spans(b)]
            o = dot(with_sums(jnp.concatenate(v, axis=1)), p_ref[b, b * QB :, :], ((1,), (0,)))
            acc = acc_ref[0, b] * fades[b]
            new = jnp.concatenate([o[:HEAD_DIM, :QB], o[HEAD_DIM:PAIR, QB:]], axis=1)
            store(b, acc[0:1] + o[PAIR : PAIR + 1], acc[16:] + new)

    @pl.when((where_ref[1] > 0) & (core == 0))
    def _():
        units((kf_ref, vf_ref), (kn_ref, vn_ref))

    @pl.when((where_ref[1] > 0) & (core == 1))
    def _():
        units((kn_ref, vn_ref), (kf_ref, vf_ref))


def fine_own(q, k, v):
    count, width = q.shape
    blocks = count // QB
    pairs = width // PAIR
    return pl.pallas_call(
        fine_own_kernel,
        name="fine_own",
        grid=(pairs,),
        in_specs=[
            pl.BlockSpec((count, PAIR), lambda i: (0, i)),
            pl.BlockSpec((count, PAIR), lambda i: (0, i)),
            pl.BlockSpec((PAIR, count), lambda i: (i, 0)),
        ],
        out_specs=[
            pl.BlockSpec((1, blocks, 8, 2 * QB), lambda i: (i, 0, 0, 0)),
            pl.BlockSpec((1, blocks, 16 + HEAD_DIM, 2 * QB), lambda i: (i, 0, 0, 0)),
        ],
        out_shape=[
            jax.ShapeDtypeStruct((pairs, blocks, 8, 2 * QB), jnp.float32),
            jax.ShapeDtypeStruct((pairs, blocks, 16 + HEAD_DIM, 2 * QB), jnp.float32),
        ],
        scratch_shapes=[
            pltpu.VMEM((blocks, count, 2 * QB), jnp.float32),
            pltpu.VMEM((blocks, count, 2 * QB), jnp.bfloat16),
        ],
        compiler_params=params(),
        cost_estimate=pl.CostEstimate(flops=1, bytes_accessed=1, transcendentals=0),
    )(q, k, v)


def fine_before(where, q, keys, values, state):
    count, width = q.shape
    blocks = count // QB
    half = count // 2
    return pl.pallas_call(
        fine_before_kernel,
        name="fine_before",
        grid=(width // PAIR,),
        in_specs=[pl.BlockSpec(memory_space=pltpu.SMEM), pl.BlockSpec((count, PAIR), lambda i: (0, i))]
        + [pl.BlockSpec((half, PAIR), lambda i: (0, i))] * 2
        + [pl.BlockSpec((PAIR, half), lambda i: (i, 0))] * 2
        + [
            pl.BlockSpec((1, blocks, 8, 2 * QB), lambda i: (i, 0, 0, 0)),
            pl.BlockSpec((1, blocks, 16 + HEAD_DIM, 2 * QB), lambda i: (i, 0, 0, 0)),
        ],
        out_specs=pl.BlockSpec((2, half, PAIR), lambda i: (0, 0, i)),
        out_shape=jax.ShapeDtypeStruct((2, half, width), jnp.bfloat16),
        scratch_shapes=[
            pltpu.VMEM((blocks, count, 2 * QB), jnp.float32),
            pltpu.VMEM((blocks, count, 2 * QB), jnp.bfloat16),
        ],
        compiler_params=params(),
        cost_estimate=pl.CostEstimate(flops=1, bytes_accessed=1, transcendentals=0),
    )(where, q, *keys, *values, *state)


def shorten_kernel(spots_of, where_ref, *refs):
    grouped, pieces, outs = refs[:4], refs[4:-4], refs[-4:]
    parts, rows, depth = grouped[0].shape
    total = None
    for (distance, other), piece in zip(spots_of, pieces):
        size = piece.shape[0]
        x = (where_ref[0] + parts - distance) % parts
        core = 1 - where_ref[1] if other else where_ref[1]
        columns = pl.ds(pl.multiple_of(core * size, size), size)
        part = jnp.concatenate([ref[x, :, columns] for ref in grouped], axis=0)
        term = dot(part, piece[...], ((1,), (0,)))
        total = term if total is None else total + term
    for r in range(4):
        outs[r][...] = total[r * rows : (r + 1) * rows].astype(jnp.bfloat16)


def shorten(where, grouped, pieces, spots_of):
    parts, rows, depth = grouped[0].shape
    width = pieces[0].shape[1]
    tile = width // 2
    return pl.pallas_call(
        functools.partial(shorten_kernel, spots_of),
        name="shorten",
        grid=(2,),
        in_specs=[pl.BlockSpec(memory_space=pltpu.SMEM)]
        + [pl.BlockSpec(grouped[0].shape, lambda i: (0, 0, 0))] * 4
        + [pl.BlockSpec((piece.shape[0], tile), lambda i: (0, i)) for piece in pieces],
        out_specs=[pl.BlockSpec((rows, tile), lambda i: (0, i))] * 4,
        out_shape=[jax.ShapeDtypeStruct((rows, width), jnp.bfloat16)] * 4,
        compiler_params=params(60),
    )(where, *grouped, *pieces)


def coarse_project_kernel(*refs):
    parts, (q_ref, k_ref, v_ref, short_ref, qkv_ref, norm_ref) = refs[:4], refs[4:]

    @pl.when(pl.program_id(0) == 0)
    def _():
        short = sum(ref[...].astype(jnp.float32) for ref in parts).astype(jnp.bfloat16)
        short_ref[...] = short
        norm_ref[...] = normed(short)

    rows = norm_ref[...]
    for i, (ref, scale) in enumerate(((k_ref, None), (v_ref, None), (q_ref, SCALE))):
        out = dot(rows, ref[...], ((1,), (0,)))
        if scale is not None:
            out = out * scale
        out = out.astype(jnp.bfloat16)
        for h in range(qkv_ref.shape[0]):
            qkv_ref[h, :, i * HEAD_DIM : (i + 1) * HEAD_DIM] = out[:, h * HEAD_DIM : (h + 1) * HEAD_DIM]


def coarse_project(partial, query, key, value):
    rows, width = partial[0].shape
    tile = 4 * HEAD_DIM
    spec = pl.BlockSpec((width, tile), lambda i: (0, i))
    return pl.pallas_call(
        coarse_project_kernel,
        name="coarse_project",
        grid=(width // tile,),
        in_specs=[pl.BlockSpec((rows, width), lambda i: (0, 0))] * 4 + [spec, spec, spec],
        out_specs=[
            pl.BlockSpec((rows, width), lambda i: (0, 0)),
            pl.BlockSpec((4, rows, 3 * HEAD_DIM), lambda i: (i, 0, 0)),
        ],
        out_shape=[
            jax.ShapeDtypeStruct((rows, width), jnp.bfloat16),
            jax.ShapeDtypeStruct((HEADS, rows, 3 * HEAD_DIM), jnp.bfloat16),
        ],
        scratch_shapes=[pltpu.VMEM((rows, width), jnp.bfloat16)],
        compiler_params=params(60),
    )(*partial, query, key, value)


def finish_kernel(mixed_ref, out_weight_ref, short_ref, hidden_ref, out_ref, rows_ref):
    heads, rows, _ = mixed_ref.shape
    rows = 2 * rows

    @pl.when(pl.program_id(0) == 0)
    def _():
        for h in range(heads):
            m = mixed_ref[h]
            rows_ref[:, h * HEAD_DIM : (h + 1) * HEAD_DIM] = jnp.concatenate(
                [m[:, :HEAD_DIM], m[:, HEAD_DIM:]], axis=0
            )

    refined = short_ref[...].astype(jnp.float32) + dot(rows_ref[...], out_weight_ref[...], ((1,), (0,)))
    tile = refined.shape[1]
    spread = jnp.broadcast_to(refined[:, None, :], (rows, SHORT, tile)).reshape(rows * SHORT, tile)
    out_ref[...] = (hidden_ref[...].astype(jnp.float32) + spread).astype(jnp.bfloat16)


def finish(mixed, out_weight, short, hidden):
    count, width = hidden.shape
    rows = count // SHORT
    tile = width // 4
    return pl.pallas_call(
        finish_kernel,
        name="finish",
        grid=(4,),
        in_specs=[
            pl.BlockSpec(mixed.shape, lambda i: (0, 0, 0)),
            pl.BlockSpec((width, tile), lambda i: (0, i)),
            pl.BlockSpec((rows, tile), lambda i: (0, i)),
            pl.BlockSpec((count, tile), lambda i: (0, i)),
        ],
        out_specs=pl.BlockSpec((count, tile), lambda i: (0, i)),
        out_shape=jax.ShapeDtypeStruct((count, width), jnp.bfloat16),
        scratch_shapes=[pltpu.VMEM((rows, width), jnp.bfloat16)],
        compiler_params=params(60),
    )(mixed, out_weight, short, hidden)


def coarse_kernel(number, first, final, where_ref, q_ref, *refs):
    parts = refs[:number]
    old = None if first else refs[number : number + 2]
    outs = refs[number if first else number + 2 :]
    blocks, rows, _ = parts[0].shape
    tile = 4 * rows
    tiles = blocks // 4
    lane = lax.broadcasted_iota(jnp.int32, (1, tile), 1)
    row = lax.broadcasted_iota(jnp.int32, (tile, tile), 0)
    stride = 8 * rows
    place = (row // rows) * stride + row % rows
    limit = (lane // rows) * stride + where_ref[0] * rows + lane % rows
    ones = jnp.ones((16, number * tile), jnp.bfloat16)
    queries = []
    for t in range(tiles):
        q = q_ref[4 * t : 4 * t + 4, :, 2 * HEAD_DIM :].reshape(tile, HEAD_DIM)
        queries.append(jnp.concatenate([q, jnp.zeros_like(q)], axis=1))
    if first:
        tops = [jnp.full((1, tile), NEG, jnp.float32)] * tiles
        accs = [jnp.zeros((16 + HEAD_DIM, tile), jnp.float32)] * tiles
    else:
        tops = [old[0][t, 0:1, :] for t in range(tiles)]
        accs = [old[1][t] for t in range(tiles)]
    for g in range(tiles):
        kv = jnp.concatenate([part[4 * g : 4 * g + 4].reshape(tile, PAIR) for part in parts], axis=0)
        v = jnp.concatenate([ones, kv.T[HEAD_DIM:, :]], axis=0)
        live = range(g, tiles)
        scores = [dot(kv, queries[t], ((1,), (1,))) for t in live]
        keep = jnp.concatenate(
            [place <= limit - where_ref[1 + i] * rows for i in range(number)], axis=0
        )
        scores[0] = jnp.where(keep, scores[0], NEG)
        news = [jnp.maximum(tops[t], jnp.max(s, axis=0, keepdims=True)) for t, s in zip(live, scores)]
        ps = [jnp.exp2(s - top).astype(jnp.bfloat16) for s, top in zip(scores, news)]
        for t, top, p in zip(live, news, ps):
            accs[t] = accs[t] * jnp.exp2(tops[t] - top) + dot(v, p, ((1,), (0,)))
            tops[t] = top
    for t in range(tiles):
        if final:
            o = accs[t][16:] * (1.0 / accs[t][0:1])
            o = o.T.astype(jnp.bfloat16)
            for i in range(0, tile, rows):
                low, high = o[i : i + rows // 2], o[i + rows // 2 : i + rows]
                outs[0][4 * t + i // rows] = jnp.concatenate([low, high], axis=1)
        else:
            outs[0][t] = jnp.broadcast_to(tops[t], (8, tile))
            outs[1][t] = accs[t]


def coarse_attend(places, q, parts, state, final):
    heads, rows, _ = q.shape
    tile = 4 * rows
    if final:
        out_shape = jax.ShapeDtypeStruct((heads, rows // 2, PAIR), jnp.bfloat16)
    else:
        out_shape = [
            jax.ShapeDtypeStruct((heads // 4, 8, tile), jnp.float32),
            jax.ShapeDtypeStruct((heads // 4, 16 + HEAD_DIM, tile), jnp.float32),
        ]
    first = state is None
    arrays = [q, *parts] + ([] if first else list(state))
    share = len(parts) / 8
    return pl.pallas_call(
        functools.partial(coarse_kernel, len(parts), first, final),
        in_specs=[pl.BlockSpec(memory_space=pltpu.SMEM)]
        + [pl.BlockSpec(memory_space=pltpu.VMEM)] * len(arrays),
        out_shape=out_shape,
        name="coarse_attend",
        compiler_params=params(),
        cost_estimate=pl.CostEstimate(
            flops=int(share * 6 * 2**30), bytes_accessed=2 * 2**20, transcendentals=int(share * 5 * 2**20)
        ),
    )(jnp.stack(places).astype(jnp.int32), *arrays)


def body(
    tokens,
    fine_query,
    fine_key,
    fine_value,
    fine_out,
    short_weight,
    coarse_query,
    coarse_key,
    coarse_value,
    coarse_out,
):
    count, width = tokens.shape
    bf = jnp.bfloat16
    place = lax.axis_index(ALL).astype(jnp.int32)
    core = lax.axis_index("c").astype(jnp.int32)

    def across(block):
        return lax.ppermute(block, "c", [(0, 1), (1, 0)])

    far = from_behind(tokens, 2)
    mate = across(tokens)
    weights = [fine_key, fine_value.T]
    chip = jnp.concatenate(
        [jnp.where(core == 0, tokens, mate), jnp.where(core == 0, mate, tokens)], axis=0
    )

    def along_x(block, distance):
        return lax.ppermute(block, "x", [(i, (i + distance) % 4) for i in range(4)])

    together = lax.optimization_barrier
    keys, values, query = project(core, chip, [*weights, fine_query])
    state = fine_own(query, keys, values)
    mate_weight = across(short_weight)
    far, state, query, short_weight, mate_weight = together((far, state, query, short_weight, mate_weight))
    near = across(far)
    behind, ahead = along_x(short_weight, 1), along_x(short_weight, 3)
    far_keys, far_values = project(core, far, weights)
    near_keys, near_values = project(core, near, weights)
    where = jnp.stack([core, (place > 1).astype(jnp.int32)])
    fine_mixed = fine_before(where, query, (far_keys, near_keys), (far_values, near_values), state)
    fine_mixed, behind, ahead = together((fine_mixed, behind, ahead))
    two_away = along_x(ahead, 3)
    theirs = across(fine_mixed[1])
    tail = from_behind(tail_project(core, tokens, fine_mixed, theirs, fine_out), 1)
    hidden, natural = out_project(core, tokens, fine_mixed, theirs, fine_out)
    mate_behind, mate_ahead = across(behind), across(ahead)
    hidden, mate_behind, mate_ahead = together((hidden, mate_behind, mate_ahead))
    y = lax.axis_index("y").astype(jnp.int32)

    def along_y(block, distance):
        return lax.ppermute(block, "y", [(i, (i + distance) % 4) for i in range(4)])

    def exchange(blocks, sign):
        return [along_y(block, sign * r) if r > 0 else block for r, block in enumerate(blocks)]

    grouped = exchange(pack(y, hidden, tail), 1)
    *grouped, two_away = together((*grouped, two_away))
    pieces = [short_weight, behind, two_away, ahead, mate_weight, mate_behind, across(two_away), mate_ahead]
    spots_of = [(distance, other) for other in (0, 1) for distance in range(4)]
    where = jnp.stack([lax.axis_index("x").astype(jnp.int32), core])
    partial = exchange(shorten(where, grouped, pieces, spots_of), -1)
    shortened, qkv = coarse_project(partial, coarse_query, coarse_key, coarse_value)
    qkv = lax.all_to_all(qkv, ("z", "x"), 0, 0)
    kv = qkv[:, :, : 2 * HEAD_DIM]
    c = core
    mine = y * 2 + c

    def spot(distance, other=0):
        return ((y + distance) % 4) * 2 + (1 - c if other else c)

    mate_kv = across(kv)
    below, above, beyond = along_y(kv, 1), along_y(kv, 3), along_y(kv, 2)
    state = coarse_attend((mine, mine, spot(0, 1)), qkv, (kv, mate_kv), None, False)
    others = (below, above, beyond)
    state, *others = lax.optimization_barrier((state, *others))
    swapped = [across(block) for block in others]
    state = coarse_attend((mine, spot(3), spot(1), spot(2)), qkv, others, state, False)
    state, *swapped = lax.optimization_barrier((state, *swapped))
    mixed = coarse_attend((mine, spot(3, 1), spot(1, 1), spot(2, 1)), qkv, swapped, state, True)
    mixed = lax.all_to_all(mixed, ("z", "x"), 0, 0)
    return finish(mixed, coarse_out, shortened, natural)


def solution(mesh):
    fine = Mesh(mesh.devices.reshape(4, 4, 4, 2), ALL)
    return jax.shard_map(
        body,
        mesh=fine,
        in_specs=(P(ALL, None), P(), P(), P(), P(), P(("x", "y", "c"), None), P(), P(), P(), P()),
        out_specs=P(ALL, None),
        check_vma=False,
    )
```

```python
import functools
import math

import jax
import jax.numpy as jnp
from jax import lax
from jax.experimental import pallas as pl
from jax.experimental.pallas import tpu as pltpu
from jax.sharding import Mesh, PartitionSpec as P

HEAD_DIM = 64
HEADS = 16
SHORT = 8
WIN = 1024
SCALE = math.log2(math.e) / math.sqrt(HEAD_DIM)
ALL = ("z", "x", "y", "c")
QB = 128
PAIR = 2 * HEAD_DIM
NEG = -1e30


def from_behind(block, distance):
    devices = range(128)
    route = [(i - distance, i) for i in devices if i - distance in devices]
    return lax.ppermute(block, ALL, route)


def normed(rows):
    values = rows.astype(jnp.float32)
    scale = lax.rsqrt(jnp.mean(values * values, axis=-1, keepdims=True) + 1e-06)
    return (values * scale).astype(jnp.bfloat16)


def dot(a, b, contract):
    return lax.dot_general(a, b, (contract, ((), ())), preferred_element_type=jnp.float32)


def params(mib=24):
    return pltpu.CompilerParams(vmem_limit_bytes=mib * 2**20)


def spots(index):
    groups = QB // SHORT
    return (index % groups) * SHORT + index // groups


def two_heads(q_ref, b):
    lane = lax.broadcasted_iota(jnp.int32, (QB, PAIR), 1)
    q = q_ref[b * QB : (b + 1) * QB, :]
    zero = jnp.zeros_like(q)
    return jnp.concatenate(
        [jnp.where(lane < HEAD_DIM, q, zero), jnp.where(lane < HEAD_DIM, zero, q)], axis=0
    )


def with_sums(v):
    return jnp.concatenate([v, jnp.ones((16, v.shape[1]), jnp.bfloat16)], axis=0)


def moves(rows, take):
    col = lax.broadcasted_iota(jnp.int32, (rows, QB), 1)
    row = lax.broadcasted_iota(jnp.int32, (rows, QB), 0)
    return jnp.where(take(row) == col, 1.0, 0.0).astype(jnp.bfloat16)


def reorder(move, rows):
    parts = [dot(move, rows[i : i + QB], ((1,), (0,))) for i in range(0, rows.shape[0], QB)]
    return jnp.concatenate(parts, axis=0)


def project_kernel(number, core_ref, rows_ref, *refs):
    weights, outs = refs[:number], refs[number:]
    rows = normed(rows_ref[...])
    if number == 3:
        rows = reorder(moves(QB, spots), rows).astype(jnp.bfloat16)
        outs[2][...] = (dot(rows, weights[2][...], ((1,), (0,))) * SCALE).astype(jnp.bfloat16)
    outs[0][...] = dot(rows, weights[0][...], ((1,), (0,))).astype(jnp.bfloat16)
    outs[1][...] = dot(weights[1][...], rows, ((1,), (1,))).astype(jnp.bfloat16)


def project(core, rows, weights):
    count, width = rows.shape
    half = width // 2
    tile = 512
    by_row = pl.BlockSpec((tile, half), lambda i, c: (i, 0))
    columns = pl.BlockSpec((width, half), lambda i, c: (0, c[0]))
    number = len(weights)
    return pl.pallas_call(
        functools.partial(project_kernel, number),
        name="project",
        grid_spec=pltpu.PrefetchScalarGridSpec(
            num_scalar_prefetch=1,
            grid=(count // tile,),
            in_specs=[pl.BlockSpec((tile, width), lambda i, c: (i, 0))]
            + [columns, pl.BlockSpec((half, width), lambda i, c: (c[0], 0)), columns][:number],
            out_specs=[by_row, pl.BlockSpec((half, tile), lambda i, c: (0, i)), by_row][:number],
        ),
        out_shape=[
            jax.ShapeDtypeStruct((count, half), jnp.bfloat16),
            jax.ShapeDtypeStruct((half, count), jnp.bfloat16),
            jax.ShapeDtypeStruct((count, half), jnp.bfloat16),
        ][:number],
        compiler_params=params(20),
        cost_estimate=pl.CostEstimate(flops=1, bytes_accessed=1, transcendentals=0),
    )(core.reshape(1), *[rows, *weights])


def tail_project_kernel(core_ref, tokens_ref, mine_ref, theirs_ref, my_ref, their_ref, tail_ref):
    groups = QB // SHORT
    total = dot(moves(16, lambda r: r + QB - SHORT), tokens_ref[...], ((1,), (0,)))
    take = moves(16, lambda r: r * groups + groups - 1)
    mine = dot(take, mine_ref[0], ((1,), (0,))).astype(jnp.bfloat16)
    theirs = dot(take, theirs_ref[...], ((1,), (0,))).astype(jnp.bfloat16)
    total = total + dot(mine, my_ref[...], ((1,), (0,))) + dot(theirs, their_ref[...], ((1,), (0,)))
    tail_ref[...] = total.astype(jnp.bfloat16)


def tail_project(core, tokens, mixed, theirs, weight):
    count, width = tokens.shape
    half = width // 2
    last = count // QB - 1
    tile = width // 2
    return pl.pallas_call(
        tail_project_kernel,
        name="tail_project",
        grid_spec=pltpu.PrefetchScalarGridSpec(
            num_scalar_prefetch=1,
            grid=(2,),
            in_specs=[
                pl.BlockSpec((QB, tile), lambda i, c: (last, i)),
                pl.BlockSpec((1, QB, half), lambda i, c: (0, last, 0)),
                pl.BlockSpec((QB, half), lambda i, c: (last, 0)),
                pl.BlockSpec((half, tile), lambda i, c: (c[0], i)),
                pl.BlockSpec((half, tile), lambda i, c: (1 - c[0], i)),
            ],
            out_specs=pl.BlockSpec((16, tile), lambda i, c: (0, i)),
        ),
        out_shape=jax.ShapeDtypeStruct((16, width), jnp.bfloat16),
        compiler_params=params(20),
    )(core.reshape(1), tokens, mixed, theirs, weight, weight)


def out_project_kernel(core_ref, tokens_ref, mine_ref, theirs_ref, my_ref, their_ref, hidden_ref, natural_ref):
    total = reorder(moves(QB, spots), tokens_ref[...])
    total = total + dot(mine_ref[0], my_ref[...], ((1,), (0,)))
    total = total + dot(theirs_ref[...], their_ref[...], ((1,), (0,)))
    hidden = total.astype(jnp.bfloat16)
    hidden_ref[...] = hidden
    groups = QB // SHORT
    natural_ref[...] = reorder(moves(QB, lambda r: (r % SHORT) * groups + r // SHORT), hidden).astype(jnp.bfloat16)


def out_project(core, tokens, mixed, theirs, weight):
    count, width = tokens.shape
    half = width // 2
    by_column = pl.BlockSpec((count, half), lambda i, c: (0, i))
    return pl.pallas_call(
        out_project_kernel,
        name="out_project",
        grid_spec=pltpu.PrefetchScalarGridSpec(
            num_scalar_prefetch=1,
            grid=(2,),
            in_specs=[
                by_column,
                pl.BlockSpec((1, count, half), lambda i, c: (0, 0, 0)),
                pl.BlockSpec((count, half), lambda i, c: (0, 0)),
                pl.BlockSpec((half, half), lambda i, c: (c[0], i)),
                pl.BlockSpec((half, half), lambda i, c: (1 - c[0], i)),
            ],
            out_specs=[by_column, by_column],
        ),
        out_shape=[jax.ShapeDtypeStruct((count, width), jnp.bfloat16)] * 2,
        compiler_params=params(20),
    )(core.reshape(1), tokens, mixed, theirs, weight, weight)


def pack_kernel(y_ref, hidden_ref, tail_ref, *refs):
    outs, all_ref = refs[:4], refs[4]
    blocks, places, groups, width = hidden_ref.shape
    rows = blocks * groups
    half = width // 2
    for j in range(SHORT):
        p = (j + 1) % SHORT
        part = hidden_ref[:, p].reshape(rows, width)
        if p > 0:
            wide = part.astype(jnp.float32)
            tail = tail_ref[p : p + 1, :].astype(jnp.float32)
            first = lax.broadcasted_iota(jnp.int32, wide.shape, 0) == 0
            wide = jnp.where(first, tail, pltpu.roll(wide, 1, 0))
            part = wide.astype(jnp.bfloat16)
        for f in range(2):
            all_ref[(j % 2) * 2 + f, j // 2] = part[:, f * half : (f + 1) * half]
    for r in range(4):
        outs[r][...] = all_ref[(y_ref[0] + r) % 4]


def pack(y, hidden, tail):
    count, width = hidden.shape
    groups = QB // SHORT
    blocks = count // QB
    shape = (4, count // SHORT, width // 2)
    return pl.pallas_call(
        pack_kernel,
        name="pack",
        in_specs=[pl.BlockSpec(memory_space=pltpu.SMEM)] + [pl.BlockSpec(memory_space=pltpu.VMEM)] * 2,
        out_shape=[jax.ShapeDtypeStruct(shape, jnp.bfloat16)] * 4,
        scratch_shapes=[pltpu.VMEM((4, *shape), jnp.bfloat16)],
        compiler_params=params(),
    )(y.reshape(1), hidden.reshape(blocks, SHORT, groups, width), tail)


def fine_own_kernel(q_ref, k_ref, v_ref, top_ref, acc_ref, s_ref, p_ref):
    blocks = q_ref.shape[0] // QB
    row = lax.broadcasted_iota(jnp.int32, (QB, 2 * QB), 0)
    col = lax.broadcasted_iota(jnp.int32, (QB, 2 * QB), 1) % QB
    keep = spots(row) <= spots(col)
    for b in range(blocks):
        both = two_heads(q_ref, b)
        if b > 0:
            s_ref[b, : b * QB, :] = dot(k_ref[: b * QB, :], both, ((1,), (1,)))
        s = dot(k_ref[b * QB : (b + 1) * QB, :], both, ((1,), (1,)))
        s_ref[b, b * QB : (b + 1) * QB, :] = jnp.where(keep, s, NEG)
    for b in range(blocks):
        end = (b + 1) * QB
        top = jnp.max(s_ref[b, :end, :], axis=0, keepdims=True)
        p_ref[b, :end, :] = jnp.exp2(s_ref[b, :end, :] - top).astype(jnp.bfloat16)
        top_ref[0, b] = jnp.broadcast_to(top, (8, 2 * QB))
    for b in range(blocks):
        end = (b + 1) * QB
        o = dot(with_sums(v_ref[:, :end]), p_ref[b, :end, :], ((1,), (0,)))
        acc_ref[0, b, :16, :] = o[PAIR:]
        acc_ref[0, b, 16:, :QB] = o[:HEAD_DIM, :QB]
        acc_ref[0, b, 16:, QB:] = o[HEAD_DIM:PAIR, QB:]


def fine_before_kernel(
    where_ref, q_ref, kf_ref, kn_ref, vf_ref, vn_ref, top_ref, acc_ref, out_ref, s_ref, p_ref
):
    half = kf_ref.shape[0]
    blocks = q_ref.shape[0] // QB
    core = where_ref[0]
    row = lax.broadcasted_iota(jnp.int32, (QB, 2 * QB), 0)
    col = lax.broadcasted_iota(jnp.int32, (QB, 2 * QB), 1) % QB
    keep = row > spots(col)

    def store(b, total, o):
        o = o * (1.0 / total)
        mixed = jnp.concatenate([o[:, :QB], o[:, QB:]], axis=0)
        at = b * QB // half
        out_ref[(at + core) % 2, b * QB - at * half : (b + 1) * QB - at * half, :] = mixed.T.astype(jnp.bfloat16)

    @pl.when(where_ref[1] == 0)
    def _():
        for b in range(blocks):
            store(b, acc_ref[0, b, 0:1, :], acc_ref[0, b, 16:, :])

    def units(low, high):
        def spans(b):
            if b * QB < half:
                return [(low, b * QB, half - b * QB), (high, 0, half)]
            return [(high, b * QB - half, 2 * half - b * QB)]

        for b in range(blocks):
            both = two_heads(q_ref, b)
            at = b * QB
            for (k_ref, _), first, size in spans(b):
                if at == b * QB:
                    s = dot(k_ref[first : first + QB, :], both, ((1,), (1,)))
                    s_ref[b, at : at + QB, :] = jnp.where(keep, s, NEG)
                    at, first, size = at + QB, first + QB, size - QB
                if size > 0:
                    s_ref[b, at : at + size, :] = dot(k_ref[first : first + size, :], both, ((1,), (1,)))
                at += size
        fades = []
        for b in range(blocks):
            old = top_ref[0, b, 0:1, :]
            top = jnp.maximum(old, jnp.max(s_ref[b, b * QB :, :], axis=0, keepdims=True))
            p_ref[b, b * QB :, :] = jnp.exp2(s_ref[b, b * QB :, :] - top).astype(jnp.bfloat16)
            fades.append(jnp.exp2(old - top))
        for b in range(blocks):
            v = [v_ref[:, first : first + size] for (_, v_ref), first, size in spans(b)]
            o = dot(with_sums(jnp.concatenate(v, axis=1)), p_ref[b, b * QB :, :], ((1,), (0,)))
            acc = acc_ref[0, b] * fades[b]
            new = jnp.concatenate([o[:HEAD_DIM, :QB], o[HEAD_DIM:PAIR, QB:]], axis=1)
            store(b, acc[0:1] + o[PAIR : PAIR + 1], acc[16:] + new)

    @pl.when((where_ref[1] > 0) & (core == 0))
    def _():
        units((kf_ref, vf_ref), (kn_ref, vn_ref))

    @pl.when((where_ref[1] > 0) & (core == 1))
    def _():
        units((kn_ref, vn_ref), (kf_ref, vf_ref))


def fine_own(q, k, v):
    count, width = q.shape
    blocks = count // QB
    pairs = width // PAIR
    return pl.pallas_call(
        fine_own_kernel,
        name="fine_own",
        grid=(pairs,),
        in_specs=[
            pl.BlockSpec((count, PAIR), lambda i: (0, i)),
            pl.BlockSpec((count, PAIR), lambda i: (0, i)),
            pl.BlockSpec((PAIR, count), lambda i: (i, 0)),
        ],
        out_specs=[
            pl.BlockSpec((1, blocks, 8, 2 * QB), lambda i: (i, 0, 0, 0)),
            pl.BlockSpec((1, blocks, 16 + HEAD_DIM, 2 * QB), lambda i: (i, 0, 0, 0)),
        ],
        out_shape=[
            jax.ShapeDtypeStruct((pairs, blocks, 8, 2 * QB), jnp.float32),
            jax.ShapeDtypeStruct((pairs, blocks, 16 + HEAD_DIM, 2 * QB), jnp.float32),
        ],
        scratch_shapes=[
            pltpu.VMEM((blocks, count, 2 * QB), jnp.float32),
            pltpu.VMEM((blocks, count, 2 * QB), jnp.bfloat16),
        ],
        compiler_params=params(),
        cost_estimate=pl.CostEstimate(flops=1, bytes_accessed=1, transcendentals=0),
    )(q, k, v)


def fine_before(where, q, keys, values, state):
    count, width = q.shape
    blocks = count // QB
    half = count // 2
    return pl.pallas_call(
        fine_before_kernel,
        name="fine_before",
        grid=(width // PAIR,),
        in_specs=[pl.BlockSpec(memory_space=pltpu.SMEM), pl.BlockSpec((count, PAIR), lambda i: (0, i))]
        + [pl.BlockSpec((half, PAIR), lambda i: (0, i))] * 2
        + [pl.BlockSpec((PAIR, half), lambda i: (i, 0))] * 2
        + [
            pl.BlockSpec((1, blocks, 8, 2 * QB), lambda i: (i, 0, 0, 0)),
            pl.BlockSpec((1, blocks, 16 + HEAD_DIM, 2 * QB), lambda i: (i, 0, 0, 0)),
        ],
        out_specs=pl.BlockSpec((2, half, PAIR), lambda i: (0, 0, i)),
        out_shape=jax.ShapeDtypeStruct((2, half, width), jnp.bfloat16),
        scratch_shapes=[
            pltpu.VMEM((blocks, count, 2 * QB), jnp.float32),
            pltpu.VMEM((blocks, count, 2 * QB), jnp.bfloat16),
        ],
        compiler_params=params(),
        cost_estimate=pl.CostEstimate(flops=1, bytes_accessed=1, transcendentals=0),
    )(where, q, *keys, *values, *state)


def shorten_kernel(spots_of, where_ref, *refs):
    grouped, pieces, outs = refs[:4], refs[4:-4], refs[-4:]
    parts, rows, depth = grouped[0].shape
    total = None
    for (distance, other), piece in zip(spots_of, pieces):
        size = piece.shape[0]
        x = (where_ref[0] + parts - distance) % parts
        core = 1 - where_ref[1] if other else where_ref[1]
        columns = pl.ds(pl.multiple_of(core * size, size), size)
        part = jnp.concatenate([ref[x, :, columns] for ref in grouped], axis=0)
        term = dot(part, piece[...], ((1,), (0,)))
        total = term if total is None else total + term
    for r in range(4):
        outs[r][...] = total[r * rows : (r + 1) * rows].astype(jnp.bfloat16)


def shorten(where, grouped, pieces, spots_of):
    parts, rows, depth = grouped[0].shape
    width = pieces[0].shape[1]
    tile = width // 2
    return pl.pallas_call(
        functools.partial(shorten_kernel, spots_of),
        name="shorten",
        grid=(2,),
        in_specs=[pl.BlockSpec(memory_space=pltpu.SMEM)]
        + [pl.BlockSpec(grouped[0].shape, lambda i: (0, 0, 0))] * 4
        + [pl.BlockSpec((piece.shape[0], tile), lambda i: (0, i)) for piece in pieces],
        out_specs=[pl.BlockSpec((rows, tile), lambda i: (0, i))] * 4,
        out_shape=[jax.ShapeDtypeStruct((rows, width), jnp.bfloat16)] * 4,
        compiler_params=params(60),
    )(where, *grouped, *pieces)


def coarse_project_kernel(*refs):
    parts, (k_ref, v_ref, q_ref, short_ref, qkv_ref, weight_ref, sems) = refs[:4], refs[4:]
    copies = [
        pltpu.make_async_copy(ref, weight_ref.at[i], sems.at[i])
        for i, ref in enumerate((k_ref, v_ref, q_ref))
    ]
    for copy in copies:
        copy.start()
    short = sum(ref[...].astype(jnp.float32) for ref in parts).astype(jnp.bfloat16)
    short_ref[...] = short
    rows = normed(short)
    for i, copy in enumerate(copies):
        copy.wait()
        out = dot(rows, weight_ref[i], ((1,), (0,)))
        if i == 2:
            out = out * SCALE
        out = out.astype(jnp.bfloat16)
        for h in range(HEADS):
            qkv_ref[h, :, i * HEAD_DIM : (i + 1) * HEAD_DIM] = out[:, h * HEAD_DIM : (h + 1) * HEAD_DIM]


def coarse_project(partial, query, key, value):
    rows, width = partial[0].shape
    vmem = pl.BlockSpec(memory_space=pltpu.VMEM)
    return pl.pallas_call(
        coarse_project_kernel,
        name="coarse_project",
        in_specs=[vmem] * 4 + [pl.BlockSpec(memory_space=pl.ANY)] * 3,
        out_specs=[vmem] * 2,
        out_shape=[
            jax.ShapeDtypeStruct((rows, width), jnp.bfloat16),
            jax.ShapeDtypeStruct((HEADS, rows, 3 * HEAD_DIM), jnp.bfloat16),
        ],
        scratch_shapes=[
            pltpu.VMEM((3, width, width), jnp.bfloat16),
            pltpu.SemaphoreType.DMA((3,)),
        ],
        compiler_params=params(60),
    )(*partial, key, value, query)


def finish_kernel(mixed_ref, out_weight_ref, short_ref, hidden_ref, out_ref, rows_ref):
    heads, rows, _ = mixed_ref.shape
    rows = 2 * rows

    @pl.when(pl.program_id(0) == 0)
    def _():
        for h in range(heads):
            m = mixed_ref[h]
            rows_ref[:, h * HEAD_DIM : (h + 1) * HEAD_DIM] = jnp.concatenate(
                [m[:, :HEAD_DIM], m[:, HEAD_DIM:]], axis=0
            )

    refined = short_ref[...].astype(jnp.float32) + dot(rows_ref[...], out_weight_ref[...], ((1,), (0,)))
    tile = refined.shape[1]
    spread = jnp.broadcast_to(refined[:, None, :], (rows, SHORT, tile)).reshape(rows * SHORT, tile)
    out_ref[...] = (hidden_ref[...].astype(jnp.float32) + spread).astype(jnp.bfloat16)


def finish(mixed, out_weight, short, hidden):
    count, width = hidden.shape
    rows = count // SHORT
    tile = width // 2
    return pl.pallas_call(
        finish_kernel,
        name="finish",
        grid=(2,),
        in_specs=[
            pl.BlockSpec(mixed.shape, lambda i: (0, 0, 0)),
            pl.BlockSpec((width, tile), lambda i: (0, i)),
            pl.BlockSpec((rows, tile), lambda i: (0, i)),
            pl.BlockSpec((count, tile), lambda i: (0, i)),
        ],
        out_specs=pl.BlockSpec((count, tile), lambda i: (0, i)),
        out_shape=jax.ShapeDtypeStruct((count, width), jnp.bfloat16),
        scratch_shapes=[pltpu.VMEM((rows, width), jnp.bfloat16)],
        compiler_params=params(60),
    )(mixed, out_weight, short, hidden)


def coarse_kernel(number, first, final, where_ref, q_ref, *refs):
    parts = refs[:number]
    old = None if first else refs[number : number + 2]
    outs = refs[number if first else number + 2 :]
    blocks, rows, _ = parts[0].shape
    tile = 4 * rows
    tiles = blocks // 4
    lane = lax.broadcasted_iota(jnp.int32, (1, tile), 1)
    row = lax.broadcasted_iota(jnp.int32, (tile, tile), 0)
    stride = 8 * rows
    place = (row // rows) * stride + row % rows
    limit = (lane // rows) * stride + where_ref[0] * rows + lane % rows
    ones = jnp.ones((16, number * tile), jnp.bfloat16)
    queries = []
    for t in range(tiles):
        q = q_ref[4 * t : 4 * t + 4, :, 2 * HEAD_DIM :].reshape(tile, HEAD_DIM)
        queries.append(jnp.concatenate([q, jnp.zeros_like(q)], axis=1))
    if first:
        tops = [jnp.full((1, tile), NEG, jnp.float32)] * tiles
        accs = [jnp.zeros((16 + HEAD_DIM, tile), jnp.float32)] * tiles
    else:
        tops = [old[0][t, 0:1, :] for t in range(tiles)]
        accs = [old[1][t] for t in range(tiles)]
    for g in range(tiles):
        kv = jnp.concatenate([part[4 * g : 4 * g + 4].reshape(tile, PAIR) for part in parts], axis=0)
        v = jnp.concatenate([ones, kv.T[HEAD_DIM:, :]], axis=0)
        live = range(g, tiles)
        scores = [dot(kv, queries[t], ((1,), (1,))) for t in live]
        keep = jnp.concatenate(
            [place <= limit - where_ref[1 + i] * rows for i in range(number)], axis=0
        )
        scores[0] = jnp.where(keep, scores[0], NEG)
        news = [jnp.maximum(tops[t], jnp.max(s, axis=0, keepdims=True)) for t, s in zip(live, scores)]
        ps = [jnp.exp2(s - top).astype(jnp.bfloat16) for s, top in zip(scores, news)]
        for t, top, p in zip(live, news, ps):
            accs[t] = accs[t] * jnp.exp2(tops[t] - top) + dot(v, p, ((1,), (0,)))
            tops[t] = top
    for t in range(tiles):
        if final:
            o = accs[t][16:] * (1.0 / accs[t][0:1])
            o = o.T.astype(jnp.bfloat16)
            for i in range(0, tile, rows):
                low, high = o[i : i + rows // 2], o[i + rows // 2 : i + rows]
                outs[0][4 * t + i // rows] = jnp.concatenate([low, high], axis=1)
        else:
            outs[0][t] = jnp.broadcast_to(tops[t], (8, tile))
            outs[1][t] = accs[t]


def coarse_attend(places, q, parts, state, final):
    heads, rows, _ = q.shape
    tile = 4 * rows
    if final:
        out_shape = jax.ShapeDtypeStruct((heads, rows // 2, PAIR), jnp.bfloat16)
    else:
        out_shape = [
            jax.ShapeDtypeStruct((heads // 4, 8, tile), jnp.float32),
            jax.ShapeDtypeStruct((heads // 4, 16 + HEAD_DIM, tile), jnp.float32),
        ]
    first = state is None
    arrays = [q, *parts] + ([] if first else list(state))
    share = len(parts) / 8
    return pl.pallas_call(
        functools.partial(coarse_kernel, len(parts), first, final),
        in_specs=[pl.BlockSpec(memory_space=pltpu.SMEM)]
        + [pl.BlockSpec(memory_space=pltpu.VMEM)] * len(arrays),
        out_shape=out_shape,
        name="coarse_attend",
        compiler_params=params(),
        cost_estimate=pl.CostEstimate(
            flops=int(share * 6 * 2**30), bytes_accessed=2 * 2**20, transcendentals=int(share * 5 * 2**20)
        ),
    )(jnp.stack(places).astype(jnp.int32), *arrays)


def body(
    tokens,
    fine_query,
    fine_key,
    fine_value,
    fine_out,
    short_weight,
    coarse_query,
    coarse_key,
    coarse_value,
    coarse_out,
):
    count, width = tokens.shape
    bf = jnp.bfloat16
    place = lax.axis_index(ALL).astype(jnp.int32)
    core = lax.axis_index("c").astype(jnp.int32)

    def across(block):
        return lax.ppermute(block, "c", [(0, 1), (1, 0)])

    far = from_behind(tokens, 2)
    mate = across(tokens)
    weights = [fine_key, fine_value.T]
    chip = jnp.concatenate(
        [jnp.where(core == 0, tokens, mate), jnp.where(core == 0, mate, tokens)], axis=0
    )

    def along_x(block, distance):
        return lax.ppermute(block, "x", [(i, (i + distance) % 4) for i in range(4)])

    together = lax.optimization_barrier
    keys, values, query = project(core, chip, [*weights, fine_query])
    state = fine_own(query, keys, values)
    mate_weight = across(short_weight)
    far, state, query, short_weight, mate_weight = together((far, state, query, short_weight, mate_weight))
    near = across(far)
    behind, ahead = along_x(short_weight, 1), along_x(short_weight, 3)
    far_keys, far_values = project(core, far, weights)
    near_keys, near_values = project(core, near, weights)
    where = jnp.stack([core, (place > 1).astype(jnp.int32)])
    fine_mixed = fine_before(where, query, (far_keys, near_keys), (far_values, near_values), state)
    fine_mixed, behind, ahead = together((fine_mixed, behind, ahead))
    two_away = along_x(ahead, 3)
    theirs = across(fine_mixed[1])
    tail = from_behind(tail_project(core, tokens, fine_mixed, theirs, fine_out), 1)
    hidden, natural = out_project(core, tokens, fine_mixed, theirs, fine_out)
    mate_behind, mate_ahead = across(behind), across(ahead)
    hidden, mate_behind, mate_ahead = together((hidden, mate_behind, mate_ahead))
    y = lax.axis_index("y").astype(jnp.int32)

    def along_y(block, distance):
        return lax.ppermute(block, "y", [(i, (i + distance) % 4) for i in range(4)])

    def exchange(blocks, sign):
        return [along_y(block, sign * r) if r > 0 else block for r, block in enumerate(blocks)]

    grouped = exchange(pack(y, hidden, tail), 1)
    *grouped, two_away = together((*grouped, two_away))
    pieces = [short_weight, behind, two_away, ahead, mate_weight, mate_behind, across(two_away), mate_ahead]
    spots_of = [(distance, other) for other in (0, 1) for distance in range(4)]
    where = jnp.stack([lax.axis_index("x").astype(jnp.int32), core])
    partial = exchange(shorten(where, grouped, pieces, spots_of), -1)
    shortened, qkv = coarse_project(partial, coarse_query, coarse_key, coarse_value)
    qkv = lax.all_to_all(qkv, ("z", "x"), 0, 0)
    kv = qkv[:, :, : 2 * HEAD_DIM]
    c = core
    mine = y * 2 + c

    def spot(distance, other=0):
        return ((y + distance) % 4) * 2 + (1 - c if other else c)

    mate_kv = across(kv)
    below, above, beyond = along_y(kv, 1), along_y(kv, 3), along_y(kv, 2)
    state = coarse_attend((mine, mine, spot(0, 1)), qkv, (kv, mate_kv), None, False)
    others = (below, above, beyond)
    state, *others = lax.optimization_barrier((state, *others))
    swapped = [across(block) for block in others]
    state = coarse_attend((mine, spot(3), spot(1), spot(2)), qkv, others, state, False)
    state, *swapped = lax.optimization_barrier((state, *swapped))
    mixed = coarse_attend((mine, spot(3, 1), spot(1, 1), spot(2, 1)), qkv, swapped, state, True)
    mixed = lax.all_to_all(mixed, ("z", "x"), 0, 0)
    return finish(mixed, coarse_out, shortened, natural)


def solution(mesh):
    fine = Mesh(mesh.devices.reshape(4, 4, 4, 2), ALL)
    return jax.shard_map(
        body,
        mesh=fine,
        in_specs=(P(ALL, None), P(), P(), P(), P(), P(("x", "y", "c"), None), P(), P(), P(), P()),
        out_specs=P(ALL, None),
        check_vma=False,
    )
```

```python
import functools
import math

import jax
import jax.numpy as jnp
from jax import lax
from jax.experimental import pallas as pl
from jax.experimental.pallas import tpu as pltpu
from jax.sharding import Mesh, PartitionSpec as P

HEAD_DIM = 64
HEADS = 16
SHORT = 8
WIN = 1024
SCALE = math.log2(math.e) / math.sqrt(HEAD_DIM)
ALL = ("z", "x", "y", "c")
QB = 128
PAIR = 2 * HEAD_DIM
NEG = -1e30


def from_behind(block, distance):
    devices = range(128)
    route = [(i - distance, i) for i in devices if i - distance in devices]
    return lax.ppermute(block, ALL, route)


def normed(rows):
    values = rows.astype(jnp.float32)
    scale = lax.rsqrt(jnp.mean(values * values, axis=-1, keepdims=True) + 1e-06)
    return (values * scale).astype(jnp.bfloat16)


def dot(a, b, contract):
    return lax.dot_general(a, b, (contract, ((), ())), preferred_element_type=jnp.float32)


def params(mib=24):
    return pltpu.CompilerParams(vmem_limit_bytes=mib * 2**20)


def spots(index):
    groups = QB // SHORT
    return (index % groups) * SHORT + index // groups


def two_heads(q_ref, b):
    lane = lax.broadcasted_iota(jnp.int32, (QB, PAIR), 1)
    q = q_ref[b * QB : (b + 1) * QB, :]
    zero = jnp.zeros_like(q)
    return jnp.concatenate(
        [jnp.where(lane < HEAD_DIM, q, zero), jnp.where(lane < HEAD_DIM, zero, q)], axis=0
    )


def with_sums(v):
    return jnp.concatenate([v, jnp.ones((16, v.shape[1]), jnp.bfloat16)], axis=0)


def moves(rows, take):
    col = lax.broadcasted_iota(jnp.int32, (rows, QB), 1)
    row = lax.broadcasted_iota(jnp.int32, (rows, QB), 0)
    return jnp.where(take(row) == col, 1.0, 0.0).astype(jnp.bfloat16)


def reorder(move, rows):
    parts = [dot(move, rows[i : i + QB], ((1,), (0,))) for i in range(0, rows.shape[0], QB)]
    return jnp.concatenate(parts, axis=0)


def project_kernel(number, core_ref, rows_ref, *refs):
    weights, outs = refs[:number], refs[number:]
    rows = normed(rows_ref[...])
    if number == 3:
        rows = reorder(moves(QB, spots), rows).astype(jnp.bfloat16)
        outs[2][...] = (dot(rows, weights[2][...], ((1,), (0,))) * SCALE).astype(jnp.bfloat16)
    outs[0][...] = dot(rows, weights[0][...], ((1,), (0,))).astype(jnp.bfloat16)
    outs[1][...] = dot(weights[1][...], rows, ((1,), (1,))).astype(jnp.bfloat16)


def project(core, rows, weights):
    count, width = rows.shape
    half = width // 2
    tile = 512
    by_row = pl.BlockSpec((tile, half), lambda i, c: (i, 0))
    columns = pl.BlockSpec((width, half), lambda i, c: (0, c[0]))
    number = len(weights)
    return pl.pallas_call(
        functools.partial(project_kernel, number),
        name="project",
        grid_spec=pltpu.PrefetchScalarGridSpec(
            num_scalar_prefetch=1,
            grid=(count // tile,),
            in_specs=[pl.BlockSpec((tile, width), lambda i, c: (i, 0))]
            + [columns, pl.BlockSpec((half, width), lambda i, c: (c[0], 0)), columns][:number],
            out_specs=[by_row, pl.BlockSpec((half, tile), lambda i, c: (0, i)), by_row][:number],
        ),
        out_shape=[
            jax.ShapeDtypeStruct((count, half), jnp.bfloat16),
            jax.ShapeDtypeStruct((half, count), jnp.bfloat16),
            jax.ShapeDtypeStruct((count, half), jnp.bfloat16),
        ][:number],
        compiler_params=params(20),
        cost_estimate=pl.CostEstimate(flops=1, bytes_accessed=1, transcendentals=0),
    )(core.reshape(1), *[rows, *weights])


def tail_project_kernel(core_ref, tokens_ref, mine_ref, theirs_ref, my_ref, their_ref, tail_ref):
    groups = QB // SHORT
    total = dot(moves(16, lambda r: r + QB - SHORT), tokens_ref[...], ((1,), (0,)))
    take = moves(16, lambda r: r * groups + groups - 1)
    mine = dot(take, mine_ref[0], ((1,), (0,))).astype(jnp.bfloat16)
    theirs = dot(take, theirs_ref[...], ((1,), (0,))).astype(jnp.bfloat16)
    total = total + dot(mine, my_ref[...], ((1,), (0,))) + dot(theirs, their_ref[...], ((1,), (0,)))
    tail_ref[...] = total.astype(jnp.bfloat16)


def tail_project(core, tokens, mixed, theirs, weight):
    count, width = tokens.shape
    half = width // 2
    last = count // QB - 1
    tile = width // 2
    return pl.pallas_call(
        tail_project_kernel,
        name="tail_project",
        grid_spec=pltpu.PrefetchScalarGridSpec(
            num_scalar_prefetch=1,
            grid=(2,),
            in_specs=[
                pl.BlockSpec((QB, tile), lambda i, c: (last, i)),
                pl.BlockSpec((1, QB, half), lambda i, c: (0, last, 0)),
                pl.BlockSpec((QB, half), lambda i, c: (last, 0)),
                pl.BlockSpec((half, tile), lambda i, c: (c[0], i)),
                pl.BlockSpec((half, tile), lambda i, c: (1 - c[0], i)),
            ],
            out_specs=pl.BlockSpec((16, tile), lambda i, c: (0, i)),
        ),
        out_shape=jax.ShapeDtypeStruct((16, width), jnp.bfloat16),
        compiler_params=params(20),
    )(core.reshape(1), tokens, mixed, theirs, weight, weight)


def out_project_kernel(core_ref, tokens_ref, mine_ref, theirs_ref, my_ref, their_ref, hidden_ref, natural_ref):
    total = reorder(moves(QB, spots), tokens_ref[...])
    total = total + dot(mine_ref[0], my_ref[...], ((1,), (0,)))
    total = total + dot(theirs_ref[...], their_ref[...], ((1,), (0,)))
    hidden = total.astype(jnp.bfloat16)
    hidden_ref[...] = hidden
    groups = QB // SHORT
    natural_ref[...] = reorder(moves(QB, lambda r: (r % SHORT) * groups + r // SHORT), hidden).astype(jnp.bfloat16)


def out_project(core, tokens, mixed, theirs, weight):
    count, width = tokens.shape
    half = width // 2
    by_column = pl.BlockSpec((count, half), lambda i, c: (0, i))
    return pl.pallas_call(
        out_project_kernel,
        name="out_project",
        grid_spec=pltpu.PrefetchScalarGridSpec(
            num_scalar_prefetch=1,
            grid=(2,),
            in_specs=[
                by_column,
                pl.BlockSpec((1, count, half), lambda i, c: (0, 0, 0)),
                pl.BlockSpec((count, half), lambda i, c: (0, 0)),
                pl.BlockSpec((half, half), lambda i, c: (c[0], i)),
                pl.BlockSpec((half, half), lambda i, c: (1 - c[0], i)),
            ],
            out_specs=[by_column, by_column],
        ),
        out_shape=[jax.ShapeDtypeStruct((count, width), jnp.bfloat16)] * 2,
        compiler_params=params(20),
    )(core.reshape(1), tokens, mixed, theirs, weight, weight)


def pack_kernel(y_ref, hidden_ref, tail_ref, *refs):
    outs, all_ref = refs[:4], refs[4]
    blocks, places, groups, width = hidden_ref.shape
    rows = blocks * groups
    half = width // 2
    for j in range(SHORT):
        p = (j + 1) % SHORT
        part = hidden_ref[:, p].reshape(rows, width)
        if p > 0:
            wide = part.astype(jnp.float32)
            tail = tail_ref[p : p + 1, :].astype(jnp.float32)
            first = lax.broadcasted_iota(jnp.int32, wide.shape, 0) == 0
            wide = jnp.where(first, tail, pltpu.roll(wide, 1, 0))
            part = wide.astype(jnp.bfloat16)
        for f in range(2):
            all_ref[(j % 2) * 2 + f, j // 2] = part[:, f * half : (f + 1) * half]
    for r in range(4):
        outs[r][...] = all_ref[(y_ref[0] + r) % 4]


def pack(y, hidden, tail):
    count, width = hidden.shape
    groups = QB // SHORT
    blocks = count // QB
    shape = (4, count // SHORT, width // 2)
    return pl.pallas_call(
        pack_kernel,
        name="pack",
        in_specs=[pl.BlockSpec(memory_space=pltpu.SMEM)] + [pl.BlockSpec(memory_space=pltpu.VMEM)] * 2,
        out_shape=[jax.ShapeDtypeStruct(shape, jnp.bfloat16)] * 4,
        scratch_shapes=[pltpu.VMEM((4, *shape), jnp.bfloat16)],
        compiler_params=params(),
    )(y.reshape(1), hidden.reshape(blocks, SHORT, groups, width), tail)


def fine_own_kernel(q_ref, k_ref, v_ref, top_ref, acc_ref, s_ref, p_ref):
    blocks = q_ref.shape[0] // QB
    row = lax.broadcasted_iota(jnp.int32, (QB, 2 * QB), 0)
    col = lax.broadcasted_iota(jnp.int32, (QB, 2 * QB), 1) % QB
    keep = spots(row) <= spots(col)
    for b in range(blocks):
        both = two_heads(q_ref, b)
        if b > 0:
            s_ref[b, : b * QB, :] = dot(k_ref[: b * QB, :], both, ((1,), (1,)))
        s = dot(k_ref[b * QB : (b + 1) * QB, :], both, ((1,), (1,)))
        s_ref[b, b * QB : (b + 1) * QB, :] = jnp.where(keep, s, NEG)
    for b in range(blocks):
        end = (b + 1) * QB
        top = jnp.max(s_ref[b, :end, :], axis=0, keepdims=True)
        p_ref[b, :end, :] = jnp.exp2(s_ref[b, :end, :] - top).astype(jnp.bfloat16)
        top_ref[0, b] = jnp.broadcast_to(top, (8, 2 * QB))
    for b in range(blocks):
        end = (b + 1) * QB
        o = dot(with_sums(v_ref[:, :end]), p_ref[b, :end, :], ((1,), (0,)))
        acc_ref[0, b, :16, :] = o[PAIR:]
        acc_ref[0, b, 16:, :QB] = o[:HEAD_DIM, :QB]
        acc_ref[0, b, 16:, QB:] = o[HEAD_DIM:PAIR, QB:]


def fine_before_kernel(
    where_ref, q_ref, kf_ref, kn_ref, vf_ref, vn_ref, top_ref, acc_ref, out_ref, s_ref, p_ref
):
    half = kf_ref.shape[0]
    blocks = q_ref.shape[0] // QB
    core = where_ref[0]
    row = lax.broadcasted_iota(jnp.int32, (QB, 2 * QB), 0)
    col = lax.broadcasted_iota(jnp.int32, (QB, 2 * QB), 1) % QB
    keep = row > spots(col)

    def store(b, total, o):
        o = o * (1.0 / total)
        mixed = jnp.concatenate([o[:, :QB], o[:, QB:]], axis=0)
        at = b * QB // half
        out_ref[(at + core) % 2, b * QB - at * half : (b + 1) * QB - at * half, :] = mixed.T.astype(jnp.bfloat16)

    @pl.when(where_ref[1] == 0)
    def _():
        for b in range(blocks):
            store(b, acc_ref[0, b, 0:1, :], acc_ref[0, b, 16:, :])

    def units(low, high):
        def spans(b):
            if b * QB < half:
                return [(low, b * QB, half - b * QB), (high, 0, half)]
            return [(high, b * QB - half, 2 * half - b * QB)]

        for b in range(blocks):
            both = two_heads(q_ref, b)
            at = b * QB
            for (k_ref, _), first, size in spans(b):
                if at == b * QB:
                    s = dot(k_ref[first : first + QB, :], both, ((1,), (1,)))
                    s_ref[b, at : at + QB, :] = jnp.where(keep, s, NEG)
                    at, first, size = at + QB, first + QB, size - QB
                if size > 0:
                    s_ref[b, at : at + size, :] = dot(k_ref[first : first + size, :], both, ((1,), (1,)))
                at += size
        fades = []
        for b in range(blocks):
            old = top_ref[0, b, 0:1, :]
            top = jnp.maximum(old, jnp.max(s_ref[b, b * QB :, :], axis=0, keepdims=True))
            p_ref[b, b * QB :, :] = jnp.exp2(s_ref[b, b * QB :, :] - top).astype(jnp.bfloat16)
            fades.append(jnp.exp2(old - top))
        for b in range(blocks):
            v = [v_ref[:, first : first + size] for (_, v_ref), first, size in spans(b)]
            o = dot(with_sums(jnp.concatenate(v, axis=1)), p_ref[b, b * QB :, :], ((1,), (0,)))
            acc = acc_ref[0, b] * fades[b]
            new = jnp.concatenate([o[:HEAD_DIM, :QB], o[HEAD_DIM:PAIR, QB:]], axis=1)
            store(b, acc[0:1] + o[PAIR : PAIR + 1], acc[16:] + new)

    @pl.when((where_ref[1] > 0) & (core == 0))
    def _():
        units((kf_ref, vf_ref), (kn_ref, vn_ref))

    @pl.when((where_ref[1] > 0) & (core == 1))
    def _():
        units((kn_ref, vn_ref), (kf_ref, vf_ref))


def fine_own(q, k, v):
    count, width = q.shape
    blocks = count // QB
    pairs = width // PAIR
    return pl.pallas_call(
        fine_own_kernel,
        name="fine_own",
        grid=(pairs,),
        in_specs=[
            pl.BlockSpec((count, PAIR), lambda i: (0, i)),
            pl.BlockSpec((count, PAIR), lambda i: (0, i)),
            pl.BlockSpec((PAIR, count), lambda i: (i, 0)),
        ],
        out_specs=[
            pl.BlockSpec((1, blocks, 8, 2 * QB), lambda i: (i, 0, 0, 0)),
            pl.BlockSpec((1, blocks, 16 + HEAD_DIM, 2 * QB), lambda i: (i, 0, 0, 0)),
        ],
        out_shape=[
            jax.ShapeDtypeStruct((pairs, blocks, 8, 2 * QB), jnp.float32),
            jax.ShapeDtypeStruct((pairs, blocks, 16 + HEAD_DIM, 2 * QB), jnp.float32),
        ],
        scratch_shapes=[
            pltpu.VMEM((blocks, count, 2 * QB), jnp.float32),
            pltpu.VMEM((blocks, count, 2 * QB), jnp.bfloat16),
        ],
        compiler_params=params(),
        cost_estimate=pl.CostEstimate(flops=1, bytes_accessed=1, transcendentals=0),
    )(q, k, v)


def fine_before(where, q, keys, values, state):
    count, width = q.shape
    blocks = count // QB
    half = count // 2
    return pl.pallas_call(
        fine_before_kernel,
        name="fine_before",
        grid=(width // PAIR,),
        in_specs=[pl.BlockSpec(memory_space=pltpu.SMEM), pl.BlockSpec((count, PAIR), lambda i: (0, i))]
        + [pl.BlockSpec((half, PAIR), lambda i: (0, i))] * 2
        + [pl.BlockSpec((PAIR, half), lambda i: (i, 0))] * 2
        + [
            pl.BlockSpec((1, blocks, 8, 2 * QB), lambda i: (i, 0, 0, 0)),
            pl.BlockSpec((1, blocks, 16 + HEAD_DIM, 2 * QB), lambda i: (i, 0, 0, 0)),
        ],
        out_specs=pl.BlockSpec((2, half, PAIR), lambda i: (0, 0, i)),
        out_shape=jax.ShapeDtypeStruct((2, half, width), jnp.bfloat16),
        scratch_shapes=[
            pltpu.VMEM((blocks, count, 2 * QB), jnp.float32),
            pltpu.VMEM((blocks, count, 2 * QB), jnp.bfloat16),
        ],
        compiler_params=params(),
        cost_estimate=pl.CostEstimate(flops=1, bytes_accessed=1, transcendentals=0),
    )(where, q, *keys, *values, *state)


def shorten_kernel(spots_of, where_ref, *refs):
    grouped, pieces, outs = refs[:4], refs[4:-4], refs[-4:]
    parts, rows, depth = grouped[0].shape
    total = None
    for (distance, other), piece in zip(spots_of, pieces):
        size = piece.shape[0]
        x = (where_ref[0] + parts - distance) % parts
        core = 1 - where_ref[1] if other else where_ref[1]
        columns = pl.ds(pl.multiple_of(core * size, size), size)
        part = jnp.concatenate([ref[x, :, columns] for ref in grouped], axis=0)
        term = dot(part, piece[...], ((1,), (0,)))
        total = term if total is None else total + term
    for r in range(4):
        outs[r][...] = total[r * rows : (r + 1) * rows].astype(jnp.bfloat16)


def shorten(where, grouped, pieces, spots_of):
    parts, rows, depth = grouped[0].shape
    width = pieces[0].shape[1]
    tile = width // 2
    return pl.pallas_call(
        functools.partial(shorten_kernel, spots_of),
        name="shorten",
        grid=(2,),
        in_specs=[pl.BlockSpec(memory_space=pltpu.SMEM)]
        + [pl.BlockSpec(grouped[0].shape, lambda i: (0, 0, 0))] * 4
        + [pl.BlockSpec((piece.shape[0], tile), lambda i: (0, i)) for piece in pieces],
        out_specs=[pl.BlockSpec((rows, tile), lambda i: (0, i))] * 4,
        out_shape=[jax.ShapeDtypeStruct((rows, width), jnp.bfloat16)] * 4,
        compiler_params=params(60),
    )(where, *grouped, *pieces)


def coarse_project_kernel(*refs):
    parts, (k_ref, v_ref, q_ref, short_ref, qkv_ref, weight_ref, sems) = refs[:4], refs[4:]
    copies = [
        pltpu.make_async_copy(ref, weight_ref.at[i], sems.at[i])
        for i, ref in enumerate((k_ref, v_ref, q_ref))
    ]
    for copy in copies:
        copy.start()
    short = sum(ref[...].astype(jnp.float32) for ref in parts).astype(jnp.bfloat16)
    short_ref[...] = short
    rows = normed(short)
    for i, copy in enumerate(copies):
        copy.wait()
        out = dot(rows, weight_ref[i], ((1,), (0,)))
        if i == 2:
            out = out * SCALE
        out = out.astype(jnp.bfloat16)
        for h in range(HEADS):
            qkv_ref[h, :, i * HEAD_DIM : (i + 1) * HEAD_DIM] = out[:, h * HEAD_DIM : (h + 1) * HEAD_DIM]


def coarse_project(partial, query, key, value):
    rows, width = partial[0].shape
    vmem = pl.BlockSpec(memory_space=pltpu.VMEM)
    return pl.pallas_call(
        coarse_project_kernel,
        name="coarse_project",
        in_specs=[vmem] * 4 + [pl.BlockSpec(memory_space=pl.ANY)] * 3,
        out_specs=[vmem] * 2,
        out_shape=[
            jax.ShapeDtypeStruct((rows, width), jnp.bfloat16),
            jax.ShapeDtypeStruct((HEADS, rows, 3 * HEAD_DIM), jnp.bfloat16),
        ],
        scratch_shapes=[
            pltpu.VMEM((3, width, width), jnp.bfloat16),
            pltpu.SemaphoreType.DMA((3,)),
        ],
        compiler_params=params(60),
    )(*partial, key, value, query)


def finish_kernel(mixed_ref, out_weight_ref, short_ref, hidden_ref, out_ref, rows_ref):
    heads, rows, _ = mixed_ref.shape
    rows = 2 * rows

    @pl.when(pl.program_id(0) == 0)
    def _():
        for h in range(heads):
            m = mixed_ref[h]
            rows_ref[:, h * HEAD_DIM : (h + 1) * HEAD_DIM] = jnp.concatenate(
                [m[:, :HEAD_DIM], m[:, HEAD_DIM:]], axis=0
            )

    refined = short_ref[...].astype(jnp.float32) + dot(rows_ref[...], out_weight_ref[...], ((1,), (0,)))
    tile = refined.shape[1]
    spread = jnp.broadcast_to(refined[:, None, :], (rows, SHORT, tile)).reshape(rows * SHORT, tile)
    out_ref[...] = (hidden_ref[...].astype(jnp.float32) + spread).astype(jnp.bfloat16)


def finish(mixed, out_weight, short, hidden):
    count, width = hidden.shape
    rows = count // SHORT
    tile = width // 2
    return pl.pallas_call(
        finish_kernel,
        name="finish",
        grid=(2,),
        in_specs=[
            pl.BlockSpec(mixed.shape, lambda i: (0, 0, 0)),
            pl.BlockSpec((width, tile), lambda i: (0, i)),
            pl.BlockSpec((rows, tile), lambda i: (0, i)),
            pl.BlockSpec((count, tile), lambda i: (0, i)),
        ],
        out_specs=pl.BlockSpec((count, tile), lambda i: (0, i)),
        out_shape=jax.ShapeDtypeStruct((count, width), jnp.bfloat16),
        scratch_shapes=[pltpu.VMEM((rows, width), jnp.bfloat16)],
        compiler_params=params(60),
    )(mixed, out_weight, short, hidden)


def coarse_kernel(number, first, final, where_ref, q_ref, *refs):
    parts = refs[:number]
    old = None if first else refs[number : number + 2]
    outs = refs[number if first else number + 2 :]
    blocks, rows, _ = parts[0].shape
    tile = 4 * rows
    tiles = blocks // 4
    lane = lax.broadcasted_iota(jnp.int32, (1, tile), 1)
    row = lax.broadcasted_iota(jnp.int32, (tile, tile), 0)
    stride = 8 * rows
    place = (row // rows) * stride + row % rows
    limit = (lane // rows) * stride + where_ref[0] * rows + lane % rows
    ones = jnp.ones((16, number * tile), jnp.bfloat16)
    queries = []
    for t in range(tiles):
        q = q_ref[4 * t : 4 * t + 4, :, 2 * HEAD_DIM :].reshape(tile, HEAD_DIM)
        queries.append(jnp.concatenate([q, jnp.zeros_like(q)], axis=1))
    if first:
        tops = [jnp.full((1, tile), NEG, jnp.float32)] * tiles
        accs = [jnp.zeros((16 + HEAD_DIM, tile), jnp.float32)] * tiles
    else:
        tops = [old[0][t, 0:1, :] for t in range(tiles)]
        accs = [old[1][t] for t in range(tiles)]
    for g in range(tiles):
        kv = jnp.concatenate([part[4 * g : 4 * g + 4].reshape(tile, PAIR) for part in parts], axis=0)
        v = jnp.concatenate([ones, kv.T[HEAD_DIM:, :]], axis=0)
        live = range(g, tiles)
        scores = [dot(kv, queries[t], ((1,), (1,))) for t in live]
        keep = jnp.concatenate(
            [place <= limit - where_ref[1 + i] * rows for i in range(number)], axis=0
        )
        scores[0] = jnp.where(keep, scores[0], NEG)
        news = [jnp.maximum(tops[t], jnp.max(s, axis=0, keepdims=True)) for t, s in zip(live, scores)]
        ps = [jnp.exp2(s - top).astype(jnp.bfloat16) for s, top in zip(scores, news)]
        for t, top, p in zip(live, news, ps):
            accs[t] = accs[t] * jnp.exp2(tops[t] - top) + dot(v, p, ((1,), (0,)))
            tops[t] = top
    for t in range(tiles):
        if final:
            o = accs[t][16:] * (1.0 / accs[t][0:1])
            o = o.T.astype(jnp.bfloat16)
            for i in range(0, tile, rows):
                low, high = o[i : i + rows // 2], o[i + rows // 2 : i + rows]
                outs[0][4 * t + i // rows] = jnp.concatenate([low, high], axis=1)
        else:
            outs[0][t] = jnp.broadcast_to(tops[t], (8, tile))
            outs[1][t] = accs[t]


def coarse_attend(places, q, parts, state, final):
    heads, rows, _ = q.shape
    tile = 4 * rows
    if final:
        out_shape = jax.ShapeDtypeStruct((heads, rows // 2, PAIR), jnp.bfloat16)
    else:
        out_shape = [
            jax.ShapeDtypeStruct((heads // 4, 8, tile), jnp.float32),
            jax.ShapeDtypeStruct((heads // 4, 16 + HEAD_DIM, tile), jnp.float32),
        ]
    first = state is None
    arrays = [q, *parts] + ([] if first else list(state))
    return pl.pallas_call(
        functools.partial(coarse_kernel, len(parts), first, final),
        in_specs=[pl.BlockSpec(memory_space=pltpu.SMEM)]
        + [pl.BlockSpec(memory_space=pltpu.VMEM)] * len(arrays),
        out_shape=out_shape,
        name="coarse_attend",
        compiler_params=params(),
        cost_estimate=pl.CostEstimate(flops=1, bytes_accessed=1, transcendentals=0),
    )(jnp.stack(places).astype(jnp.int32), *arrays)


def body(
    tokens,
    fine_query,
    fine_key,
    fine_value,
    fine_out,
    short_weight,
    coarse_query,
    coarse_key,
    coarse_value,
    coarse_out,
):
    count, width = tokens.shape
    bf = jnp.bfloat16
    place = lax.axis_index(ALL).astype(jnp.int32)
    core = lax.axis_index("c").astype(jnp.int32)

    def across(block):
        return lax.ppermute(block, "c", [(0, 1), (1, 0)])

    far = from_behind(tokens, 2)
    mate = across(tokens)
    weights = [fine_key, fine_value.T]
    chip = jnp.concatenate(
        [jnp.where(core == 0, tokens, mate), jnp.where(core == 0, mate, tokens)], axis=0
    )

    def along_x(block, distance):
        return lax.ppermute(block, "x", [(i, (i + distance) % 4) for i in range(4)])

    together = lax.optimization_barrier
    keys, values, query = project(core, chip, [*weights, fine_query])
    state = fine_own(query, keys, values)
    mate_weight = across(short_weight)
    far, state, query, short_weight, mate_weight = together((far, state, query, short_weight, mate_weight))
    near = across(far)
    behind, ahead = along_x(short_weight, 1), along_x(short_weight, 3)
    far_keys, far_values = project(core, far, weights)
    near_keys, near_values = project(core, near, weights)
    where = jnp.stack([core, (place > 1).astype(jnp.int32)])
    fine_mixed = fine_before(where, query, (far_keys, near_keys), (far_values, near_values), state)
    fine_mixed, behind, ahead = together((fine_mixed, behind, ahead))
    two_away = along_x(ahead, 3)
    theirs = across(fine_mixed[1])
    tail = from_behind(tail_project(core, tokens, fine_mixed, theirs, fine_out), 1)
    hidden, natural = out_project(core, tokens, fine_mixed, theirs, fine_out)
    mate_behind, mate_ahead = across(behind), across(ahead)
    hidden, mate_behind, mate_ahead = together((hidden, mate_behind, mate_ahead))
    y = lax.axis_index("y").astype(jnp.int32)

    def along_y(block, distance):
        return lax.ppermute(block, "y", [(i, (i + distance) % 4) for i in range(4)])

    def exchange(blocks, sign):
        return [along_y(block, sign * r) if r > 0 else block for r, block in enumerate(blocks)]

    grouped = exchange(pack(y, hidden, tail), 1)
    *grouped, two_away = together((*grouped, two_away))
    pieces = [short_weight, behind, two_away, ahead, mate_weight, mate_behind, across(two_away), mate_ahead]
    spots_of = [(distance, other) for other in (0, 1) for distance in range(4)]
    where = jnp.stack([lax.axis_index("x").astype(jnp.int32), core])
    partial = exchange(shorten(where, grouped, pieces, spots_of), -1)
    shortened, qkv = coarse_project(partial, coarse_query, coarse_key, coarse_value)
    qkv = lax.all_to_all(qkv, ("z", "x"), 0, 0)
    kv = qkv[:, :, : 2 * HEAD_DIM]
    c = core
    mine = y * 2 + c

    def spot(distance, other=0):
        return ((y + distance) % 4) * 2 + (1 - c if other else c)

    mate_kv = across(kv)
    below, above, beyond = along_y(kv, 1), along_y(kv, 3), along_y(kv, 2)
    state = coarse_attend((mine, mine, spot(0, 1)), qkv, (kv, mate_kv), None, False)
    state, below, above = together((state, below, above))
    state = coarse_attend((mine, spot(3), spot(1)), qkv, (below, above), state, False)
    mate_below, mate_above = across(below), across(above)
    state, beyond, mate_below, mate_above = together((state, beyond, mate_below, mate_above))
    places = (mine, spot(3, 1), spot(1, 1), spot(2), spot(2, 1))
    parts = (mate_below, mate_above, beyond, across(beyond))
    mixed = coarse_attend(places, qkv, parts, state, True)
    mixed = lax.all_to_all(mixed, ("z", "x"), 0, 0)
    return finish(mixed, coarse_out, shortened, natural)


def solution(mesh):
    fine = Mesh(mesh.devices.reshape(4, 4, 4, 2), ALL)
    return jax.shard_map(
        body,
        mesh=fine,
        in_specs=(P(ALL, None), P(), P(), P(), P(), P(("x", "y", "c"), None), P(), P(), P(), P()),
        out_specs=P(ALL, None),
        check_vma=False,
    )
```

```python
import functools
import math

import jax
import jax.numpy as jnp
from jax import lax
from jax.experimental import pallas as pl
from jax.experimental.pallas import tpu as pltpu
from jax.sharding import Mesh, PartitionSpec as P

HEAD_DIM = 64
HEADS = 16
SHORT = 8
WIN = 1024
SCALE = math.log2(math.e) / math.sqrt(HEAD_DIM)
ALL = ("z", "x", "y", "c")
QB = 128
PAIR = 2 * HEAD_DIM
NEG = -1e30


def from_behind(block, distance):
    devices = range(128)
    route = [(i - distance, i) for i in devices if i - distance in devices]
    return lax.ppermute(block, ALL, route)


def normed(rows):
    values = rows.astype(jnp.float32)
    scale = lax.rsqrt(jnp.mean(values * values, axis=-1, keepdims=True) + 1e-06)
    return (values * scale).astype(jnp.bfloat16)


def dot(a, b, contract):
    return lax.dot_general(a, b, (contract, ((), ())), preferred_element_type=jnp.float32)


def params(mib=24):
    return pltpu.CompilerParams(vmem_limit_bytes=mib * 2**20)


def spots(index):
    groups = QB // SHORT
    return (index % groups) * SHORT + index // groups


def two_heads(q_ref, b):
    lane = lax.broadcasted_iota(jnp.int32, (QB, PAIR), 1)
    q = q_ref[b * QB : (b + 1) * QB, :]
    zero = jnp.zeros_like(q)
    return jnp.concatenate(
        [jnp.where(lane < HEAD_DIM, q, zero), jnp.where(lane < HEAD_DIM, zero, q)], axis=0
    )


def with_sums(v):
    return jnp.concatenate([v, jnp.ones((16, v.shape[1]), jnp.bfloat16)], axis=0)


def moves(rows, take):
    col = lax.broadcasted_iota(jnp.int32, (rows, QB), 1)
    row = lax.broadcasted_iota(jnp.int32, (rows, QB), 0)
    return jnp.where(take(row) == col, 1.0, 0.0).astype(jnp.bfloat16)


def reorder(move, rows):
    parts = [dot(move, rows[i : i + QB], ((1,), (0,))) for i in range(0, rows.shape[0], QB)]
    return jnp.concatenate(parts, axis=0)


def project_kernel(number, core_ref, rows_ref, *refs):
    weights, outs = refs[:number], refs[number:]
    rows = normed(rows_ref[...])
    if number == 3:
        rows = reorder(moves(QB, spots), rows).astype(jnp.bfloat16)
        outs[2][...] = (dot(rows, weights[2][...], ((1,), (0,))) * SCALE).astype(jnp.bfloat16)
    outs[0][...] = dot(rows, weights[0][...], ((1,), (0,))).astype(jnp.bfloat16)
    outs[1][...] = dot(weights[1][...], rows, ((1,), (1,))).astype(jnp.bfloat16)


def project(core, rows, weights):
    count, width = rows.shape
    half = width // 2
    tile = 512
    by_row = pl.BlockSpec((tile, half), lambda i, c: (i, 0))
    columns = pl.BlockSpec((width, half), lambda i, c: (0, c[0]))
    number = len(weights)
    return pl.pallas_call(
        functools.partial(project_kernel, number),
        name="project",
        grid_spec=pltpu.PrefetchScalarGridSpec(
            num_scalar_prefetch=1,
            grid=(count // tile,),
            in_specs=[pl.BlockSpec((tile, width), lambda i, c: (i, 0))]
            + [columns, pl.BlockSpec((half, width), lambda i, c: (c[0], 0)), columns][:number],
            out_specs=[by_row, pl.BlockSpec((half, tile), lambda i, c: (0, i)), by_row][:number],
        ),
        out_shape=[
            jax.ShapeDtypeStruct((count, half), jnp.bfloat16),
            jax.ShapeDtypeStruct((half, count), jnp.bfloat16),
            jax.ShapeDtypeStruct((count, half), jnp.bfloat16),
        ][:number],
        compiler_params=params(20),
        cost_estimate=pl.CostEstimate(flops=1, bytes_accessed=1, transcendentals=0),
    )(core.reshape(1), *[rows, *weights])


def tail_project_kernel(core_ref, tokens_ref, mine_ref, theirs_ref, my_ref, their_ref, tail_ref):
    groups = QB // SHORT
    total = dot(moves(16, lambda r: r + QB - SHORT), tokens_ref[...], ((1,), (0,)))
    take = moves(16, lambda r: r * groups + groups - 1)
    mine = dot(take, mine_ref[0], ((1,), (0,))).astype(jnp.bfloat16)
    theirs = dot(take, theirs_ref[...], ((1,), (0,))).astype(jnp.bfloat16)
    total = total + dot(mine, my_ref[...], ((1,), (0,))) + dot(theirs, their_ref[...], ((1,), (0,)))
    tail_ref[...] = total.astype(jnp.bfloat16)


def tail_project(core, tokens, mixed, theirs, weight):
    count, width = tokens.shape
    half = width // 2
    last = count // QB - 1
    tile = width // 2
    return pl.pallas_call(
        tail_project_kernel,
        name="tail_project",
        grid_spec=pltpu.PrefetchScalarGridSpec(
            num_scalar_prefetch=1,
            grid=(2,),
            in_specs=[
                pl.BlockSpec((QB, tile), lambda i, c: (last, i)),
                pl.BlockSpec((1, QB, half), lambda i, c: (0, last, 0)),
                pl.BlockSpec((QB, half), lambda i, c: (last, 0)),
                pl.BlockSpec((half, tile), lambda i, c: (c[0], i)),
                pl.BlockSpec((half, tile), lambda i, c: (1 - c[0], i)),
            ],
            out_specs=pl.BlockSpec((16, tile), lambda i, c: (0, i)),
        ),
        out_shape=jax.ShapeDtypeStruct((16, width), jnp.bfloat16),
        compiler_params=params(20),
    )(core.reshape(1), tokens, mixed, theirs, weight, weight)


def out_project_kernel(core_ref, tokens_ref, mine_ref, theirs_ref, my_ref, their_ref, hidden_ref, natural_ref):
    total = reorder(moves(QB, spots), tokens_ref[...])
    total = total + dot(mine_ref[0], my_ref[...], ((1,), (0,)))
    total = total + dot(theirs_ref[...], their_ref[...], ((1,), (0,)))
    hidden = total.astype(jnp.bfloat16)
    hidden_ref[...] = hidden
    groups = QB // SHORT
    natural_ref[...] = reorder(moves(QB, lambda r: (r % SHORT) * groups + r // SHORT), hidden).astype(jnp.bfloat16)


def out_project(core, tokens, mixed, theirs, weight):
    count, width = tokens.shape
    half = width // 2
    by_column = pl.BlockSpec((count, half), lambda i, c: (0, i))
    return pl.pallas_call(
        out_project_kernel,
        name="out_project",
        grid_spec=pltpu.PrefetchScalarGridSpec(
            num_scalar_prefetch=1,
            grid=(2,),
            in_specs=[
                by_column,
                pl.BlockSpec((1, count, half), lambda i, c: (0, 0, 0)),
                pl.BlockSpec((count, half), lambda i, c: (0, 0)),
                pl.BlockSpec((half, half), lambda i, c: (c[0], i)),
                pl.BlockSpec((half, half), lambda i, c: (1 - c[0], i)),
            ],
            out_specs=[by_column, by_column],
        ),
        out_shape=[jax.ShapeDtypeStruct((count, width), jnp.bfloat16)] * 2,
        compiler_params=params(20),
    )(core.reshape(1), tokens, mixed, theirs, weight, weight)


def pack_kernel(y_ref, hidden_ref, tail_ref, *refs):
    outs, all_ref = refs[:4], refs[4]
    blocks, places, groups, width = hidden_ref.shape
    rows = blocks * groups
    half = width // 2
    for j in range(SHORT):
        p = (j + 1) % SHORT
        part = hidden_ref[:, p].reshape(rows, width)
        if p > 0:
            wide = part.astype(jnp.float32)
            tail = tail_ref[p : p + 1, :].astype(jnp.float32)
            first = lax.broadcasted_iota(jnp.int32, wide.shape, 0) == 0
            wide = jnp.where(first, tail, pltpu.roll(wide, 1, 0))
            part = wide.astype(jnp.bfloat16)
        for f in range(2):
            all_ref[(j % 2) * 2 + f, j // 2] = part[:, f * half : (f + 1) * half]
    for r in range(4):
        outs[r][...] = all_ref[(y_ref[0] + r) % 4]


def pack(y, hidden, tail):
    count, width = hidden.shape
    groups = QB // SHORT
    blocks = count // QB
    shape = (4, count // SHORT, width // 2)
    return pl.pallas_call(
        pack_kernel,
        name="pack",
        in_specs=[pl.BlockSpec(memory_space=pltpu.SMEM)] + [pl.BlockSpec(memory_space=pltpu.VMEM)] * 2,
        out_shape=[jax.ShapeDtypeStruct(shape, jnp.bfloat16)] * 4,
        scratch_shapes=[pltpu.VMEM((4, *shape), jnp.bfloat16)],
        compiler_params=params(),
    )(y.reshape(1), hidden.reshape(blocks, SHORT, groups, width), tail)


def fine_own_kernel(q_ref, k_ref, v_ref, top_ref, acc_ref, s_ref, p_ref):
    blocks = q_ref.shape[0] // QB
    row = lax.broadcasted_iota(jnp.int32, (QB, 2 * QB), 0)
    col = lax.broadcasted_iota(jnp.int32, (QB, 2 * QB), 1) % QB
    keep = spots(row) <= spots(col)
    for b in range(blocks):
        both = two_heads(q_ref, b)
        if b > 0:
            s_ref[b, : b * QB, :] = dot(k_ref[: b * QB, :], both, ((1,), (1,)))
        s = dot(k_ref[b * QB : (b + 1) * QB, :], both, ((1,), (1,)))
        s_ref[b, b * QB : (b + 1) * QB, :] = jnp.where(keep, s, NEG)
    for b in range(blocks):
        end = (b + 1) * QB
        top = jnp.max(s_ref[b, :end, :], axis=0, keepdims=True)
        p_ref[b, :end, :] = jnp.exp2(s_ref[b, :end, :] - top).astype(jnp.bfloat16)
        top_ref[0, b] = jnp.broadcast_to(top, (8, 2 * QB))
    for b in range(blocks):
        end = (b + 1) * QB
        o = dot(with_sums(v_ref[:, :end]), p_ref[b, :end, :], ((1,), (0,)))
        acc_ref[0, b, :16, :] = o[PAIR:]
        acc_ref[0, b, 16:, :QB] = o[:HEAD_DIM, :QB]
        acc_ref[0, b, 16:, QB:] = o[HEAD_DIM:PAIR, QB:]


def fine_before_kernel(
    where_ref, q_ref, kf_ref, kn_ref, vf_ref, vn_ref, top_ref, acc_ref, out_ref, s_ref, p_ref
):
    half = kf_ref.shape[0]
    blocks = q_ref.shape[0] // QB
    core = where_ref[0]
    row = lax.broadcasted_iota(jnp.int32, (QB, 2 * QB), 0)
    col = lax.broadcasted_iota(jnp.int32, (QB, 2 * QB), 1) % QB
    keep = row > spots(col)

    def store(b, total, o):
        o = o * (1.0 / total)
        mixed = jnp.concatenate([o[:, :QB], o[:, QB:]], axis=0)
        at = b * QB // half
        out_ref[(at + core) % 2, b * QB - at * half : (b + 1) * QB - at * half, :] = mixed.astype(jnp.bfloat16).T

    @pl.when(where_ref[1] == 0)
    def _():
        for b in range(blocks):
            store(b, acc_ref[0, b, 0:1, :], acc_ref[0, b, 16:, :])

    def units(low, high):
        def spans(b):
            if b * QB < half:
                return [(low, b * QB, half - b * QB), (high, 0, half)]
            return [(high, b * QB - half, 2 * half - b * QB)]

        for b in range(blocks):
            both = two_heads(q_ref, b)
            at = b * QB
            for (k_ref, _), first, size in spans(b):
                if at == b * QB:
                    s = dot(k_ref[first : first + QB, :], both, ((1,), (1,)))
                    s_ref[b, at : at + QB, :] = jnp.where(keep, s, NEG)
                    at, first, size = at + QB, first + QB, size - QB
                if size > 0:
                    s_ref[b, at : at + size, :] = dot(k_ref[first : first + size, :], both, ((1,), (1,)))
                at += size
        fades = []
        for b in range(blocks):
            old = top_ref[0, b, 0:1, :]
            top = jnp.maximum(old, jnp.max(s_ref[b, b * QB :, :], axis=0, keepdims=True))
            p_ref[b, b * QB :, :] = jnp.exp2(s_ref[b, b * QB :, :] - top).astype(jnp.bfloat16)
            fades.append(jnp.exp2(old - top))
        for b in range(blocks):
            v = [v_ref[:, first : first + size] for (_, v_ref), first, size in spans(b)]
            o = dot(with_sums(jnp.concatenate(v, axis=1)), p_ref[b, b * QB :, :], ((1,), (0,)))
            acc = acc_ref[0, b] * fades[b]
            new = jnp.concatenate([o[:HEAD_DIM, :QB], o[HEAD_DIM:PAIR, QB:]], axis=1)
            store(b, acc[0:1] + o[PAIR : PAIR + 1], acc[16:] + new)

    @pl.when((where_ref[1] > 0) & (core == 0))
    def _():
        units((kf_ref, vf_ref), (kn_ref, vn_ref))

    @pl.when((where_ref[1] > 0) & (core == 1))
    def _():
        units((kn_ref, vn_ref), (kf_ref, vf_ref))


def fine_own(q, k, v):
    count, width = q.shape
    blocks = count // QB
    pairs = width // PAIR
    return pl.pallas_call(
        fine_own_kernel,
        name="fine_own",
        grid=(pairs,),
        in_specs=[
            pl.BlockSpec((count, PAIR), lambda i: (0, i)),
            pl.BlockSpec((count, PAIR), lambda i: (0, i)),
            pl.BlockSpec((PAIR, count), lambda i: (i, 0)),
        ],
        out_specs=[
            pl.BlockSpec((1, blocks, 8, 2 * QB), lambda i: (i, 0, 0, 0)),
            pl.BlockSpec((1, blocks, 16 + HEAD_DIM, 2 * QB), lambda i: (i, 0, 0, 0)),
        ],
        out_shape=[
            jax.ShapeDtypeStruct((pairs, blocks, 8, 2 * QB), jnp.float32),
            jax.ShapeDtypeStruct((pairs, blocks, 16 + HEAD_DIM, 2 * QB), jnp.float32),
        ],
        scratch_shapes=[
            pltpu.VMEM((blocks, count, 2 * QB), jnp.float32),
            pltpu.VMEM((blocks, count, 2 * QB), jnp.bfloat16),
        ],
        compiler_params=params(),
        cost_estimate=pl.CostEstimate(flops=1, bytes_accessed=1, transcendentals=0),
    )(q, k, v)


def fine_before(where, q, keys, values, state):
    count, width = q.shape
    blocks = count // QB
    half = count // 2
    return pl.pallas_call(
        fine_before_kernel,
        name="fine_before",
        grid=(width // PAIR,),
        in_specs=[pl.BlockSpec(memory_space=pltpu.SMEM), pl.BlockSpec((count, PAIR), lambda i: (0, i))]
        + [pl.BlockSpec((half, PAIR), lambda i: (0, i))] * 2
        + [pl.BlockSpec((PAIR, half), lambda i: (i, 0))] * 2
        + [
            pl.BlockSpec((1, blocks, 8, 2 * QB), lambda i: (i, 0, 0, 0)),
            pl.BlockSpec((1, blocks, 16 + HEAD_DIM, 2 * QB), lambda i: (i, 0, 0, 0)),
        ],
        out_specs=pl.BlockSpec((2, half, PAIR), lambda i: (0, 0, i)),
        out_shape=jax.ShapeDtypeStruct((2, half, width), jnp.bfloat16),
        scratch_shapes=[
            pltpu.VMEM((blocks, count, 2 * QB), jnp.float32),
            pltpu.VMEM((blocks, count, 2 * QB), jnp.bfloat16),
        ],
        compiler_params=params(),
        cost_estimate=pl.CostEstimate(flops=1, bytes_accessed=1, transcendentals=0),
    )(where, q, *keys, *values, *state)


def shorten_kernel(spots_of, where_ref, *refs):
    grouped, pieces, outs = refs[:4], refs[4:-4], refs[-4:]
    parts, rows, depth = grouped[0].shape
    total = None
    for (distance, other), piece in zip(spots_of, pieces):
        size = piece.shape[0]
        x = (where_ref[0] + parts - distance) % parts
        core = 1 - where_ref[1] if other else where_ref[1]
        columns = pl.ds(pl.multiple_of(core * size, size), size)
        part = jnp.concatenate([ref[x, :, columns] for ref in grouped], axis=0)
        term = dot(part, piece[...], ((1,), (0,)))
        total = term if total is None else total + term
    for r in range(4):
        outs[r][...] = total[r * rows : (r + 1) * rows].astype(jnp.bfloat16)


def shorten(where, grouped, pieces, spots_of):
    parts, rows, depth = grouped[0].shape
    width = pieces[0].shape[1]
    tile = width // 2
    return pl.pallas_call(
        functools.partial(shorten_kernel, spots_of),
        name="shorten",
        grid=(2,),
        in_specs=[pl.BlockSpec(memory_space=pltpu.SMEM)]
        + [pl.BlockSpec(grouped[0].shape, lambda i: (0, 0, 0))] * 4
        + [pl.BlockSpec((piece.shape[0], tile), lambda i: (0, i)) for piece in pieces],
        out_specs=[pl.BlockSpec((rows, tile), lambda i: (0, i))] * 4,
        out_shape=[jax.ShapeDtypeStruct((rows, width), jnp.bfloat16)] * 4,
        compiler_params=params(60),
    )(where, *grouped, *pieces)


def coarse_project_kernel(*refs):
    parts, (k_ref, v_ref, q_ref, short_ref, qkv_ref, weight_ref, sems) = refs[:4], refs[4:]
    copies = [
        pltpu.make_async_copy(ref, weight_ref.at[i], sems.at[i])
        for i, ref in enumerate((k_ref, v_ref, q_ref))
    ]
    for copy in copies:
        copy.start()
    short = sum(ref[...].astype(jnp.float32) for ref in parts).astype(jnp.bfloat16)
    short_ref[...] = short
    rows = normed(short)
    for i, copy in enumerate(copies):
        copy.wait()
        out = dot(rows, weight_ref[i], ((1,), (0,)))
        if i == 2:
            out = out * SCALE
        out = out.astype(jnp.bfloat16)
        count = out.shape[0]
        for h in range(HEADS):
            head = out[:, h * HEAD_DIM : (h + 1) * HEAD_DIM]
            if i < 2:
                qkv_ref[h, :count, i * HEAD_DIM : (i + 1) * HEAD_DIM] = head
            else:
                qkv_ref[h, count:, :HEAD_DIM] = head[: count // 2]
                qkv_ref[h, count:, HEAD_DIM:] = head[count // 2 :]


def coarse_project(partial, query, key, value):
    rows, width = partial[0].shape
    vmem = pl.BlockSpec(memory_space=pltpu.VMEM)
    return pl.pallas_call(
        coarse_project_kernel,
        name="coarse_project",
        in_specs=[vmem] * 4 + [pl.BlockSpec(memory_space=pl.ANY)] * 3,
        out_specs=[vmem] * 2,
        out_shape=[
            jax.ShapeDtypeStruct((rows, width), jnp.bfloat16),
            jax.ShapeDtypeStruct((HEADS, rows + rows // 2, PAIR), jnp.bfloat16),
        ],
        scratch_shapes=[
            pltpu.VMEM((3, width, width), jnp.bfloat16),
            pltpu.SemaphoreType.DMA((3,)),
        ],
        compiler_params=params(60),
    )(*partial, key, value, query)


def finish_kernel(mixed_ref, out_weight_ref, short_ref, hidden_ref, out_ref, rows_ref):
    heads, rows, _ = mixed_ref.shape
    rows = 2 * rows

    @pl.when(pl.program_id(0) == 0)
    def _():
        for h in range(heads):
            m = mixed_ref[h]
            rows_ref[:, h * HEAD_DIM : (h + 1) * HEAD_DIM] = jnp.concatenate(
                [m[:, :HEAD_DIM], m[:, HEAD_DIM:]], axis=0
            )

    refined = short_ref[...].astype(jnp.float32) + dot(rows_ref[...], out_weight_ref[...], ((1,), (0,)))
    tile = refined.shape[1]
    spread = jnp.broadcast_to(refined[:, None, :], (rows, SHORT, tile)).reshape(rows * SHORT, tile)
    out_ref[...] = (hidden_ref[...].astype(jnp.float32) + spread).astype(jnp.bfloat16)


def finish(mixed, out_weight, short, hidden):
    count, width = hidden.shape
    rows = count // SHORT
    tile = width // 2
    return pl.pallas_call(
        finish_kernel,
        name="finish",
        grid=(2,),
        in_specs=[
            pl.BlockSpec(mixed.shape, lambda i: (0, 0, 0)),
            pl.BlockSpec((width, tile), lambda i: (0, i)),
            pl.BlockSpec((rows, tile), lambda i: (0, i)),
            pl.BlockSpec((count, tile), lambda i: (0, i)),
        ],
        out_specs=pl.BlockSpec((count, tile), lambda i: (0, i)),
        out_shape=jax.ShapeDtypeStruct((count, width), jnp.bfloat16),
        scratch_shapes=[pltpu.VMEM((rows, width), jnp.bfloat16)],
        compiler_params=params(60),
    )(mixed, out_weight, short, hidden)


def coarse_kernel(number, first, final, where_ref, q_ref, *refs):
    parts = refs[:number]
    old = None if first else refs[number : number + 2]
    outs = refs[number if first else number + 2 :]
    blocks, rows, _ = parts[0].shape
    tile = 4 * rows
    tiles = blocks // 4
    lane = lax.broadcasted_iota(jnp.int32, (1, tile), 1)
    row = lax.broadcasted_iota(jnp.int32, (tile, tile), 0)
    stride = 8 * rows
    place = (row // rows) * stride + row % rows
    limit = (lane // rows) * stride + where_ref[0] * rows + lane % rows
    ones = jnp.ones((16, number * tile), jnp.bfloat16)
    queries = []
    for t in range(tiles):
        halves = [q_ref[4 * t + i, rows:, :] for i in range(4)]
        q = jnp.concatenate([half[:, at : at + HEAD_DIM] for half in halves for at in (0, HEAD_DIM)], axis=0)
        queries.append(jnp.concatenate([q, jnp.zeros_like(q)], axis=1))
    if first:
        tops = [jnp.full((1, tile), NEG, jnp.float32)] * tiles
        accs = [jnp.zeros((16 + HEAD_DIM, tile), jnp.float32)] * tiles
    else:
        tops = [old[0][t, 0:1, :] for t in range(tiles)]
        accs = [old[1][t] for t in range(tiles)]
    for g in range(tiles):
        kv = jnp.concatenate([part[4 * g : 4 * g + 4].reshape(tile, PAIR) for part in parts], axis=0)
        v = jnp.concatenate([ones, kv.T[HEAD_DIM:, :]], axis=0)
        live = range(g, tiles)
        scores = [dot(kv, queries[t], ((1,), (1,))) for t in live]
        keep = jnp.concatenate(
            [place <= limit - where_ref[1 + i] * rows for i in range(number)], axis=0
        )
        scores[0] = jnp.where(keep, scores[0], NEG)
        news = [jnp.maximum(tops[t], jnp.max(s, axis=0, keepdims=True)) for t, s in zip(live, scores)]
        ps = [jnp.exp2(s - top).astype(jnp.bfloat16) for s, top in zip(scores, news)]
        for t, top, p in zip(live, news, ps):
            accs[t] = accs[t] * jnp.exp2(tops[t] - top) + dot(v, p, ((1,), (0,)))
            tops[t] = top
    for t in range(tiles):
        if final:
            o = accs[t][16:] * (1.0 / accs[t][0:1])
            o = o.astype(jnp.bfloat16).T
            for i in range(0, tile, rows):
                low, high = o[i : i + rows // 2], o[i + rows // 2 : i + rows]
                outs[0][4 * t + i // rows] = jnp.concatenate([low, high], axis=1)
        else:
            outs[0][t] = jnp.broadcast_to(tops[t], (8, tile))
            outs[1][t] = accs[t]


def coarse_attend(places, q, parts, state, final):
    heads, rows, _ = parts[0].shape
    tile = 4 * rows
    if final:
        out_shape = jax.ShapeDtypeStruct((heads, rows // 2, PAIR), jnp.bfloat16)
    else:
        out_shape = [
            jax.ShapeDtypeStruct((heads // 4, 8, tile), jnp.float32),
            jax.ShapeDtypeStruct((heads // 4, 16 + HEAD_DIM, tile), jnp.float32),
        ]
    first = state is None
    arrays = [q, *parts] + ([] if first else list(state))
    share = len(parts) / 8
    return pl.pallas_call(
        functools.partial(coarse_kernel, len(parts), first, final),
        in_specs=[pl.BlockSpec(memory_space=pltpu.SMEM)]
        + [pl.BlockSpec(memory_space=pltpu.VMEM)] * len(arrays),
        out_shape=out_shape,
        name="coarse_attend",
        compiler_params=params(),
        cost_estimate=pl.CostEstimate(
            flops=int(share * 6 * 2**30), bytes_accessed=2 * 2**20, transcendentals=int(share * 5 * 2**20)
        ),
    )(jnp.stack(places).astype(jnp.int32), *arrays)


def body(
    tokens,
    fine_query,
    fine_key,
    fine_value,
    fine_out,
    short_weight,
    coarse_query,
    coarse_key,
    coarse_value,
    coarse_out,
):
    count, width = tokens.shape
    bf = jnp.bfloat16
    place = lax.axis_index(ALL).astype(jnp.int32)
    core = lax.axis_index("c").astype(jnp.int32)

    def across(block):
        return lax.ppermute(block, "c", [(0, 1), (1, 0)])

    far = from_behind(tokens, 2)
    mate = across(tokens)
    weights = [fine_key, fine_value.T]
    chip = jnp.concatenate(
        [jnp.where(core == 0, tokens, mate), jnp.where(core == 0, mate, tokens)], axis=0
    )

    def along_x(block, distance):
        return lax.ppermute(block, "x", [(i, (i + distance) % 4) for i in range(4)])

    together = lax.optimization_barrier
    keys, values, query = project(core, chip, [*weights, fine_query])
    state = fine_own(query, keys, values)
    mate_weight = across(short_weight)
    far, state, query, short_weight, mate_weight = together((far, state, query, short_weight, mate_weight))
    near = across(far)
    behind, ahead = along_x(short_weight, 1), along_x(short_weight, 3)
    far_keys, far_values = project(core, far, weights)
    near_keys, near_values = project(core, near, weights)
    where = jnp.stack([core, (place > 1).astype(jnp.int32)])
    fine_mixed = fine_before(where, query, (far_keys, near_keys), (far_values, near_values), state)
    fine_mixed, behind, ahead = together((fine_mixed, behind, ahead))
    two_away = along_x(ahead, 3)
    theirs = across(fine_mixed[1])
    tail = from_behind(tail_project(core, tokens, fine_mixed, theirs, fine_out), 1)
    hidden, natural = out_project(core, tokens, fine_mixed, theirs, fine_out)
    mate_behind, mate_ahead = across(behind), across(ahead)
    hidden, mate_behind, mate_ahead = together((hidden, mate_behind, mate_ahead))
    y = lax.axis_index("y").astype(jnp.int32)

    def along_y(block, distance):
        return lax.ppermute(block, "y", [(i, (i + distance) % 4) for i in range(4)])

    def exchange(blocks, sign):
        return [along_y(block, sign * r) if r > 0 else block for r, block in enumerate(blocks)]

    grouped = exchange(pack(y, hidden, tail), 1)
    *grouped, two_away = together((*grouped, two_away))
    pieces = [short_weight, behind, two_away, ahead, mate_weight, mate_behind, across(two_away), mate_ahead]
    spots_of = [(distance, other) for other in (0, 1) for distance in range(4)]
    where = jnp.stack([lax.axis_index("x").astype(jnp.int32), core])
    partial = exchange(shorten(where, grouped, pieces, spots_of), -1)
    shortened, qkv = coarse_project(partial, coarse_query, coarse_key, coarse_value)
    qkv = lax.all_to_all(qkv, ("z", "x"), 0, 0)
    kv = qkv[:, : count // SHORT]
    c = core
    mine = y * 2 + c

    def spot(distance, other=0):
        return ((y + distance) % 4) * 2 + (1 - c if other else c)

    mate_kv = across(kv)
    below, above, beyond = along_y(kv, 1), along_y(kv, 3), along_y(kv, 2)
    state = coarse_attend((mine, mine, spot(0, 1)), qkv, (kv, mate_kv), None, False)
    others = (below, above, beyond)
    state, *others = lax.optimization_barrier((state, *others))
    swapped = [across(block) for block in others]
    state = coarse_attend((mine, spot(3), spot(1), spot(2)), qkv, others, state, False)
    state, *swapped = lax.optimization_barrier((state, *swapped))
    mixed = coarse_attend((mine, spot(3, 1), spot(1, 1), spot(2, 1)), qkv, swapped, state, True)
    mixed = lax.all_to_all(mixed, ("z", "x"), 0, 0)
    return finish(mixed, coarse_out, shortened, natural)


def solution(mesh):
    fine = Mesh(mesh.devices.reshape(4, 4, 4, 2), ALL)
    return jax.shard_map(
        body,
        mesh=fine,
        in_specs=(P(ALL, None), P(), P(), P(), P(), P(("x", "y", "c"), None), P(), P(), P(), P()),
        out_specs=P(ALL, None),
        check_vma=False,
    )
```

```python
import functools
import math

import jax
import jax.numpy as jnp
from jax import lax
from jax.experimental import pallas as pl
from jax.experimental.pallas import tpu as pltpu
from jax.sharding import Mesh, PartitionSpec as P

HEAD_DIM = 64
HEADS = 16
SHORT = 8
WIN = 1024
SCALE = math.log2(math.e) / math.sqrt(HEAD_DIM)
ALL = ("z", "x", "y", "c")
QB = 128
PAIR = 2 * HEAD_DIM
NEG = -1e30


def from_behind(block, distance):
    devices = range(128)
    route = [(i - distance, i) for i in devices if i - distance in devices]
    return lax.ppermute(block, ALL, route)


def normed(rows):
    values = rows.astype(jnp.float32)
    scale = lax.rsqrt(jnp.mean(values * values, axis=-1, keepdims=True) + 1e-06)
    return (values * scale).astype(jnp.bfloat16)


def dot(a, b, contract):
    return lax.dot_general(a, b, (contract, ((), ())), preferred_element_type=jnp.float32)


def params(mib=24):
    return pltpu.CompilerParams(vmem_limit_bytes=mib * 2**20)


def spots(index):
    groups = QB // SHORT
    return (index % groups) * SHORT + index // groups


def two_heads(q_ref, b):
    lane = lax.broadcasted_iota(jnp.int32, (QB, PAIR), 1)
    q = q_ref[b * QB : (b + 1) * QB, :]
    zero = jnp.zeros_like(q)
    return jnp.concatenate(
        [jnp.where(lane < HEAD_DIM, q, zero), jnp.where(lane < HEAD_DIM, zero, q)], axis=0
    )


def with_sums(v):
    return jnp.concatenate([v, jnp.ones((16, v.shape[1]), jnp.bfloat16)], axis=0)


def moves(rows, take):
    col = lax.broadcasted_iota(jnp.int32, (rows, QB), 1)
    row = lax.broadcasted_iota(jnp.int32, (rows, QB), 0)
    return jnp.where(take(row) == col, 1.0, 0.0).astype(jnp.bfloat16)


def reorder(move, rows):
    parts = [dot(move, rows[i : i + QB], ((1,), (0,))) for i in range(0, rows.shape[0], QB)]
    return jnp.concatenate(parts, axis=0)


def project_kernel(number, core_ref, rows_ref, *refs):
    weights, outs = refs[:number], refs[number:]
    rows = normed(rows_ref[...])
    if number == 3:
        rows = reorder(moves(QB, spots), rows).astype(jnp.bfloat16)
        outs[2][...] = (dot(rows, weights[2][...], ((1,), (0,))) * SCALE).astype(jnp.bfloat16)
    outs[0][...] = dot(rows, weights[0][...], ((1,), (0,))).astype(jnp.bfloat16)
    outs[1][...] = dot(weights[1][...], rows, ((1,), (1,))).astype(jnp.bfloat16)


def project(core, rows, weights):
    count, width = rows.shape
    half = width // 2
    tile = 512
    by_row = pl.BlockSpec((tile, half), lambda i, c: (i, 0))
    columns = pl.BlockSpec((width, half), lambda i, c: (0, c[0]))
    number = len(weights)
    return pl.pallas_call(
        functools.partial(project_kernel, number),
        name="project",
        grid_spec=pltpu.PrefetchScalarGridSpec(
            num_scalar_prefetch=1,
            grid=(count // tile,),
            in_specs=[pl.BlockSpec((tile, width), lambda i, c: (i, 0))]
            + [columns, pl.BlockSpec((half, width), lambda i, c: (c[0], 0)), columns][:number],
            out_specs=[by_row, pl.BlockSpec((half, tile), lambda i, c: (0, i)), by_row][:number],
        ),
        out_shape=[
            jax.ShapeDtypeStruct((count, half), jnp.bfloat16),
            jax.ShapeDtypeStruct((half, count), jnp.bfloat16),
            jax.ShapeDtypeStruct((count, half), jnp.bfloat16),
        ][:number],
        compiler_params=params(20),
        cost_estimate=pl.CostEstimate(flops=1, bytes_accessed=1, transcendentals=0),
    )(core.reshape(1), *[rows, *weights])


def tail_project_kernel(core_ref, tokens_ref, mine_ref, theirs_ref, my_ref, their_ref, tail_ref):
    groups = QB // SHORT
    total = dot(moves(16, lambda r: r + QB - SHORT), tokens_ref[...], ((1,), (0,)))
    take = moves(16, lambda r: r * groups + groups - 1)
    mine = dot(take, mine_ref[0], ((1,), (0,))).astype(jnp.bfloat16)
    theirs = dot(take, theirs_ref[...], ((1,), (0,))).astype(jnp.bfloat16)
    total = total + dot(mine, my_ref[...], ((1,), (0,))) + dot(theirs, their_ref[...], ((1,), (0,)))
    tail_ref[...] = total.astype(jnp.bfloat16)


def tail_project(core, tokens, mixed, theirs, weight):
    count, width = tokens.shape
    half = width // 2
    last = count // QB - 1
    tile = width // 2
    return pl.pallas_call(
        tail_project_kernel,
        name="tail_project",
        grid_spec=pltpu.PrefetchScalarGridSpec(
            num_scalar_prefetch=1,
            grid=(2,),
            in_specs=[
                pl.BlockSpec((QB, tile), lambda i, c: (last, i)),
                pl.BlockSpec((1, QB, half), lambda i, c: (0, last, 0)),
                pl.BlockSpec((QB, half), lambda i, c: (last, 0)),
                pl.BlockSpec((half, tile), lambda i, c: (c[0], i)),
                pl.BlockSpec((half, tile), lambda i, c: (1 - c[0], i)),
            ],
            out_specs=pl.BlockSpec((16, tile), lambda i, c: (0, i)),
        ),
        out_shape=jax.ShapeDtypeStruct((16, width), jnp.bfloat16),
        compiler_params=params(20),
    )(core.reshape(1), tokens, mixed, theirs, weight, weight)


def out_project_kernel(core_ref, tokens_ref, mine_ref, theirs_ref, my_ref, their_ref, hidden_ref, natural_ref):
    total = reorder(moves(QB, spots), tokens_ref[...])
    total = total + dot(mine_ref[0], my_ref[...], ((1,), (0,)))
    total = total + dot(theirs_ref[...], their_ref[...], ((1,), (0,)))
    hidden = total.astype(jnp.bfloat16)
    hidden_ref[...] = hidden
    groups = QB // SHORT
    natural_ref[...] = reorder(moves(QB, lambda r: (r % SHORT) * groups + r // SHORT), hidden).astype(jnp.bfloat16)


def out_project(core, tokens, mixed, theirs, weight):
    count, width = tokens.shape
    half = width // 2
    by_column = pl.BlockSpec((count, half), lambda i, c: (0, i))
    return pl.pallas_call(
        out_project_kernel,
        name="out_project",
        grid_spec=pltpu.PrefetchScalarGridSpec(
            num_scalar_prefetch=1,
            grid=(2,),
            in_specs=[
                by_column,
                pl.BlockSpec((1, count, half), lambda i, c: (0, 0, 0)),
                pl.BlockSpec((count, half), lambda i, c: (0, 0)),
                pl.BlockSpec((half, half), lambda i, c: (c[0], i)),
                pl.BlockSpec((half, half), lambda i, c: (1 - c[0], i)),
            ],
            out_specs=[by_column, by_column],
        ),
        out_shape=[jax.ShapeDtypeStruct((count, width), jnp.bfloat16)] * 2,
        compiler_params=params(20),
    )(core.reshape(1), tokens, mixed, theirs, weight, weight)


def pack_kernel(y_ref, hidden_ref, tail_ref, *refs):
    outs, all_ref = refs[:4], refs[4]
    blocks, places, groups, width = hidden_ref.shape
    rows = blocks * groups
    half = width // 2
    for j in range(SHORT):
        p = (j + 1) % SHORT
        part = hidden_ref[:, p].reshape(rows, width)
        if p > 0:
            wide = part.astype(jnp.float32)
            tail = tail_ref[p : p + 1, :].astype(jnp.float32)
            first = lax.broadcasted_iota(jnp.int32, wide.shape, 0) == 0
            wide = jnp.where(first, tail, pltpu.roll(wide, 1, 0))
            part = wide.astype(jnp.bfloat16)
        for f in range(2):
            all_ref[(j % 2) * 2 + f, j // 2] = part[:, f * half : (f + 1) * half]
    for r in range(4):
        outs[r][...] = all_ref[(y_ref[0] + r) % 4]


def pack(y, hidden, tail):
    count, width = hidden.shape
    groups = QB // SHORT
    blocks = count // QB
    shape = (4, count // SHORT, width // 2)
    return pl.pallas_call(
        pack_kernel,
        name="pack",
        in_specs=[pl.BlockSpec(memory_space=pltpu.SMEM)] + [pl.BlockSpec(memory_space=pltpu.VMEM)] * 2,
        out_shape=[jax.ShapeDtypeStruct(shape, jnp.bfloat16)] * 4,
        scratch_shapes=[pltpu.VMEM((4, *shape), jnp.bfloat16)],
        compiler_params=params(),
    )(y.reshape(1), hidden.reshape(blocks, SHORT, groups, width), tail)


def fine_own_kernel(q_ref, k_ref, v_ref, top_ref, acc_ref, s_ref, p_ref):
    blocks = q_ref.shape[0] // QB
    row = lax.broadcasted_iota(jnp.int32, (QB, 2 * QB), 0)
    col = lax.broadcasted_iota(jnp.int32, (QB, 2 * QB), 1) % QB
    keep = spots(row) <= spots(col)
    for b in range(blocks):
        both = two_heads(q_ref, b)
        if b > 0:
            s_ref[b, : b * QB, :] = dot(k_ref[: b * QB, :], both, ((1,), (1,)))
        s = dot(k_ref[b * QB : (b + 1) * QB, :], both, ((1,), (1,)))
        s_ref[b, b * QB : (b + 1) * QB, :] = jnp.where(keep, s, NEG)
    for b in range(blocks):
        end = (b + 1) * QB
        top = jnp.max(s_ref[b, :end, :], axis=0, keepdims=True)
        p_ref[b, :end, :] = jnp.exp2(s_ref[b, :end, :] - top).astype(jnp.bfloat16)
        top_ref[0, b] = jnp.broadcast_to(top, (8, 2 * QB))
    for b in range(blocks):
        end = (b + 1) * QB
        o = dot(with_sums(v_ref[:, :end]), p_ref[b, :end, :], ((1,), (0,)))
        acc_ref[0, b, :16, :] = o[PAIR:]
        acc_ref[0, b, 16:, :QB] = o[:HEAD_DIM, :QB]
        acc_ref[0, b, 16:, QB:] = o[HEAD_DIM:PAIR, QB:]


def fine_before_kernel(
    where_ref, q_ref, kf_ref, kn_ref, vf_ref, vn_ref, top_ref, acc_ref, out_ref, s_ref, p_ref
):
    half = kf_ref.shape[0]
    blocks = q_ref.shape[0] // QB
    core = where_ref[0]
    row = lax.broadcasted_iota(jnp.int32, (QB, 2 * QB), 0)
    col = lax.broadcasted_iota(jnp.int32, (QB, 2 * QB), 1) % QB
    keep = row > spots(col)

    def store(b, total, o):
        o = o * (1.0 / total)
        mixed = jnp.concatenate([o[:, :QB], o[:, QB:]], axis=0)
        at = b * QB // half
        out_ref[(at + core) % 2, b * QB - at * half : (b + 1) * QB - at * half, :] = mixed.astype(jnp.bfloat16).T

    @pl.when(where_ref[1] == 0)
    def _():
        for b in range(blocks):
            store(b, acc_ref[0, b, 0:1, :], acc_ref[0, b, 16:, :])

    def units(low, high):
        def spans(b):
            if b * QB < half:
                return [(low, b * QB, half - b * QB), (high, 0, half)]
            return [(high, b * QB - half, 2 * half - b * QB)]

        for b in range(blocks):
            both = two_heads(q_ref, b)
            at = b * QB
            for (k_ref, _), first, size in spans(b):
                if at == b * QB:
                    s = dot(k_ref[first : first + QB, :], both, ((1,), (1,)))
                    s_ref[b, at : at + QB, :] = jnp.where(keep, s, NEG)
                    at, first, size = at + QB, first + QB, size - QB
                if size > 0:
                    s_ref[b, at : at + size, :] = dot(k_ref[first : first + size, :], both, ((1,), (1,)))
                at += size
        fades = []
        for b in range(blocks):
            old = top_ref[0, b, 0:1, :]
            top = jnp.maximum(old, jnp.max(s_ref[b, b * QB :, :], axis=0, keepdims=True))
            p_ref[b, b * QB :, :] = jnp.exp2(s_ref[b, b * QB :, :] - top).astype(jnp.bfloat16)
            fades.append(jnp.exp2(old - top))
        for b in range(blocks):
            v = [v_ref[:, first : first + size] for (_, v_ref), first, size in spans(b)]
            o = dot(with_sums(jnp.concatenate(v, axis=1)), p_ref[b, b * QB :, :], ((1,), (0,)))
            acc = acc_ref[0, b] * fades[b]
            new = jnp.concatenate([o[:HEAD_DIM, :QB], o[HEAD_DIM:PAIR, QB:]], axis=1)
            store(b, acc[0:1] + o[PAIR : PAIR + 1], acc[16:] + new)

    @pl.when((where_ref[1] > 0) & (core == 0))
    def _():
        units((kf_ref, vf_ref), (kn_ref, vn_ref))

    @pl.when((where_ref[1] > 0) & (core == 1))
    def _():
        units((kn_ref, vn_ref), (kf_ref, vf_ref))


def fine_own(q, k, v):
    count, width = q.shape
    blocks = count // QB
    pairs = width // PAIR
    return pl.pallas_call(
        fine_own_kernel,
        name="fine_own",
        grid=(pairs,),
        in_specs=[
            pl.BlockSpec((count, PAIR), lambda i: (0, i)),
            pl.BlockSpec((count, PAIR), lambda i: (0, i)),
            pl.BlockSpec((PAIR, count), lambda i: (i, 0)),
        ],
        out_specs=[
            pl.BlockSpec((1, blocks, 8, 2 * QB), lambda i: (i, 0, 0, 0)),
            pl.BlockSpec((1, blocks, 16 + HEAD_DIM, 2 * QB), lambda i: (i, 0, 0, 0)),
        ],
        out_shape=[
            jax.ShapeDtypeStruct((pairs, blocks, 8, 2 * QB), jnp.float32),
            jax.ShapeDtypeStruct((pairs, blocks, 16 + HEAD_DIM, 2 * QB), jnp.float32),
        ],
        scratch_shapes=[
            pltpu.VMEM((blocks, count, 2 * QB), jnp.float32),
            pltpu.VMEM((blocks, count, 2 * QB), jnp.bfloat16),
        ],
        compiler_params=params(),
        cost_estimate=pl.CostEstimate(flops=1, bytes_accessed=1, transcendentals=0),
    )(q, k, v)


def fine_before(where, q, keys, values, state):
    count, width = q.shape
    blocks = count // QB
    half = count // 2
    return pl.pallas_call(
        fine_before_kernel,
        name="fine_before",
        grid=(width // PAIR,),
        in_specs=[pl.BlockSpec(memory_space=pltpu.SMEM), pl.BlockSpec((count, PAIR), lambda i: (0, i))]
        + [pl.BlockSpec((half, PAIR), lambda i: (0, i))] * 2
        + [pl.BlockSpec((PAIR, half), lambda i: (i, 0))] * 2
        + [
            pl.BlockSpec((1, blocks, 8, 2 * QB), lambda i: (i, 0, 0, 0)),
            pl.BlockSpec((1, blocks, 16 + HEAD_DIM, 2 * QB), lambda i: (i, 0, 0, 0)),
        ],
        out_specs=pl.BlockSpec((2, half, PAIR), lambda i: (0, 0, i)),
        out_shape=jax.ShapeDtypeStruct((2, half, width), jnp.bfloat16),
        scratch_shapes=[
            pltpu.VMEM((blocks, count, 2 * QB), jnp.float32),
            pltpu.VMEM((blocks, count, 2 * QB), jnp.bfloat16),
        ],
        compiler_params=params(),
        cost_estimate=pl.CostEstimate(flops=1, bytes_accessed=1, transcendentals=0),
    )(where, q, *keys, *values, *state)


def shorten_kernel(spots_of, where_ref, *refs):
    grouped, pieces, outs = refs[:4], refs[4:-4], refs[-4:]
    parts, rows, depth = grouped[0].shape
    total = None
    for (distance, other), piece in zip(spots_of, pieces):
        size = piece.shape[0]
        x = (where_ref[0] + parts - distance) % parts
        core = 1 - where_ref[1] if other else where_ref[1]
        columns = pl.ds(pl.multiple_of(core * size, size), size)
        part = jnp.concatenate([ref[x, :, columns] for ref in grouped], axis=0)
        term = dot(part, piece[...], ((1,), (0,)))
        total = term if total is None else total + term
    for r in range(4):
        outs[r][...] = total[r * rows : (r + 1) * rows].astype(jnp.bfloat16)


def shorten(where, grouped, pieces, spots_of):
    parts, rows, depth = grouped[0].shape
    width = pieces[0].shape[1]
    tile = width // 2
    return pl.pallas_call(
        functools.partial(shorten_kernel, spots_of),
        name="shorten",
        grid=(2,),
        in_specs=[pl.BlockSpec(memory_space=pltpu.SMEM)]
        + [pl.BlockSpec(grouped[0].shape, lambda i: (0, 0, 0))] * 4
        + [pl.BlockSpec((piece.shape[0], tile), lambda i: (0, i)) for piece in pieces],
        out_specs=[pl.BlockSpec((rows, tile), lambda i: (0, i))] * 4,
        out_shape=[jax.ShapeDtypeStruct((rows, width), jnp.bfloat16)] * 4,
        compiler_params=params(24),
    )(where, *grouped, *pieces)


def coarse_project_kernel(*refs):
    parts, (k_ref, v_ref, q_ref, short_ref, qkv_ref, weight_ref, sems) = refs[:4], refs[4:]
    copies = [
        pltpu.make_async_copy(ref, weight_ref.at[i], sems.at[i])
        for i, ref in enumerate((k_ref, v_ref, q_ref))
    ]
    for copy in copies:
        copy.start()
    short = sum(ref[...].astype(jnp.float32) for ref in parts).astype(jnp.bfloat16)
    short_ref[...] = short
    rows = normed(short)
    for i, copy in enumerate(copies):
        copy.wait()
        out = dot(rows, weight_ref[i], ((1,), (0,)))
        if i == 2:
            out = out * SCALE
        out = out.astype(jnp.bfloat16)
        count = out.shape[0]
        for h in range(HEADS):
            head = out[:, h * HEAD_DIM : (h + 1) * HEAD_DIM]
            if i < 2:
                qkv_ref[h, :count, i * HEAD_DIM : (i + 1) * HEAD_DIM] = head
            else:
                qkv_ref[h, count:, :HEAD_DIM] = head[: count // 2]
                qkv_ref[h, count:, HEAD_DIM:] = head[count // 2 :]


def coarse_project(partial, query, key, value):
    rows, width = partial[0].shape
    vmem = pl.BlockSpec(memory_space=pltpu.VMEM)
    return pl.pallas_call(
        coarse_project_kernel,
        name="coarse_project",
        in_specs=[vmem] * 4 + [pl.BlockSpec(memory_space=pl.ANY)] * 3,
        out_specs=[vmem] * 2,
        out_shape=[
            jax.ShapeDtypeStruct((rows, width), jnp.bfloat16),
            jax.ShapeDtypeStruct((HEADS, rows + rows // 2, PAIR), jnp.bfloat16),
        ],
        scratch_shapes=[
            pltpu.VMEM((3, width, width), jnp.bfloat16),
            pltpu.SemaphoreType.DMA((3,)),
        ],
        compiler_params=params(60),
    )(*partial, key, value, query)


def finish_kernel(mixed_ref, out_weight_ref, short_ref, hidden_ref, out_ref, rows_ref):
    heads, rows, _ = mixed_ref.shape
    rows = 2 * rows

    @pl.when(pl.program_id(0) == 0)
    def _():
        for h in range(heads):
            m = mixed_ref[h]
            rows_ref[:, h * HEAD_DIM : (h + 1) * HEAD_DIM] = jnp.concatenate(
                [m[:, :HEAD_DIM], m[:, HEAD_DIM:]], axis=0
            )

    refined = short_ref[...].astype(jnp.float32) + dot(rows_ref[...], out_weight_ref[...], ((1,), (0,)))
    tile = refined.shape[1]
    spread = jnp.broadcast_to(refined[:, None, :], (rows, SHORT, tile)).reshape(rows * SHORT, tile)
    out_ref[...] = (hidden_ref[...].astype(jnp.float32) + spread).astype(jnp.bfloat16)


def finish(mixed, out_weight, short, hidden):
    count, width = hidden.shape
    rows = count // SHORT
    tile = width // 2
    return pl.pallas_call(
        finish_kernel,
        name="finish",
        grid=(2,),
        in_specs=[
            pl.BlockSpec(mixed.shape, lambda i: (0, 0, 0)),
            pl.BlockSpec((width, tile), lambda i: (0, i)),
            pl.BlockSpec((rows, tile), lambda i: (0, i)),
            pl.BlockSpec((count, tile), lambda i: (0, i)),
        ],
        out_specs=pl.BlockSpec((count, tile), lambda i: (0, i)),
        out_shape=jax.ShapeDtypeStruct((count, width), jnp.bfloat16),
        scratch_shapes=[pltpu.VMEM((rows, width), jnp.bfloat16)],
        compiler_params=params(60),
    )(mixed, out_weight, short, hidden)


def coarse_kernel(number, first, final, where_ref, q_ref, *refs):
    parts = refs[:number]
    old = None if first else refs[number : number + 2]
    outs = refs[number if first else number + 2 :]
    blocks, rows, _ = parts[0].shape
    tile = 4 * rows
    tiles = blocks // 4
    lane = lax.broadcasted_iota(jnp.int32, (1, tile), 1)
    row = lax.broadcasted_iota(jnp.int32, (tile, tile), 0)
    stride = 8 * rows
    place = (row // rows) * stride + row % rows
    limit = (lane // rows) * stride + where_ref[0] * rows + lane % rows
    ones = jnp.ones((16, number * tile), jnp.bfloat16)
    queries = []
    for t in range(tiles):
        halves = [q_ref[4 * t + i, rows:, :] for i in range(4)]
        q = jnp.concatenate([half[:, at : at + HEAD_DIM] for half in halves for at in (0, HEAD_DIM)], axis=0)
        queries.append(jnp.concatenate([q, jnp.zeros_like(q)], axis=1))
    if first:
        tops = [jnp.full((1, tile), NEG, jnp.float32)] * tiles
        accs = [jnp.zeros((16 + HEAD_DIM, tile), jnp.float32)] * tiles
    else:
        tops = [old[0][t, 0:1, :] for t in range(tiles)]
        accs = [old[1][t] for t in range(tiles)]
    for g in range(tiles):
        kv = jnp.concatenate([part[4 * g : 4 * g + 4].reshape(tile, PAIR) for part in parts], axis=0)
        v = jnp.concatenate([ones, kv.T[HEAD_DIM:, :]], axis=0)
        live = range(g, tiles)
        scores = [dot(kv, queries[t], ((1,), (1,))) for t in live]
        keep = jnp.concatenate(
            [place <= limit - where_ref[1 + i] * rows for i in range(number)], axis=0
        )
        scores[0] = jnp.where(keep, scores[0], NEG)
        news = [jnp.maximum(tops[t], jnp.max(s, axis=0, keepdims=True)) for t, s in zip(live, scores)]
        ps = [jnp.exp2(s - top).astype(jnp.bfloat16) for s, top in zip(scores, news)]
        for t, top, p in zip(live, news, ps):
            accs[t] = accs[t] * jnp.exp2(tops[t] - top) + dot(v, p, ((1,), (0,)))
            tops[t] = top
    for t in range(tiles):
        if final:
            o = accs[t][16:] * (1.0 / accs[t][0:1])
            o = o.astype(jnp.bfloat16).T
            for i in range(0, tile, rows):
                low, high = o[i : i + rows // 2], o[i + rows // 2 : i + rows]
                outs[0][4 * t + i // rows] = jnp.concatenate([low, high], axis=1)
        else:
            outs[0][t] = jnp.broadcast_to(tops[t], (8, tile))
            outs[1][t] = accs[t]


def coarse_attend(places, q, parts, state, final):
    heads, rows, _ = parts[0].shape
    tile = 4 * rows
    if final:
        out_shape = jax.ShapeDtypeStruct((heads, rows // 2, PAIR), jnp.bfloat16)
    else:
        out_shape = [
            jax.ShapeDtypeStruct((heads // 4, 8, tile), jnp.float32),
            jax.ShapeDtypeStruct((heads // 4, 16 + HEAD_DIM, tile), jnp.float32),
        ]
    first = state is None
    arrays = [q, *parts] + ([] if first else list(state))
    share = len(parts) / 8
    return pl.pallas_call(
        functools.partial(coarse_kernel, len(parts), first, final),
        in_specs=[pl.BlockSpec(memory_space=pltpu.SMEM)]
        + [pl.BlockSpec(memory_space=pltpu.VMEM)] * len(arrays),
        out_shape=out_shape,
        name="coarse_attend",
        compiler_params=params(),
        cost_estimate=pl.CostEstimate(
            flops=int(share * 6 * 2**30), bytes_accessed=2 * 2**20, transcendentals=int(share * 5 * 2**20)
        ),
    )(jnp.stack(places).astype(jnp.int32), *arrays)


def body(
    tokens,
    fine_query,
    fine_key,
    fine_value,
    fine_out,
    short_weight,
    coarse_query,
    coarse_key,
    coarse_value,
    coarse_out,
):
    count, width = tokens.shape
    bf = jnp.bfloat16
    place = lax.axis_index(ALL).astype(jnp.int32)
    core = lax.axis_index("c").astype(jnp.int32)

    def across(block):
        return lax.ppermute(block, "c", [(0, 1), (1, 0)])

    far = from_behind(tokens, 2)
    mate = across(tokens)
    weights = [fine_key, fine_value.T]
    chip = jnp.concatenate(
        [jnp.where(core == 0, tokens, mate), jnp.where(core == 0, mate, tokens)], axis=0
    )

    def along_x(block, distance):
        return lax.ppermute(block, "x", [(i, (i + distance) % 4) for i in range(4)])

    together = lax.optimization_barrier
    keys, values, query = project(core, chip, [*weights, fine_query])
    state = fine_own(query, keys, values)
    mate_weight = across(short_weight)
    far, state, query, short_weight, mate_weight = together((far, state, query, short_weight, mate_weight))
    near = across(far)
    behind, ahead = along_x(short_weight, 1), along_x(short_weight, 3)
    far_keys, far_values = project(core, far, weights)
    near_keys, near_values = project(core, near, weights)
    where = jnp.stack([core, (place > 1).astype(jnp.int32)])
    fine_mixed = fine_before(where, query, (far_keys, near_keys), (far_values, near_values), state)
    fine_mixed, behind, ahead = together((fine_mixed, behind, ahead))
    two_away = along_x(ahead, 3)
    theirs = across(fine_mixed[1])
    tail = from_behind(tail_project(core, tokens, fine_mixed, theirs, fine_out), 1)
    hidden, natural = out_project(core, tokens, fine_mixed, theirs, fine_out)
    mate_behind, mate_ahead = across(behind), across(ahead)
    hidden, mate_behind, mate_ahead = together((hidden, mate_behind, mate_ahead))
    y = lax.axis_index("y").astype(jnp.int32)

    def along_y(block, distance):
        return lax.ppermute(block, "y", [(i, (i + distance) % 4) for i in range(4)])

    def exchange(blocks, sign):
        return [along_y(block, sign * r) if r > 0 else block for r, block in enumerate(blocks)]

    grouped = exchange(pack(y, hidden, tail), 1)
    *grouped, two_away = together((*grouped, two_away))
    pieces = [short_weight, behind, two_away, ahead, mate_weight, mate_behind, across(two_away), mate_ahead]
    spots_of = [(distance, other) for other in (0, 1) for distance in range(4)]
    where = jnp.stack([lax.axis_index("x").astype(jnp.int32), core])
    partial = exchange(shorten(where, grouped, pieces, spots_of), -1)
    shortened, qkv = coarse_project(partial, coarse_query, coarse_key, coarse_value)
    qkv = lax.all_to_all(qkv, ("z", "x"), 0, 0)
    kv = qkv[:, : count // SHORT]
    c = core
    mine = y * 2 + c

    def spot(distance, other=0):
        return ((y + distance) % 4) * 2 + (1 - c if other else c)

    mate_kv = across(kv)
    below, above, beyond = along_y(kv, 1), along_y(kv, 3), along_y(kv, 2)
    state = coarse_attend((mine, mine, spot(0, 1)), qkv, (kv, mate_kv), None, False)
    others = (below, above, beyond)
    state, *others = lax.optimization_barrier((state, *others))
    swapped = [across(block) for block in others]
    state = coarse_attend((mine, spot(3), spot(1), spot(2)), qkv, others, state, False)
    state, *swapped = lax.optimization_barrier((state, *swapped))
    mixed = coarse_attend((mine, spot(3, 1), spot(1, 1), spot(2, 1)), qkv, swapped, state, True)
    mixed = lax.all_to_all(mixed, ("z", "x"), 0, 0)
    return finish(mixed, coarse_out, shortened, natural)


def solution(mesh):
    fine = Mesh(mesh.devices.reshape(4, 4, 4, 2), ALL)
    return jax.shard_map(
        body,
        mesh=fine,
        in_specs=(P(ALL, None), P(), P(), P(), P(), P(("x", "y", "c"), None), P(), P(), P(), P()),
        out_specs=P(ALL, None),
        check_vma=False,
    )
```
